32 devices in a mesh: dp: 4 (over y, core), ulysses: 8 (over z, x).
Axes of the slice: x: 2, y: 2, z: 4, core: 2. Of those that a mesh axis runs over, the one named last changes fastest.
Arguments:
- query_rows: bfloat16 [4096, 1024], P(('dp', 'ulysses')), may hold values from -6 to 6
- key_rows: bfloat16 [4096, 128], P(('dp', 'ulysses')), may hold values from -6 to 6
- value_rows: bfloat16 [4096, 128], P(('dp', 'ulysses')), may hold values from -6 to 6
- grad_out: bfloat16 [4096, 1024], P(('dp', 'ulysses')), may hold values from -6 to 6
- doc_lengths: int32 [4, 12], replicated, may hold values from 1 to 512, 1024 in all within a row
Outputs:
- attention: bfloat16 [4096, 1024], P(('dp', 'ulysses'))
- grad_queries: bfloat16 [4096, 1024], P(('dp', 'ulysses'))
- grad_keys: bfloat16 [4096, 128], P(('dp', 'ulysses'))
- grad_values: bfloat16 [4096, 128], P(('dp', 'ulysses'))
The draws below stay inside these ranges and needn't reach their ends.
Inputs may be any that keep to these rules, and one draw needn't show every extreme that they name: `doc_lengths`: each row's 12 lengths sum to 1024, and the longest is 512.
All inputs are finite; a program needn't handle non-finite values.
Results may differ from the reference program's by a relative error of at most 0.011.
Values may be sent and summed in bfloat16 or wider, within the bound.
No kernel may reach another device: no remote copies, remote signals or barrier semaphores. Data moves between devices by JAX's collectives and lax.ppermute only.
A program may use at most 64 MiB of HBM per device.

```python
import math
import jax
import jax.numpy as jnp
import numpy as np
from jax import lax

HD = 128
DOCS = 12
BLOCK = 512
HQ = 8
KVH = 1
SEQ = 1024
ROWS = 4
MAXDOC = 512


def draw_query_rows(key, part):
    tokens_all = ROWS * SEQ
    own_key = jax.random.fold_in(key, 3)
    values_now = jnp.clip(jax.random.normal(own_key, (tokens_all, HQ, HD), jnp.float32), -6.0, 6.0)
    return values_now.reshape(tokens_all, HQ * HD).astype(jnp.bfloat16)


def draw_key_rows(key, part):
    tokens_all = ROWS * SEQ
    own_key = jax.random.fold_in(key, 5)
    values_now = jnp.clip(jax.random.normal(own_key, (tokens_all, KVH, HD), jnp.float32), -6.0, 6.0)
    return values_now.reshape(tokens_all, KVH * HD).astype(jnp.bfloat16)


def block_levels(stream_key, extent, pieces, low, high):
    factor_of = 1.0
    for dim, parts in pieces:
        steps = jax.random.uniform(jax.random.fold_in(jax.random.fold_in(stream_key, 6), dim), (parts,), jnp.float32, low / len(pieces), high / len(pieces))
        factor_of = factor_of * jnp.repeat(jnp.exp(steps), extent[dim] // parts).reshape((-1,) + (1,) * (len(extent) - 1 - dim))
    return factor_of


def split_up(amount, total, limit, skew):
    loads = [(1 << 20) // math.isqrt(standing ** skew) + 1 for standing in range(2, amount + 1)]
    spare, holding = total - limit - (amount - 1), [1] * (amount - 1)
    while spare > 0:
        free = [i for i in range(amount - 1) if holding[i] < limit]
        whole, left = sum([loads[i] for i in free]), spare
        for i in free:
            addition = min(limit - holding[i], max(1, left * loads[i] // whole), spare)
            holding[i] = holding[i] + addition
            spare = spare - addition
    return np.array([limit] + holding)


def ragged(rng, number_of, total, bound, slope):
    if number_of == 2:
        one = jax.random.randint(rng, (), max(1, total - bound), min(bound, total - 1) + 1)
        return jnp.stack([one, total - one])
    sizes = jnp.asarray(split_up(number_of, total, bound, slope), jnp.int32)
    couples = (number_of - 1) // 2
    giver, sink = sizes[1:1 + 2 * couples:2], sizes[2:2 + 2 * couples:2]
    margin = jnp.minimum(giver - 1, bound - sink)
    moved = jax.random.randint(jax.random.fold_in(rng, 1), (couples,), 0, 1 << 20) % (margin + 1)
    sizes = sizes.at[1:1 + 2 * couples:2].set(giver - moved).at[2:2 + 2 * couples:2].set(sink + moved)
    return sizes[jax.random.permutation(jax.random.fold_in(rng, 2), number_of)]


def scatter_about(key, dims, deviation, reach, shards=(), kind=jnp.bfloat16):
    drawn = jax.random.normal(key, dims, jnp.float32) * deviation
    if len(shards) > 0:
        drawn = block_levels(key, dims, shards, -0.22, 0.18) * drawn
    return jnp.clip(drawn, min=-reach, max=reach).astype(kind)


def setup_inputs(seed: int = 0) -> dict:
    splits = jax.random.split(jax.random.key(seed), 6)
    query_rows = draw_query_rows(jax.random.fold_in(splits[5], 71), 0)
    key_rows = draw_key_rows(jax.random.fold_in(splits[5], 71), 0)
    value_rows = scatter_about(splits[2], (ROWS * SEQ, KVH * HD), 1.0, 6.0, ((0, 32),))
    grad_out = scatter_about(splits[3], (ROWS * SEQ, HQ * HD), 1.0, 6.0, ((0, 32),))
    doc_lengths = jax.vmap(lambda own: ragged(own, DOCS, SEQ, MAXDOC, 2))(jax.random.split(splits[4], ROWS)).reshape((ROWS, DOCS)).astype(jnp.int32)
    return {"query_rows": query_rows, "key_rows": key_rows, "value_rows": value_rows, "grad_out": grad_out, "doc_lengths": doc_lengths}


masked_score = -1e+30

def doc_starts(row_lengths, length):
    doc_ends = jnp.cumsum(row_lengths).astype(jnp.int32)
    positions = jnp.arange(length, dtype=jnp.int32)
    passed = (doc_ends[None, :] <= positions[:, None]).astype(jnp.int32)
    return lax.optimization_barrier(jnp.sum(passed * row_lengths[None, :], axis=1)).astype(jnp.int32)

def attend_head(query_head, key_head, value_head, grad_head, starts, owned_blocks, block_rows):
    length, head_width = query_head.shape
    blocks = length // block_rows
    score_scale = 1.0 / math.sqrt(head_width)
    offsets = jnp.arange(block_rows, dtype=jnp.int32)
    block_first = starts.reshape(blocks, block_rows)[:, 0]

    def forward_block(query_index, carried):
        output_rows, log_totals = carried
        row_start = query_index * block_rows
        query_block = lax.dynamic_slice_in_dim(query_head, row_start, block_rows, 0)
        first_key = lax.dynamic_slice_in_dim(starts, row_start, block_rows, 0)
        query_pos = row_start + offsets

        def key_step(key_index, status):
            key_start = key_index * block_rows
            needed = owned_blocks[query_index] & (key_start + block_rows - 1 >= block_first[query_index])

            def update(status):
                running_max, running_sum, totals = status
                key_block = lax.dynamic_slice_in_dim(key_head, key_start, block_rows, 0)
                value_block = lax.dynamic_slice_in_dim(value_head, key_start, block_rows, 0)
                key_pos = key_start + offsets
                allowed = (key_pos[None, :] <= query_pos[:, None]) & (key_pos[None, :] >= first_key[:, None])
                scores = jnp.dot(query_block, key_block.T, preferred_element_type=jnp.float32) * score_scale
                scores = jnp.where(allowed, scores, masked_score)
                new_max = jnp.maximum(running_max, lax.optimization_barrier(jnp.max(scores, axis=1)))
                weights = jnp.where(allowed, jnp.exp(scores - new_max[:, None]), 0.0)
                factor = jnp.exp(running_max - new_max)
                running_sum = running_sum * factor + lax.optimization_barrier(jnp.sum(weights, axis=1))
                totals = totals * factor[:, None] + jnp.dot(weights.astype(jnp.bfloat16), value_block, preferred_element_type=jnp.float32)
                return (new_max, running_sum, totals)
            return lax.cond(needed, update, lambda unchanged: unchanged, status)
        start_status = (jnp.full((block_rows,), masked_score, dtype=jnp.float32), jnp.zeros((block_rows,), jnp.float32), jnp.zeros((block_rows, head_width), jnp.float32))
        running_max, running_sum, totals = lax.fori_loop(0, query_index + 1, key_step, start_status)
        safe_sum = jnp.where(owned_blocks[query_index], running_sum, 1.0)
        output_block = (totals / safe_sum[:, None]).astype(jnp.bfloat16)
        output_rows = lax.dynamic_update_slice_in_dim(output_rows, output_block, row_start, 0)
        log_totals = lax.dynamic_update_slice_in_dim(log_totals, running_max + jnp.log(safe_sum), row_start, 0)
        return (output_rows, log_totals)
    output_rows, log_totals = lax.fori_loop(0, blocks, forward_block, (jnp.zeros((length, head_width), jnp.bfloat16), jnp.zeros((length,), jnp.float32)))
    row_dots = lax.optimization_barrier(jnp.sum(grad_head.astype(jnp.float32) * output_rows.astype(jnp.float32), axis=1))

    def backward_block(key_index, carried):
        grad_query, grad_key, grad_value = carried
        key_start = key_index * block_rows
        key_block = lax.dynamic_slice_in_dim(key_head, key_start, block_rows, 0)
        value_block = lax.dynamic_slice_in_dim(value_head, key_start, block_rows, 0)
        key_pos = key_start + offsets

        def query_step(query_index, status):
            row_start = query_index * block_rows
            needed = owned_blocks[query_index] & (key_start + block_rows - 1 >= block_first[query_index])

            def update(status):
                query_sum, key_sum, value_sum = status
                query_block = lax.dynamic_slice_in_dim(query_head, row_start, block_rows, 0)
                grad_block = lax.dynamic_slice_in_dim(grad_head, row_start, block_rows, 0)
                log_block = lax.dynamic_slice_in_dim(log_totals, row_start, block_rows, 0)
                dot_block = lax.dynamic_slice_in_dim(row_dots, row_start, block_rows, 0)
                first_key = lax.dynamic_slice_in_dim(starts, row_start, block_rows, 0)
                query_pos = row_start + offsets
                allowed = (key_pos[None, :] <= query_pos[:, None]) & (key_pos[None, :] >= first_key[:, None])
                scores = jnp.dot(query_block, key_block.T, preferred_element_type=jnp.float32) * score_scale
                weights = jnp.where(allowed, jnp.exp(scores - log_block[:, None]), 0.0)
                weights_low = weights.astype(jnp.bfloat16)
                value_sum = value_sum + jnp.dot(weights_low.T, grad_block, preferred_element_type=jnp.float32)
                grad_weights = jnp.dot(grad_block, value_block.T, preferred_element_type=jnp.float32)
                grad_scores = (weights * (grad_weights - dot_block[:, None])).astype(jnp.bfloat16)
                key_sum = key_sum + jnp.dot(grad_scores.T, query_block, preferred_element_type=jnp.float32) * score_scale
                query_now = lax.dynamic_slice_in_dim(query_sum, row_start, block_rows, 0) + jnp.dot(grad_scores, key_block, preferred_element_type=jnp.float32) * score_scale
                query_sum = lax.dynamic_update_slice_in_dim(query_sum, query_now, row_start, 0)
                return (query_sum, key_sum, value_sum)
            return lax.cond(needed, update, lambda unchanged: unchanged, status)
        zeros_block = jnp.zeros((block_rows, head_width), jnp.float32)
        grad_query, key_sum, value_sum = lax.fori_loop(key_index, blocks, query_step, (grad_query, zeros_block, zeros_block))
        grad_key = lax.dynamic_update_slice_in_dim(grad_key, key_sum, key_start, 0)
        grad_value = lax.dynamic_update_slice_in_dim(grad_value, value_sum, key_start, 0)
        return (grad_query, grad_key, grad_value)
    zero_rows = jnp.zeros((length, head_width), jnp.float32)
    grad_query, grad_key, grad_value = lax.fori_loop(0, blocks, backward_block, (zero_rows, zero_rows, zero_rows))
    return (output_rows, grad_query.astype(jnp.bfloat16), grad_key, grad_value)

def reference(query_rows, key_rows, value_rows, grad_out, doc_lengths):
    row_count = doc_lengths.shape[0]
    length = query_rows.shape[0] // row_count
    query_heads = query_rows.shape[1] // HD
    shared_heads = key_rows.shape[1] // HD
    group_size = query_heads // shared_heads
    queries = query_rows.reshape(row_count, length, query_heads, HD)
    key_split = key_rows.reshape(row_count, length, shared_heads, HD)
    value_split = value_rows.reshape(row_count, length, shared_heads, HD)
    grad_split = grad_out.reshape(row_count, length, query_heads, HD)
    owned_blocks = jnp.ones((length // BLOCK,), dtype=bool)

    def one_group(position):
        row_index = position // shared_heads
        shared = position % shared_heads
        starts = doc_starts(doc_lengths[row_index], length)
        key_head = key_split[row_index, :, shared]
        value_head = value_split[row_index, :, shared]

        def one_head(member):
            head_index = shared * group_size + member
            result = attend_head(queries[row_index, :, head_index], key_head, value_head, grad_split[row_index, :, head_index], starts, owned_blocks, BLOCK)
            return (result[0], result[1], result[2].astype(jnp.bfloat16), result[3].astype(jnp.bfloat16))
        outputs, grad_query, key_terms, value_terms = lax.map(one_head, jnp.arange(group_size, dtype=jnp.int32))
        grad_key = lax.optimization_barrier(jnp.sum(key_terms.astype(jnp.float32), axis=0)).astype(jnp.bfloat16)
        grad_value = lax.optimization_barrier(jnp.sum(value_terms.astype(jnp.float32), axis=0)).astype(jnp.bfloat16)
        return (outputs, grad_query, grad_key, grad_value)
    outputs, grad_query, grad_key, grad_value = lax.map(one_group, jnp.arange(row_count * shared_heads, dtype=jnp.int32))
    attention = outputs.reshape(row_count, shared_heads, group_size, length, HD).transpose(0, 3, 1, 2, 4).reshape(row_count * length, query_heads * HD)
    grad_queries = grad_query.reshape(row_count, shared_heads, group_size, length, HD).transpose(0, 3, 1, 2, 4).reshape(row_count * length, query_heads * HD)
    grad_keys = grad_key.reshape(row_count, shared_heads, length, HD).transpose(0, 2, 1, 3).reshape(row_count * length, shared_heads * HD)
    grad_values = grad_value.reshape(row_count, shared_heads, length, HD).transpose(0, 2, 1, 3).reshape(row_count * length, shared_heads * HD)
    return (attention, grad_queries, grad_keys, grad_values)
```

```python
import functools
import math

import jax
import jax.numpy as jnp
from jax import lax
from jax.experimental import pallas as pl
from jax.experimental.pallas import tpu as pltpu
from jax.sharding import PartitionSpec as P

HD = 128
PAIR = 2
masked_score = -1e30

NT = (((1,), (1,)), ((), ()))
TN = (((0,), (0,)), ((), ()))


def dot(a, b, dims=(((1,), (0,)), ((), ()))):
    return lax.dot_general(a, b, dims, preferred_element_type=jnp.float32)


def layer_kernel(shifts, shared_heads, doc_ref, query_ref, grad_ref, *refs):
    kv_refs = refs[: shifts + 1]
    out_ref, query_grad_ref = refs[shifts + 1 : shifts + 3]
    kv_grad_refs = refs[shifts + 3 : 2 * shifts + 4]
    weights_ref, scores_grad_ref = refs[2 * shifts + 4 :]
    tokens = query_ref.shape[0]
    group_size = query_ref.shape[1] // HD // shared_heads
    pairs = group_size // PAIR
    score_scale = 1.0 / math.sqrt(HD)

    row = lax.axis_index("dp")
    place = lax.axis_index("ulysses")
    query_pos = place * tokens + lax.broadcasted_iota(jnp.int32, (1, tokens), 1)
    first_key = jnp.zeros((1, tokens), jnp.int32)
    doc_end = jnp.int32(0)
    for doc in range(doc_ref.shape[1]):
        doc_end = doc_end + doc_ref[row, doc]
        first_key = jnp.where(doc_end <= query_pos, doc_end, first_key)
    window = (shifts + 1) * tokens
    key_pos = (place - shifts) * tokens + lax.broadcasted_iota(jnp.int32, (window, tokens), 0)
    allowed = (key_pos >= first_key) & (key_pos <= query_pos)
    bias = jnp.where(allowed, 0.0, masked_score)
    bias = jnp.concatenate([bias] * PAIR, axis=1)

    def group(shared):
        def columns(ref, head, heads=1):
            start = (shared * group_size + head) * HD
            if not isinstance(start, int):
                start = pl.multiple_of(start, HD)
            return ref[:, pl.ds(start, heads * HD)]

        def kv_start(first):
            start = (first + shared) * HD
            return start if isinstance(start, int) else pl.multiple_of(start, HD)

        keys = jnp.concatenate(
            [ref[:, pl.ds(kv_start(0), HD)] for ref in reversed(kv_refs)], axis=0
        )
        values = jnp.concatenate(
            [ref[:, pl.ds(kv_start(shared_heads), HD)] for ref in reversed(kv_refs)], axis=0
        )
        queries = jnp.concatenate([columns(query_ref, h) for h in range(group_size)], axis=0)
        grads = jnp.concatenate([columns(grad_ref, h) for h in range(group_size)], axis=0)
        for pair in range(pairs):
            part = slice(pair * PAIR * tokens, (pair + 1) * PAIR * tokens)
            scores = dot(keys, queries[part], NT) * (score_scale * math.log2(math.e)) + bias
            weights = jnp.exp2(scores - jnp.max(scores, axis=0, keepdims=True))
            weights = weights * (1.0 / jnp.sum(weights, axis=0, keepdims=True))
            weights_low = weights.astype(jnp.bfloat16)
            weights_ref[:, part] = weights_low
            out = dot(values, weights_low, TN)
            grad_weights = dot(values, grads[part], NT)
            row_dots = jnp.sum(weights * grad_weights, axis=0, keepdims=True)
            grad_scores = (weights * (grad_weights - row_dots)).astype(jnp.bfloat16)
            scores_grad_ref[:, part] = grad_scores
            query_grad = dot(keys, grad_scores, TN) * score_scale
            for member in range(PAIR):
                start = (shared * group_size + pair * PAIR + member) * HD
                if not isinstance(start, int):
                    start = pl.multiple_of(start, HD)
                own = slice(member * tokens, (member + 1) * tokens)
                out_ref[:, pl.ds(start, HD)] = out[:, own].T.astype(jnp.bfloat16)
                query_grad_ref[:, pl.ds(start, HD)] = query_grad[:, own].T.astype(jnp.bfloat16)
        value_grad = dot(weights_ref[...], grads)
        key_grad = dot(scores_grad_ref[...], queries) * score_scale
        for shift, ref in enumerate(kv_grad_refs):
            own = slice((shifts - shift) * tokens, (shifts - shift + 1) * tokens)
            ref[:, pl.ds(kv_start(0), HD)] = key_grad[own].astype(ref.dtype)
            ref[:, pl.ds(kv_start(shared_heads), HD)] = value_grad[own].astype(ref.dtype)

    if shared_heads == 1:
        group(0)
    else:
        pl.loop(0, shared_heads)(group)


def per_device(devices, query_rows, key_rows, value_rows, grad_out, doc_lengths):
    tokens, query_width = query_rows.shape
    kv_width = key_rows.shape[1]
    shared_heads = kv_width // HD
    length = tokens * devices
    shifts = min(devices - 1, (length // 2 - 1 + tokens - 1) // tokens)

    kv = jnp.concatenate([key_rows, value_rows], axis=1)
    blocks = [kv]
    for shift in range(1, shifts + 1):
        blocks.append(
            lax.ppermute(kv, "ulysses", [(d, d + shift) for d in range(devices - shift)])
        )

    window = (shifts + 1) * tokens
    columns = query_width // shared_heads // HD * tokens
    vmem = pl.BlockSpec(memory_space=pltpu.VMEM)
    flops = 6 * 2 * window * columns * HD * shared_heads
    outs = pl.pallas_call(
        functools.partial(layer_kernel, shifts, shared_heads),
        out_shape=[
            jax.ShapeDtypeStruct((tokens, query_width), jnp.bfloat16),
            jax.ShapeDtypeStruct((tokens, query_width), jnp.bfloat16),
            jax.ShapeDtypeStruct((tokens, 2 * kv_width), jnp.float32),
        ]
        + [jax.ShapeDtypeStruct((tokens, 2 * kv_width), jnp.bfloat16)] * shifts,
        in_specs=[pl.BlockSpec(memory_space=pltpu.SMEM)] + [vmem] * (shifts + 3),
        out_specs=[vmem] * (shifts + 3),
        scratch_shapes=[
            pltpu.VMEM((window, columns), jnp.bfloat16),
            pltpu.VMEM((window, columns), jnp.bfloat16),
        ],
        compiler_params=pltpu.CompilerParams(vmem_limit_bytes=40 * 1024 * 1024),
        cost_estimate=pl.CostEstimate(
            flops=flops, bytes_accessed=4 * 2 * tokens * query_width, transcendentals=window * columns
        ),
        name="layer",
    )(doc_lengths, query_rows, grad_out, *blocks)
    attention, grad_queries, total = outs[:3]
    for shift in range(1, shifts + 1):
        total = total + lax.ppermute(
            outs[2 + shift], "ulysses", [(d, d - shift) for d in range(shift, devices)]
        ).astype(jnp.float32)
    total = total.astype(jnp.bfloat16)
    return (attention, grad_queries, total[:, :kv_width], total[:, kv_width:])


def solution(mesh):
    rows = P(("dp", "ulysses"), None)
    return jax.shard_map(
        functools.partial(per_device, mesh.shape["ulysses"]),
        mesh=mesh,
        in_specs=(rows, rows, rows, rows, P()),
        out_specs=(rows, rows, rows, rows),
        check_vma=False,
    )
```

```python
import functools
import math

import jax
import jax.numpy as jnp
from jax import lax
from jax.experimental import pallas as pl
from jax.experimental.pallas import tpu as pltpu
from jax.sharding import PartitionSpec as P

HD = 128
PAIR = 2
masked_score = -1e30

NT = (((1,), (1,)), ((), ()))
TN = (((0,), (0,)), ((), ()))


def dot(a, b, dims=(((1,), (0,)), ((), ()))):
    return lax.dot_general(a, b, dims, preferred_element_type=jnp.float32)


def layer_kernel(shifts, shared_heads, doc_ref, query_ref, grad_ref, kv_ref, *refs):
    out_ref, query_grad_ref, kv_grad_ref, weights_ref, scores_grad_ref = refs
    tokens = query_ref.shape[0]
    group_size = query_ref.shape[1] // HD // shared_heads
    pairs = group_size // PAIR
    score_scale = 1.0 / math.sqrt(HD)

    row = lax.axis_index("dp")
    place = lax.axis_index("ulysses")
    query_pos = place * tokens + lax.broadcasted_iota(jnp.int32, (1, tokens), 1)
    first_key = jnp.zeros((1, tokens), jnp.int32)
    doc_end = jnp.int32(0)
    for doc in range(doc_ref.shape[1]):
        doc_end = doc_end + doc_ref[row, doc]
        first_key = jnp.where(doc_end <= query_pos, doc_end, first_key)
    window = (shifts + 1) * tokens
    window_start = pl.multiple_of(jnp.maximum(place - shifts, 0) * tokens, tokens)
    key_pos = window_start + lax.broadcasted_iota(jnp.int32, (window, tokens), 0)
    allowed = (key_pos >= first_key) & (key_pos <= query_pos)
    bias = jnp.where(allowed, 0.0, masked_score)
    bias = jnp.concatenate([bias] * PAIR, axis=1)
    kv_grad_ref[...] = jnp.zeros_like(kv_grad_ref)

    def group(shared):
        def lanes(head):
            start = head * HD
            return pl.ds(start if isinstance(start, int) else pl.multiple_of(start, HD), HD)

        rows = pl.ds(window_start, window)
        keys = kv_ref[rows, lanes(shared)]
        values = kv_ref[rows, lanes(shared_heads + shared)]
        first_head = shared * group_size
        queries = jnp.concatenate(
            [query_ref[:, lanes(first_head + h)] for h in range(group_size)], axis=0
        )
        grads = jnp.concatenate(
            [grad_ref[:, lanes(first_head + h)] for h in range(group_size)], axis=0
        )
        for pair in range(pairs):
            part = slice(pair * PAIR * tokens, (pair + 1) * PAIR * tokens)
            scores = dot(keys, queries[part], NT) * (score_scale * math.log2(math.e)) + bias
            weights = jnp.exp2(scores - jnp.max(scores, axis=0, keepdims=True))
            weights = weights * (1.0 / jnp.sum(weights, axis=0, keepdims=True))
            weights_low = weights.astype(jnp.bfloat16)
            weights_ref[:, part] = weights_low
            out = dot(values, weights_low, TN)
            grad_weights = dot(values, grads[part], NT)
            row_dots = jnp.sum(weights * grad_weights, axis=0, keepdims=True)
            grad_scores = (weights * (grad_weights - row_dots)).astype(jnp.bfloat16)
            scores_grad_ref[:, part] = grad_scores
            query_grad = dot(keys, grad_scores, TN) * score_scale
            for member in range(PAIR):
                own = slice(member * tokens, (member + 1) * tokens)
                at = lanes(first_head + pair * PAIR + member)
                out_ref[:, at] = out[:, own].T.astype(jnp.bfloat16)
                query_grad_ref[:, at] = query_grad[:, own].T.astype(jnp.bfloat16)
        value_grad = dot(weights_ref[...], grads)
        key_grad = dot(scores_grad_ref[...], queries) * score_scale
        kv_grad_ref[rows, lanes(shared)] = key_grad.astype(jnp.bfloat16)
        kv_grad_ref[rows, lanes(shared_heads + shared)] = value_grad.astype(jnp.bfloat16)

    if shared_heads == 1:
        group(0)
    else:
        pl.loop(0, shared_heads)(group)


def per_device(devices, query_rows, key_rows, value_rows, grad_out, doc_lengths):
    tokens, query_width = query_rows.shape
    kv_width = key_rows.shape[1]
    shared_heads = kv_width // HD
    length = tokens * devices
    shifts = min(devices - 1, (length // 2 - 1 + tokens - 1) // tokens)

    kv = jnp.concatenate([key_rows, value_rows], axis=1)
    kv = lax.all_gather(kv, "ulysses", axis=0, tiled=True)

    window = (shifts + 1) * tokens
    columns = query_width // shared_heads // HD * tokens
    vmem = pl.BlockSpec(memory_space=pltpu.VMEM)
    flops = 6 * 2 * window * columns * HD * shared_heads
    attention, grad_queries, kv_terms = pl.pallas_call(
        functools.partial(layer_kernel, shifts, shared_heads),
        out_shape=[
            jax.ShapeDtypeStruct((tokens, query_width), jnp.bfloat16),
            jax.ShapeDtypeStruct((tokens, query_width), jnp.bfloat16),
            jax.ShapeDtypeStruct((length, 2 * kv_width), jnp.bfloat16),
        ],
        in_specs=[pl.BlockSpec(memory_space=pltpu.SMEM)] + [vmem] * 3,
        out_specs=[vmem] * 3,
        scratch_shapes=[
            pltpu.VMEM((window, columns), jnp.bfloat16),
            pltpu.VMEM((window, columns), jnp.bfloat16),
        ],
        compiler_params=pltpu.CompilerParams(vmem_limit_bytes=40 * 1024 * 1024),
        cost_estimate=pl.CostEstimate(
            flops=flops, bytes_accessed=4 * 2 * tokens * query_width, transcendentals=window * columns
        ),
        name="layer",
    )(doc_lengths, query_rows, grad_out, kv)
    kv_terms = lax.all_to_all(
        kv_terms.reshape(devices, tokens, 2 * kv_width), "ulysses", split_axis=0, concat_axis=0
    )
    total = jnp.sum(kv_terms.astype(jnp.float32), axis=0).astype(jnp.bfloat16)
    return (attention, grad_queries, total[:, :kv_width], total[:, kv_width:])


def solution(mesh):
    rows = P(("dp", "ulysses"), None)
    return jax.shard_map(
        functools.partial(per_device, mesh.shape["ulysses"]),
        mesh=mesh,
        in_specs=(rows, rows, rows, rows, P()),
        out_specs=(rows, rows, rows, rows),
        check_vma=False,
    )
```

```python
import functools
import math

import jax
import jax.numpy as jnp
from jax import lax
from jax.experimental import pallas as pl
from jax.experimental.pallas import tpu as pltpu
from jax.sharding import PartitionSpec as P

HD = 128
PAIR = 2
masked_score = -1e30

NT = (((1,), (1,)), ((), ()))
TN = (((0,), (0,)), ((), ()))


def dot(a, b, dims=(((1,), (0,)), ((), ()))):
    return lax.dot_general(a, b, dims, preferred_element_type=jnp.float32)


def layer_kernel(shifts, shared_heads, doc_ref, query_ref, grad_ref, key_ref, value_ref, *refs):
    out_ref, query_grad_ref, kv_grad_ref, weights_ref, scores_grad_ref = refs
    tokens = query_ref.shape[0]
    group_size = query_ref.shape[1] // HD // shared_heads
    pairs = group_size // PAIR
    score_scale = 1.0 / math.sqrt(HD)

    row = lax.axis_index("dp")
    place = lax.axis_index("ulysses")
    query_pos = place * tokens + lax.broadcasted_iota(jnp.int32, (1, tokens), 1)
    first_key = jnp.zeros((1, tokens), jnp.int32)
    doc_end = jnp.int32(0)
    for doc in range(doc_ref.shape[1]):
        doc_end = doc_end + doc_ref[row, doc]
        first_key = jnp.where(doc_end <= query_pos, doc_end, first_key)
    window = (shifts + 1) * tokens
    window_start = pl.multiple_of(jnp.maximum(place - shifts, 0) * tokens, tokens)
    key_pos = window_start + lax.broadcasted_iota(jnp.int32, (window, tokens), 0)
    allowed = (key_pos >= first_key) & (key_pos <= query_pos)
    bias = jnp.where(allowed, 0.0, masked_score)
    bias = jnp.concatenate([bias] * PAIR, axis=1)
    kv_grad_ref[...] = jnp.zeros_like(kv_grad_ref)

    def group(shared):
        def lanes(head):
            start = head * HD
            return pl.ds(start if isinstance(start, int) else pl.multiple_of(start, HD), HD)

        rows = pl.ds(window_start, window)
        keys = key_ref[rows, lanes(shared)]
        values = value_ref[rows, lanes(shared)]
        first_head = shared * group_size
        queries = jnp.concatenate(
            [query_ref[:, lanes(first_head + h)] for h in range(group_size)], axis=0
        )
        grads = jnp.concatenate(
            [grad_ref[:, lanes(first_head + h)] for h in range(group_size)], axis=0
        )
        for pair in range(pairs):
            part = slice(pair * PAIR * tokens, (pair + 1) * PAIR * tokens)
            scores = dot(keys, queries[part], NT) * (score_scale * math.log2(math.e)) + bias
            weights = jnp.exp2(scores - jnp.max(scores, axis=0, keepdims=True))
            weights = weights * (1.0 / jnp.sum(weights, axis=0, keepdims=True))
            weights_low = weights.astype(jnp.bfloat16)
            weights_ref[:, part] = weights_low
            out = dot(values, weights_low, TN)
            grad_weights = dot(values, grads[part], NT)
            row_dots = jnp.sum(weights * grad_weights, axis=0, keepdims=True)
            grad_scores = (weights * (grad_weights - row_dots)).astype(jnp.bfloat16)
            scores_grad_ref[:, part] = grad_scores
            query_grad = dot(keys, grad_scores, TN) * score_scale
            for member in range(PAIR):
                own = slice(member * tokens, (member + 1) * tokens)
                at = lanes(first_head + pair * PAIR + member)
                out_ref[:, at] = out[:, own].T.astype(jnp.bfloat16)
                query_grad_ref[:, at] = query_grad[:, own].T.astype(jnp.bfloat16)
        value_grad = dot(weights_ref[...], grads)
        key_grad = dot(scores_grad_ref[...], queries) * score_scale
        kv_grad_ref[rows, lanes(shared)] = key_grad.astype(jnp.bfloat16)
        kv_grad_ref[rows, lanes(shared_heads + shared)] = value_grad.astype(jnp.bfloat16)

    if shared_heads == 1:
        group(0)
    else:
        pl.loop(0, shared_heads)(group)


def per_device(devices, query_rows, key_rows, value_rows, grad_out, doc_lengths):
    tokens, query_width = query_rows.shape
    kv_width = key_rows.shape[1]
    shared_heads = kv_width // HD
    length = tokens * devices
    shifts = min(devices - 1, (length // 2 - 1 + tokens - 1) // tokens)

    keys = lax.all_gather(key_rows, "ulysses", axis=0, tiled=True)
    values = lax.all_gather(value_rows, "ulysses", axis=0, tiled=True)

    window = (shifts + 1) * tokens
    columns = query_width // shared_heads // HD * tokens
    vmem = pl.BlockSpec(memory_space=pltpu.VMEM)
    flops = 6 * 2 * window * columns * HD * shared_heads
    attention, grad_queries, kv_terms = pl.pallas_call(
        functools.partial(layer_kernel, shifts, shared_heads),
        out_shape=[
            jax.ShapeDtypeStruct((tokens, query_width), jnp.bfloat16),
            jax.ShapeDtypeStruct((tokens, query_width), jnp.bfloat16),
            jax.ShapeDtypeStruct((length, 2 * kv_width), jnp.bfloat16),
        ],
        in_specs=[pl.BlockSpec(memory_space=pltpu.SMEM)] + [vmem] * 4,
        out_specs=[vmem] * 3,
        scratch_shapes=[
            pltpu.VMEM((window, columns), jnp.bfloat16),
            pltpu.VMEM((window, columns), jnp.bfloat16),
        ],
        compiler_params=pltpu.CompilerParams(vmem_limit_bytes=40 * 1024 * 1024),
        cost_estimate=pl.CostEstimate(
            flops=flops, bytes_accessed=4 * 2 * tokens * query_width, transcendentals=window * columns
        ),
        name="layer",
    )(doc_lengths, query_rows, grad_out, keys, values)
    total = lax.psum_scatter(
        kv_terms.reshape(devices, tokens, 2 * kv_width), "ulysses", scatter_dimension=0
    )
    return (attention, grad_queries, total[:, :kv_width], total[:, kv_width:])


def solution(mesh):
    rows = P(("dp", "ulysses"), None)
    return jax.shard_map(
        functools.partial(per_device, mesh.shape["ulysses"]),
        mesh=mesh,
        in_specs=(rows, rows, rows, rows, P()),
        out_specs=(rows, rows, rows, rows),
        check_vma=False,
    )
```

```python
import functools
import math

import jax
import jax.numpy as jnp
from jax import lax
from jax.experimental import pallas as pl
from jax.experimental.pallas import tpu as pltpu
from jax.sharding import PartitionSpec as P

HD = 128
PAIR = 2
masked_score = -1e30

NT = (((1,), (1,)), ((), ()))
TN = (((0,), (0,)), ((), ()))


def dot(a, b, dims=(((1,), (0,)), ((), ()))):
    return lax.dot_general(a, b, dims, preferred_element_type=jnp.float32)


def doublings(reach):
    steps = []
    shift = 1
    while shift <= reach:
        steps.append((shift, min(shift, reach + 1 - shift)))
        shift *= 2
    return steps


def layer_kernel(reach, shared_heads, doc_ref, query_ref, grad_ref, *refs):
    steps = len(doublings(reach))
    kv_refs = refs[: steps + 1]
    out_ref, query_grad_ref = refs[steps + 1 : steps + 3]
    kv_grad_refs = refs[steps + 3 : -2]
    weights_ref, scores_grad_ref = refs[-2:]
    tokens = query_ref.shape[0]
    group_size = query_ref.shape[1] // HD // shared_heads
    pairs = group_size // PAIR
    score_scale = 1.0 / math.sqrt(HD)

    row = lax.axis_index("dp")
    place = lax.axis_index("ulysses")
    query_pos = place * tokens + lax.broadcasted_iota(jnp.int32, (1, tokens), 1)
    first_key = jnp.zeros((1, tokens), jnp.int32)
    doc_end = jnp.int32(0)
    for doc in range(doc_ref.shape[1]):
        doc_end = doc_end + doc_ref[row, doc]
        first_key = jnp.where(doc_end <= query_pos, doc_end, first_key)
    own_pos = lax.broadcasted_iota(jnp.int32, (tokens, tokens), 0)
    key_pos = jnp.concatenate(
        [(place - back) * tokens + own_pos for back in range(reach + 1)], axis=0
    )
    allowed = (key_pos >= first_key) & (key_pos <= query_pos)
    bias = jnp.where(allowed, 0.0, masked_score)
    bias = jnp.concatenate([bias] * PAIR, axis=1)

    def group(shared):
        def lanes(head):
            start = head * HD
            return pl.ds(start if isinstance(start, int) else pl.multiple_of(start, HD), HD)

        first_head = shared * group_size
        keys = jnp.concatenate([ref[:, lanes(shared)] for ref in kv_refs], axis=0)
        values = jnp.concatenate([ref[:, lanes(shared_heads + shared)] for ref in kv_refs], axis=0)
        queries = jnp.concatenate(
            [query_ref[:, lanes(first_head + h)] for h in range(group_size)], axis=0
        )
        grads = jnp.concatenate(
            [grad_ref[:, lanes(first_head + h)] for h in range(group_size)], axis=0
        )
        for pair in range(pairs):
            part = slice(pair * PAIR * tokens, (pair + 1) * PAIR * tokens)
            scores = dot(keys, queries[part], NT) * (score_scale * math.log2(math.e)) + bias
            weights = jnp.exp2(scores - jnp.max(scores, axis=0, keepdims=True))
            weights = weights * (1.0 / jnp.sum(weights, axis=0, keepdims=True))
            weights_low = weights.astype(jnp.bfloat16)
            weights_ref[:, part] = weights_low
            out = dot(values, weights_low, TN)
            grad_weights = dot(values, grads[part], NT)
            row_dots = jnp.sum(weights * grad_weights, axis=0, keepdims=True)
            grad_scores = (weights * (grad_weights - row_dots)).astype(jnp.bfloat16)
            scores_grad_ref[:, part] = grad_scores
            query_grad = dot(keys, grad_scores, TN) * score_scale
            for member in range(PAIR):
                own = slice(member * tokens, (member + 1) * tokens)
                at = lanes(first_head + pair * PAIR + member)
                out_ref[:, at] = out[:, own].T.astype(jnp.bfloat16)
                query_grad_ref[:, at] = query_grad[:, own].T.astype(jnp.bfloat16)
        value_grad = dot(weights_ref[...], grads)
        key_grad = dot(scores_grad_ref[...], queries) * score_scale
        start = 0
        for ref in kv_grad_refs:
            own = slice(start, start + ref.shape[0])
            ref[:, lanes(shared)] = key_grad[own].astype(ref.dtype)
            ref[:, lanes(shared_heads + shared)] = value_grad[own].astype(ref.dtype)
            start += ref.shape[0]

    if shared_heads == 1:
        group(0)
    else:
        pl.loop(0, shared_heads)(group)


def per_device(devices, query_rows, key_rows, value_rows, grad_out, doc_lengths):
    tokens, query_width = query_rows.shape
    kv_width = key_rows.shape[1]
    shared_heads = kv_width // HD
    length = tokens * devices
    reach = min(devices - 1, (length // 2 - 1 + tokens - 1) // tokens)
    steps = doublings(reach)

    blocks = [jnp.concatenate([key_rows, value_rows], axis=1)]
    held = blocks[0]
    for shift, count in steps:
        if held.shape[0] < count * tokens:
            held = jnp.concatenate(blocks, axis=0)
        blocks.append(
            lax.ppermute(
                held[: count * tokens], "ulysses", [(d, d + shift) for d in range(devices - shift)]
            )
        )

    near = 1
    while near < max([count for _, count in steps], default=1):
        near *= 2
    far_steps = [(shift, count) for shift, count in steps if shift >= near]
    window = (reach + 1) * tokens
    columns = query_width // shared_heads // HD * tokens
    vmem = pl.BlockSpec(memory_space=pltpu.VMEM)
    flops = 6 * 2 * window * columns * HD * shared_heads
    attention, grad_queries, totals, *far = pl.pallas_call(
        functools.partial(layer_kernel, reach, shared_heads),
        out_shape=[
            jax.ShapeDtypeStruct((tokens, query_width), jnp.bfloat16),
            jax.ShapeDtypeStruct((tokens, query_width), jnp.bfloat16),
            jax.ShapeDtypeStruct((near * tokens, 2 * kv_width), jnp.float32),
        ]
        + [
            jax.ShapeDtypeStruct((count * tokens, 2 * kv_width), jnp.bfloat16)
            for _, count in far_steps
        ],
        in_specs=[pl.BlockSpec(memory_space=pltpu.SMEM)] + [vmem] * (len(steps) + 3),
        out_specs=[vmem] * (len(far_steps) + 3),
        scratch_shapes=[
            pltpu.VMEM((window, columns), jnp.bfloat16),
            pltpu.VMEM((window, columns), jnp.bfloat16),
        ],
        compiler_params=pltpu.CompilerParams(vmem_limit_bytes=40 * 1024 * 1024),
        cost_estimate=pl.CostEstimate(
            flops=flops, bytes_accessed=4 * 2 * tokens * query_width, transcendentals=window * columns
        ),
        name="layer",
    )(doc_lengths, query_rows, grad_out, *blocks)
    totals = [totals[back * tokens : (back + 1) * tokens] for back in range(near)]
    for shift, count in reversed(steps):
        if shift >= near:
            terms = far.pop()
        else:
            terms = jnp.concatenate(totals[shift : shift + count], axis=0).astype(jnp.bfloat16)
        terms = lax.ppermute(terms, "ulysses", [(d, d - shift) for d in range(shift, devices)])
        for back in range(count):
            totals[back] = totals[back] + terms[back * tokens : (back + 1) * tokens].astype(
                jnp.float32
            )
    total = totals[0].astype(jnp.bfloat16)
    return (attention, grad_queries, total[:, :kv_width], total[:, kv_width:])


def solution(mesh):
    rows = P(("dp", "ulysses"), None)
    return jax.shard_map(
        functools.partial(per_device, mesh.shape["ulysses"]),
        mesh=mesh,
        in_specs=(rows, rows, rows, rows, P()),
        out_specs=(rows, rows, rows, rows),
        check_vma=False,
    )
```

```python
import functools
import math

import jax
import jax.numpy as jnp
from jax import lax
from jax.experimental import pallas as pl
from jax.experimental.pallas import tpu as pltpu
from jax.sharding import PartitionSpec as P

HD = 128
PAIR = 2
masked_score = -1e30
score_scale = 1.0 / math.sqrt(HD)

NN = (((1,), (0,)), ((), ()))
NT = (((1,), (1,)), ((), ()))


def dot(a, b, dims=NN):
    return lax.dot_general(a, b, dims, preferred_element_type=jnp.float32)


def doublings(reach):
    steps = []
    shift = 1
    while shift <= reach:
        steps.append((shift, min(shift, reach + 1 - shift)))
        shift *= 2
    return steps


def block(index, size):
    return slice(index * size, (index + 1) * size)


def prepare_kernel(reach, doc_ref, query_ref, grad_ref, stacked_ref, query_t_ref, grad_t_ref, bias_ref):
    tokens = query_ref.shape[0]
    row = lax.axis_index("dp")
    place = lax.axis_index("ulysses")
    query_pos = place * tokens + lax.broadcasted_iota(jnp.int32, (1, tokens), 1)
    first_key = jnp.zeros((1, tokens), jnp.int32)
    doc_end = jnp.int32(0)
    for doc in range(doc_ref.shape[1]):
        doc_end = doc_end + doc_ref[row, doc]
        first_key = jnp.where(doc_end <= query_pos, doc_end, first_key)
    inner = lax.broadcasted_iota(jnp.int32, (tokens, tokens), 0)
    for back in range(reach + 1):
        key_pos = (place - back) * tokens + inner
        allowed = (key_pos >= first_key) & (key_pos <= query_pos)
        bias_ref[block(back, tokens), :] = jnp.where(allowed, 0.0, masked_score).astype(
            jnp.bfloat16
        )
    identity = jnp.where(
        inner == lax.broadcasted_iota(jnp.int32, (tokens, tokens), 1), 1.0, 0.0
    ).astype(jnp.bfloat16)
    for head in range(query_ref.shape[1] // HD):
        own = block(head, tokens)
        stacked_ref[own, :] = query_ref[:, block(head, HD)]
        query_t_ref[:HD, own] = query_ref[:, block(head, HD)].T
        query_t_ref[HD:, own] = identity
        grad_t_ref[:, own] = grad_ref[:, block(head, HD)].T


def gradient_terms(rows, weights_ref, scores_grad_ref, queries, scaled_grad_t):
    key_terms = dot(scores_grad_ref[rows, :], queries) * score_scale
    value_terms = dot(weights_ref[rows, :], scaled_grad_t, NT)
    return jnp.concatenate([key_terms, value_terms], axis=1)


def scores_kernel(blocks, near, query_ref, query_t_ref, grad_t_ref, bias_ref, *refs):
    kv_refs = refs[:blocks]
    weights_ref, scores_grad_ref, out_t_ref, scaled_grad_t_ref = refs[blocks : blocks + 4]
    far_refs = refs[blocks + 4 : -1]
    scores_ref = refs[-1]
    tokens = kv_refs[0].shape[0]
    columns = query_t_ref.shape[1]
    width = min(columns, PAIR * tokens)
    exponent_scale = score_scale * math.log2(math.e)

    keys = [
        jnp.concatenate([ref[:, :HD], bias_ref[block(back, tokens), :]], axis=1)
        for back, ref in enumerate(kv_refs)
    ]
    values_t = jnp.concatenate([ref[:, HD:] for ref in kv_refs], axis=0).T
    for start in range(0, columns, width):
        part = slice(start, start + width)
        top = None
        for back in range(blocks):
            scores = dot(keys[back], query_t_ref[:, part])
            scores_ref[block(back, tokens), part] = scores
            block_top = jnp.max(scores, axis=0, keepdims=True)
            top = block_top if top is None else jnp.maximum(top, block_top)
        top = top * exponent_scale
        total = jnp.zeros((1, width), jnp.float32)
        for back in range(blocks):
            rows = block(back, tokens)
            weights = jnp.exp2(scores_ref[rows, part] * exponent_scale - top)
            total = total + jnp.sum(weights, axis=0, keepdims=True)
            weights_ref[rows, part] = weights.astype(jnp.bfloat16)
        inverse = 1.0 / total
        out_t = (dot(values_t, weights_ref[:, part]) * inverse).astype(jnp.bfloat16)
        out_t_ref[:, part] = out_t
        grad_t = grad_t_ref[:, part].astype(jnp.float32) * inverse
        row_dots = jnp.sum(out_t.astype(jnp.float32) * grad_t, axis=0, keepdims=True)
        scaled_grad_t_ref[:, part] = grad_t.astype(jnp.bfloat16)
        for back in range(blocks):
            rows = block(back, tokens)
            grad_weights = dot(kv_refs[back][:, HD:], scaled_grad_t_ref[:, part])
            grad_scores = weights_ref[rows, part].astype(jnp.float32) * (grad_weights - row_dots)
            scores_grad_ref[rows, part] = grad_scores.astype(jnp.bfloat16)
    start = near * tokens
    for ref in far_refs:
        rows = slice(start, start + ref.shape[0])
        ref[...] = gradient_terms(
            rows, weights_ref, scores_grad_ref, query_ref[...], scaled_grad_t_ref[...]
        ).astype(ref.dtype)
        start += ref.shape[0]


def near_kernel(blocks, query_ref, weights_ref, scores_grad_ref, out_t_ref, scaled_grad_t_ref, *refs):
    kv_refs = refs[:blocks]
    out_ref, query_grad_ref, near_ref = refs[blocks:]
    tokens = kv_refs[0].shape[0]
    near_ref[...] = gradient_terms(
        slice(0, near_ref.shape[0]),
        weights_ref,
        scores_grad_ref,
        query_ref[...],
        scaled_grad_t_ref[...],
    )
    keys_t = jnp.concatenate([ref[:, :HD] for ref in kv_refs], axis=0).T
    query_grad_t = (dot(keys_t, scores_grad_ref[...]) * score_scale).astype(jnp.bfloat16)
    for head in range(out_ref.shape[1] // HD):
        own = block(head, tokens)
        query_grad_ref[:, block(head, HD)] = query_grad_t[:, own].T
        out_ref[:, block(head, HD)] = out_t_ref[:, own].T


def call(body, name, outs, scratch, flops, *operands):
    vmem = pl.BlockSpec(memory_space=pltpu.VMEM)
    specs = [
        pl.BlockSpec(memory_space=pltpu.SMEM) if a.dtype == jnp.int32 else vmem for a in operands
    ]
    outs = [jax.ShapeDtypeStruct(shape, dtype) for shape, dtype in outs]
    held = sum(math.prod(a.shape) * a.dtype.itemsize for a in [*operands, *outs])
    held += sum(math.prod(shape) * 4 for shape in scratch)
    return pl.pallas_call(
        body,
        out_shape=outs,
        in_specs=specs,
        out_specs=[vmem] * len(outs),
        scratch_shapes=[pltpu.VMEM(shape, jnp.float32) for shape in scratch],
        compiler_params=pltpu.CompilerParams(vmem_limit_bytes=held + 12 * 1024 * 1024),
        cost_estimate=pl.CostEstimate(flops=flops, bytes_accessed=held, transcendentals=0),
        name=name,
    )(*operands)


def per_device(devices, query_rows, key_rows, value_rows, grad_out, doc_lengths):
    tokens, query_width = query_rows.shape
    shared_heads = key_rows.shape[1] // HD
    length = tokens * devices
    reach = min(devices - 1, (length // 2 - 1 + tokens - 1) // tokens)
    blocks = reach + 1
    window = blocks * tokens
    steps = doublings(reach)
    low = jnp.bfloat16

    kv = jnp.concatenate(
        [
            rows[:, block(shared, HD)]
            for shared in range(shared_heads)
            for rows in (key_rows, value_rows)
        ],
        axis=1,
    )
    shifts = sorted(range(1, blocks), key=lambda s: (s != 2, s != 4, s != 3, s))
    arrived = {
        shift: lax.ppermute(kv, "ulysses", [(d, d + shift) for d in range(devices - shift)])
        for shift in shifts
    }
    kv_blocks = [kv] + [arrived[shift] for shift in range(1, blocks)]

    near = 1
    while near < max([count for _, count in steps], default=1):
        near *= 2
    far_steps = [(shift, count) for shift, count in steps if shift >= near]
    group_width = query_width // shared_heads
    columns = group_width // HD * tokens
    product = 2 * window * columns * HD
    attention, grad_queries, totals, far = [], [], [], []
    for shared in range(shared_heads):
        own_queries = query_rows[:, block(shared, group_width)]
        grads = grad_out[:, block(shared, group_width)]
        own_kv = [rows[:, block(shared, 2 * HD)] for rows in kv_blocks]
        queries, queries_t, grads_t, bias = call(
            functools.partial(prepare_kernel, reach),
            "prepare",
            [
                ((columns, HD), low),
                ((HD + tokens, columns), low),
                ((HD, columns), low),
                ((window, tokens), low),
            ],
            [],
            product // 4,
            doc_lengths,
            own_queries,
            grads,
        )
        weights, scores_grad, out_t, scaled_grads_t, *own_far = call(
            functools.partial(scores_kernel, blocks, near),
            "scores",
            [((window, columns), low)] * 2
            + [((HD, columns), low)] * 2
            + [((count * tokens, 2 * HD), low) for _, count in far_steps],
            [(window, columns)],
            5 * product,
            queries,
            queries_t,
            grads_t,
            bias,
            *own_kv,
        )
        own_out, own_query_grad, own_near = call(
            functools.partial(near_kernel, blocks),
            "near",
            [((tokens, group_width), low)] * 2 + [((near * tokens, 2 * HD), jnp.float32)],
            [],
            2 * product,
            queries,
            weights,
            scores_grad,
            out_t,
            scaled_grads_t,
            *own_kv,
        )
        attention.append(own_out)
        grad_queries.append(own_query_grad)
        totals.append(own_near)
        far.append(own_far)

    def side_by_side(parts):
        return parts[0] if len(parts) == 1 else jnp.concatenate(parts, axis=1)

    totals = side_by_side(totals)
    totals = [totals[block(back, tokens)] for back in range(near)]
    for shift, count in reversed(steps):
        if shift >= near:
            terms = side_by_side([own.pop() for own in far])
        else:
            terms = jnp.concatenate(totals[shift : shift + count], axis=0).astype(low)
        terms = lax.ppermute(terms, "ulysses", [(d, d - shift) for d in range(shift, devices)])
        for back in range(count):
            totals[back] = totals[back] + terms[block(back, tokens)].astype(jnp.float32)
    total = totals[0].astype(low)
    grad_keys = side_by_side([total[:, block(2 * g, HD)] for g in range(shared_heads)])
    grad_values = side_by_side([total[:, block(2 * g + 1, HD)] for g in range(shared_heads)])
    return (side_by_side(attention), side_by_side(grad_queries), grad_keys, grad_values)


def solution(mesh):
    rows = P(("dp", "ulysses"), None)
    return jax.shard_map(
        functools.partial(per_device, mesh.shape["ulysses"]),
        mesh=mesh,
        in_specs=(rows, rows, rows, rows, P()),
        out_specs=(rows, rows, rows, rows),
        check_vma=False,
    )
```

```python
import functools
import math

import jax
import jax.numpy as jnp
from jax import lax
from jax.experimental import pallas as pl
from jax.experimental.pallas import tpu as pltpu
from jax.sharding import PartitionSpec as P

HD = 128
PAIR = 2
masked_score = -1e30
IN_ORDER = (0, 2, 4, 3, 1)
OUT_ORDER = (0, 3, 4, 1, 2)
score_scale = 1.0 / math.sqrt(HD)

NN = (((1,), (0,)), ((), ()))
NT = (((1,), (1,)), ((), ()))


def dot(a, b, dims=NN):
    return lax.dot_general(a, b, dims, preferred_element_type=jnp.float32)


def block(index, size):
    return slice(index * size, (index + 1) * size)


def fetch(pairs, sems):
    copies = [pltpu.make_async_copy(src, dst, sems.at[i]) for i, (src, dst) in enumerate(pairs)]
    for copy in copies:
        copy.start()
    return copies


def join_kernel(key_hbm, value_hbm, kv_ref, sems):
    pairs = []
    for shared in range(key_hbm.shape[1] // HD):
        for part, ref in enumerate((key_hbm, value_hbm)):
            pairs.append(
                (ref.at[:, pl.ds(shared * HD, HD)], kv_ref.at[:, pl.ds((2 * shared + part) * HD, HD)])
            )
    for copy in fetch(pairs, sems):
        copy.wait()


def prepare_kernel(reach, doc_hbm, query_hbm, grad_hbm, *refs):
    stacked_ref, query_t_ref, grad_t_ref, bias_ref, doc_ref, query_ref, grad_ref, sems = refs
    docs_in, queries_in, grads_in = fetch(
        [(doc_hbm, doc_ref), (query_hbm, query_ref), (grad_hbm, grad_ref)], sems
    )
    tokens = query_ref.shape[0]
    row = lax.axis_index("dp")
    place = lax.axis_index("ulysses")
    query_pos = place * tokens + lax.broadcasted_iota(jnp.int32, (1, tokens), 1)
    first_key = jnp.zeros((1, tokens), jnp.int32)
    docs_in.wait()
    doc_end = jnp.int32(0)
    for doc in range(doc_ref.shape[1]):
        doc_end = doc_end + doc_ref[row, doc]
        first_key = jnp.where(doc_end <= query_pos, doc_end, first_key)
    inner = lax.broadcasted_iota(jnp.int32, (tokens, tokens), 0)
    for back in range(reach + 1):
        key_pos = (place - back) * tokens + inner
        allowed = (key_pos >= first_key) & (key_pos <= query_pos)
        bias_ref[block(back, tokens), :] = jnp.where(allowed, 0.0, masked_score).astype(
            jnp.bfloat16
        )
    identity = jnp.where(
        inner == lax.broadcasted_iota(jnp.int32, (tokens, tokens), 1), 1.0, 0.0
    ).astype(jnp.bfloat16)
    queries_in.wait()
    for head in range(query_ref.shape[1] // HD):
        own = block(head, tokens)
        stacked_ref[own, :] = query_ref[:, block(head, HD)]
        query_t_ref[:HD, own] = query_ref[:, block(head, HD)].T
        query_t_ref[HD:, own] = identity
    grads_in.wait()
    for head in range(query_ref.shape[1] // HD):
        own = block(head, tokens)
        grad_t_ref[:, own] = grad_ref[:, block(head, HD)].T


def gradient_terms(rows, weights_ref, scores_grad_ref, queries, scaled_grad_t):
    key_terms = dot(scores_grad_ref[rows, :], queries) * score_scale
    value_terms = dot(weights_ref[rows, :], scaled_grad_t, NT)
    return jnp.concatenate([key_terms, value_terms], axis=1)


def scores_kernel(order, query_ref, query_t_ref, grad_t_ref, bias_ref, *refs):
    blocks = len(order)
    kv_refs = [refs[order.index(back)] for back in range(blocks)]
    weights_ref, scores_grad_ref, out_t_ref, scaled_grad_t_ref = refs[blocks : blocks + 4]
    far_refs = refs[blocks + 4 : -1]
    scores_ref = refs[-1]
    tokens = kv_refs[0].shape[0]
    columns = query_t_ref.shape[1]
    width = min(columns, PAIR * tokens)
    exponent_scale = score_scale * math.log2(math.e)

    keys = [
        jnp.concatenate([ref[:, :HD], bias_ref[block(back, tokens), :]], axis=1)
        for back, ref in enumerate(kv_refs)
    ]
    values_t = jnp.concatenate([ref[:, HD:] for ref in kv_refs], axis=0).T
    for start in range(0, columns, width):
        part = slice(start, start + width)
        top = None
        for back in range(blocks):
            scores = dot(keys[back], query_t_ref[:, part])
            scores_ref[block(back, tokens), part] = scores
            block_top = jnp.max(scores, axis=0, keepdims=True)
            top = block_top if top is None else jnp.maximum(top, block_top)
        top = top * exponent_scale
        total = jnp.zeros((1, width), jnp.float32)
        for back in range(blocks):
            rows = block(back, tokens)
            weights = jnp.exp2(scores_ref[rows, part] * exponent_scale - top)
            total = total + jnp.sum(weights, axis=0, keepdims=True)
            weights_ref[rows, part] = weights.astype(jnp.bfloat16)
        inverse = 1.0 / total
        out_t = (dot(values_t, weights_ref[:, part]) * inverse).astype(jnp.bfloat16)
        out_t_ref[:, part] = out_t
        grad_t = grad_t_ref[:, part].astype(jnp.float32) * inverse
        row_dots = jnp.sum(out_t.astype(jnp.float32) * grad_t, axis=0, keepdims=True)
        scaled_grad_t_ref[:, part] = grad_t.astype(jnp.bfloat16)
        for back in range(blocks):
            rows = block(back, tokens)
            grad_weights = dot(kv_refs[back][:, HD:], scaled_grad_t_ref[:, part])
            grad_scores = weights_ref[rows, part].astype(jnp.float32) * (grad_weights - row_dots)
            scores_grad_ref[rows, part] = grad_scores.astype(jnp.bfloat16)
    terms = gradient_terms(
        slice(tokens, blocks * tokens),
        weights_ref,
        scores_grad_ref,
        query_ref[...],
        scaled_grad_t_ref[...],
    ).astype(jnp.bfloat16)
    for back, ref in enumerate(far_refs):
        ref[...] = terms[block(back, tokens)]


def near_kernel(order, query_ref, weights_ref, scores_grad_ref, out_t_ref, scaled_grad_t_ref, *refs):
    blocks = len(order)
    kv_refs = [refs[order.index(back)] for back in range(blocks)]
    out_ref, query_grad_ref, near_ref = refs[blocks:]
    tokens = kv_refs[0].shape[0]
    near_ref[...] = gradient_terms(
        slice(0, near_ref.shape[0]),
        weights_ref,
        scores_grad_ref,
        query_ref[...],
        scaled_grad_t_ref[...],
    )
    keys_t = jnp.concatenate([ref[:, :HD] for ref in kv_refs], axis=0).T
    query_grad_t = (dot(keys_t, scores_grad_ref[...]) * score_scale).astype(jnp.bfloat16)
    for head in range(out_ref.shape[1] // HD):
        own = block(head, tokens)
        query_grad_ref[:, block(head, HD)] = query_grad_t[:, own].T
        out_ref[:, block(head, HD)] = out_t_ref[:, own].T


def call(body, name, outs, scratch, flops, *operands, fetched=False):
    vmem = pl.BlockSpec(memory_space=pltpu.VMEM)
    if fetched:
        operands = [pltpu.with_memory_space_constraint(a, pltpu.HBM) for a in operands]
    held = sum(math.prod(a.shape) * a.dtype.itemsize for a in operands)
    held += sum(math.prod(shape) * dtype.dtype.itemsize for shape, dtype in outs)
    held += sum(math.prod(s.shape) * 4 for s in scratch if hasattr(s, "shape"))
    return pl.pallas_call(
        body,
        out_shape=[jax.ShapeDtypeStruct(shape, dtype) for shape, dtype in outs],
        in_specs=[pl.BlockSpec(memory_space=pltpu.HBM) if fetched else vmem] * len(operands),
        out_specs=[vmem] * len(outs),
        scratch_shapes=scratch,
        compiler_params=pltpu.CompilerParams(
            vmem_limit_bytes=held + 12 * 1024 * 1024
        ),
        cost_estimate=pl.CostEstimate(flops=flops, bytes_accessed=held, transcendentals=0),
        name=name,
    )(*operands)


def ordered(values, order):
    first = [values[place] for place in order if place < len(values)]
    return first + [v for place, v in enumerate(values) if place not in order]


def per_device(devices, query_rows, key_rows, value_rows, grad_out, doc_lengths):
    tokens, query_width = query_rows.shape
    shared_heads = key_rows.shape[1] // HD
    length = tokens * devices
    reach = min(devices - 1, (length // 2 - 1 + tokens - 1) // tokens)
    blocks = reach + 1
    window = blocks * tokens
    low = jnp.bfloat16

    (kv,) = call(
        join_kernel,
        "join",
        [((tokens, 2 * shared_heads * HD), low)],
        [pltpu.SemaphoreType.DMA((2 * shared_heads,))],
        0,
        key_rows,
        value_rows,
        fetched=True,
    )
    order = ordered(list(range(blocks)), IN_ORDER)
    kv_blocks = [
        lax.ppermute(kv, "ulysses", [(d, d + back) for d in range(devices - back)]) if back else kv
        for back in order
    ]

    group_width = query_width // shared_heads
    columns = group_width // HD * tokens
    product = 2 * window * columns * HD
    attention, grad_queries, totals, far = [], [], [], []
    for shared in range(shared_heads):
        own_queries = query_rows[:, block(shared, group_width)]
        own_grads = grad_out[:, block(shared, group_width)]
        own_kv = [rows[:, block(shared, 2 * HD)] for rows in kv_blocks]
        queries, queries_t, grads_t, bias = call(
            functools.partial(prepare_kernel, reach),
            "prepare",
            [
                ((columns, HD), low),
                ((HD + tokens, columns), low),
                ((HD, columns), low),
                ((window, tokens), low),
            ],
            [
                pltpu.SMEM(doc_lengths.shape, jnp.int32),
                pltpu.VMEM((tokens, group_width), low),
                pltpu.VMEM((tokens, group_width), low),
                pltpu.SemaphoreType.DMA((3,)),
            ],
            product // 4,
            doc_lengths,
            own_queries,
            own_grads,
            fetched=True,
        )
        weights, scores_grad, out_t, scaled_grads_t, *own_far = call(
            functools.partial(scores_kernel, order),
            "scores",
            [((window, columns), low)] * 2
            + [((HD, columns), low)] * 2
            + [((tokens, 2 * HD), low)] * reach,
            [pltpu.VMEM((window, columns), jnp.float32)],
            5 * product,
            queries,
            queries_t,
            grads_t,
            bias,
            *own_kv,
        )
        own_out, own_query_grad, own_total = call(
            functools.partial(near_kernel, order),
            "near",
            [((tokens, group_width), low)] * 2 + [((tokens, 2 * HD), jnp.float32)],
            [],
            2 * product,
            queries,
            weights,
            scores_grad,
            out_t,
            scaled_grads_t,
            *own_kv,
        )
        attention.append(own_out)
        grad_queries.append(own_query_grad)
        totals.append(own_total)
        far.append(own_far)

    def side_by_side(parts):
        return parts[0] if len(parts) == 1 else jnp.concatenate(parts, axis=1)

    total = side_by_side(totals)
    for back in ordered(list(range(blocks)), OUT_ORDER)[1:]:
        terms = side_by_side([own[back - 1] for own in far])
        terms = lax.ppermute(terms, "ulysses", [(d, d - back) for d in range(back, devices)])
        total = total + terms.astype(jnp.float32)
    total = total.astype(low)
    grad_keys = side_by_side([total[:, block(2 * g, HD)] for g in range(shared_heads)])
    grad_values = side_by_side([total[:, block(2 * g + 1, HD)] for g in range(shared_heads)])
    return (side_by_side(attention), side_by_side(grad_queries), grad_keys, grad_values)


def solution(mesh):
    rows = P(("dp", "ulysses"), None)
    return jax.shard_map(
        functools.partial(per_device, mesh.shape["ulysses"]),
        mesh=mesh,
        in_specs=(rows, rows, rows, rows, P()),
        out_specs=(rows, rows, rows, rows),
        check_vma=False,
    )
```

```python
import functools
import math

import jax
import jax.numpy as jnp
from jax import lax
from jax.experimental import pallas as pl
from jax.experimental.pallas import tpu as pltpu
from jax.sharding import PartitionSpec as P

HD = 128
PAIR = 2
masked_score = -1e30
IN_ORDER = (0, 2, 1, 4, 3)
OUT_ORDER = (0, 3, 4, 1, 2)
score_scale = 1.0 / math.sqrt(HD)
exponent_scale = score_scale * math.log2(math.e)

NN = (((1,), (0,)), ((), ()))
NT = (((1,), (1,)), ((), ()))


def dot(a, b, dims=NN):
    return lax.dot_general(a, b, dims, preferred_element_type=jnp.float32)


def block(index, size):
    return slice(index * size, (index + 1) * size)


def fetch(pairs, sems):
    copies = [pltpu.make_async_copy(src, dst, sems.at[i]) for i, (src, dst) in enumerate(pairs)]
    for copy in copies:
        copy.start()
    return copies


def join_kernel(key_hbm, value_hbm, kv_ref, sems):
    pairs = []
    for shared in range(key_hbm.shape[1] // HD):
        for part, ref in enumerate((key_hbm, value_hbm)):
            pairs.append(
                (ref.at[:, pl.ds(shared * HD, HD)], kv_ref.at[:, pl.ds((2 * shared + part) * HD, HD)])
            )
    for copy in fetch(pairs, sems):
        copy.wait()


def prepare_kernel(reach, doc_hbm, query_hbm, grad_hbm, *refs):
    stacked_ref, query_t_ref, grad_t_ref, bias_ref, doc_ref, query_ref, grad_ref, sems = refs
    docs_in, queries_in, grads_in = fetch(
        [(doc_hbm, doc_ref), (query_hbm, query_ref), (grad_hbm, grad_ref)], sems
    )
    tokens = query_ref.shape[0]
    row = lax.axis_index("dp")
    place = lax.axis_index("ulysses")
    query_pos = place * tokens + lax.broadcasted_iota(jnp.int32, (1, tokens), 1)
    first_key = jnp.zeros((1, tokens), jnp.int32)
    docs_in.wait()
    doc_end = jnp.int32(0)
    for doc in range(doc_ref.shape[1]):
        doc_end = doc_end + doc_ref[row, doc]
        first_key = jnp.where(doc_end <= query_pos, doc_end, first_key)
    inner = lax.broadcasted_iota(jnp.int32, (tokens, tokens), 0)
    for back in range(reach + 1):
        key_pos = (place - back) * tokens + inner
        allowed = (key_pos >= first_key) & (key_pos <= query_pos)
        bias_ref[block(back, tokens), :] = jnp.where(allowed, 0.0, masked_score).astype(
            jnp.bfloat16
        )
    identity = jnp.where(
        inner == lax.broadcasted_iota(jnp.int32, (tokens, tokens), 1), 1.0, 0.0
    ).astype(jnp.bfloat16)
    queries_in.wait()
    for head in range(query_ref.shape[1] // HD):
        own = block(head, tokens)
        stacked_ref[own, :] = query_ref[:, block(head, HD)]
        query_t_ref[:HD, own] = query_ref[:, block(head, HD)].T
        query_t_ref[HD:, own] = identity
    grads_in.wait()
    for head in range(query_ref.shape[1] // HD):
        own = block(head, tokens)
        grad_t_ref[:, own] = grad_ref[:, block(head, HD)].T


def gradient_terms(weights, scores_grad, queries, scaled_grad_t):
    key_terms = dot(scores_grad, queries) * score_scale
    value_terms = dot(weights, scaled_grad_t, NT)
    return jnp.concatenate([key_terms, value_terms], axis=1)


def parts(columns, tokens):
    width = min(columns, PAIR * tokens)
    return [slice(start, start + width) for start in range(0, columns, width)]


def biased_keys(kv_ref, bias_ref, back):
    tokens = kv_ref.shape[0]
    return jnp.concatenate([kv_ref[:, :HD], bias_ref[block(back, tokens), :]], axis=1)


def early_kernel(early, query_t_ref, bias_ref, *refs):
    kv_refs = refs[: len(early)]
    weights_ref, stats_ref, out_t_ref, scores_ref = refs[len(early) :]
    tokens = kv_refs[0].shape[0]
    keys = [biased_keys(ref, bias_ref, back) for back, ref in zip(early, kv_refs)]
    values_t = jnp.concatenate([ref[:, HD:] for ref in kv_refs], axis=0).T
    for part in parts(query_t_ref.shape[1], tokens):
        top = None
        for place, key_rows in enumerate(keys):
            scores = dot(key_rows, query_t_ref[:, part])
            scores_ref[block(place, tokens), part] = scores
            block_top = jnp.max(scores, axis=0, keepdims=True)
            top = block_top if top is None else jnp.maximum(top, block_top)
        top = top * exponent_scale
        total = jnp.zeros_like(top)
        for place in range(len(early)):
            rows = block(place, tokens)
            weights = jnp.exp2(scores_ref[rows, part] * exponent_scale - top)
            total = total + jnp.sum(weights, axis=0, keepdims=True)
            weights_ref[rows, part] = weights.astype(jnp.bfloat16)
        stats_ref[0:1, part] = top
        stats_ref[1:2, part] = total
        out_t_ref[:, part] = dot(values_t, weights_ref[:, part])


def late_kernel(early, late, query_ref, query_t_ref, grad_t_ref, bias_ref, *refs):
    count = len(early)
    kv_refs, late_kv_ref = refs[:count], refs[count]
    early_weights_ref, stats_ref, early_out_t_ref = refs[count + 1 : count + 4]
    late_weights_ref, scores_grad_ref, out_t_ref, scaled_grad_t_ref = refs[count + 4 : count + 8]
    late_ref, *far_refs = refs[count + 8 :]
    tokens = late_kv_ref.shape[0]
    late_keys = biased_keys(late_kv_ref, bias_ref, late)
    late_values_t = late_kv_ref[:, HD:].T
    late_rows = block(count, tokens)
    late_scaled = []
    for part in parts(query_t_ref.shape[1], tokens):
        scores = dot(late_keys, query_t_ref[:, part])
        early_top = stats_ref[0:1, part]
        top = jnp.maximum(early_top, jnp.max(scores, axis=0, keepdims=True) * exponent_scale)
        rescale = jnp.exp2(early_top - top)
        weights = jnp.exp2(scores * exponent_scale - top)
        total = rescale * stats_ref[1:2, part] + jnp.sum(weights, axis=0, keepdims=True)
        late_weights_ref[:, part] = weights.astype(jnp.bfloat16)
        inverse = 1.0 / total
        out_t = early_out_t_ref[:, part] * (rescale * inverse)
        out_t = out_t + dot(late_values_t, late_weights_ref[:, part]) * inverse
        out_t = out_t.astype(jnp.bfloat16)
        out_t_ref[:, part] = out_t
        grad_t = grad_t_ref[:, part].astype(jnp.float32) * inverse
        row_dots = jnp.sum(out_t.astype(jnp.float32) * grad_t, axis=0, keepdims=True)
        late_grad_t = grad_t.astype(jnp.bfloat16)
        late_scaled.append(late_grad_t)
        grad_weights = dot(late_kv_ref[:, HD:], late_grad_t)
        grad_scores = late_weights_ref[:, part].astype(jnp.float32) * (grad_weights - row_dots)
        scores_grad_ref[late_rows, part] = grad_scores.astype(jnp.bfloat16)
        scaled_grad_t_ref[:, part] = (grad_t * rescale).astype(jnp.bfloat16)
        row_dots = row_dots * rescale
        for place, kv_ref in enumerate(kv_refs):
            rows = block(place, tokens)
            grad_weights = dot(kv_ref[:, HD:], scaled_grad_t_ref[:, part])
            grad_scores = early_weights_ref[rows, part].astype(jnp.float32)
            grad_scores = grad_scores * (grad_weights - row_dots)
            scores_grad_ref[rows, part] = grad_scores.astype(jnp.bfloat16)
    late_ref[...] = gradient_terms(
        late_weights_ref[...],
        scores_grad_ref[late_rows, :],
        query_ref[...],
        jnp.concatenate(late_scaled, axis=1),
    ).astype(jnp.bfloat16)
    if far_refs:
        far = slice(tokens, count * tokens)
        terms = gradient_terms(
            early_weights_ref[far, :],
            scores_grad_ref[far, :],
            query_ref[...],
            scaled_grad_t_ref[...],
        ).astype(jnp.bfloat16)
        for place, ref in enumerate(far_refs):
            ref[...] = terms[block(place, tokens)]


def near_kernel(query_ref, weights_ref, scores_grad_ref, out_t_ref, scaled_grad_t_ref, *refs):
    *kv_refs, out_ref, query_grad_ref, near_ref = refs
    tokens = kv_refs[0].shape[0]
    near_ref[...] = gradient_terms(
        weights_ref[:tokens, :], scores_grad_ref[:tokens, :], query_ref[...], scaled_grad_t_ref[...]
    )
    keys_t = jnp.concatenate([ref[:, :HD] for ref in kv_refs], axis=0).T
    query_grad_t = (dot(keys_t, scores_grad_ref[...]) * score_scale).astype(jnp.bfloat16)
    for head in range(out_ref.shape[1] // HD):
        own = block(head, tokens)
        query_grad_ref[:, block(head, HD)] = query_grad_t[:, own].T
        out_ref[:, block(head, HD)] = out_t_ref[:, own].T


def call(body, name, outs, scratch, flops, *operands, fetched=False):
    vmem = pl.BlockSpec(memory_space=pltpu.VMEM)
    if fetched:
        operands = [pltpu.with_memory_space_constraint(a, pltpu.HBM) for a in operands]
    held = sum(math.prod(a.shape) * a.dtype.itemsize for a in operands)
    held += sum(math.prod(shape) * dtype.dtype.itemsize for shape, dtype in outs)
    held += sum(math.prod(s.shape) * 4 for s in scratch if hasattr(s, "shape"))
    return pl.pallas_call(
        body,
        out_shape=[jax.ShapeDtypeStruct(shape, dtype) for shape, dtype in outs],
        in_specs=[pl.BlockSpec(memory_space=pltpu.HBM) if fetched else vmem] * len(operands),
        out_specs=[vmem] * len(outs),
        scratch_shapes=scratch,
        compiler_params=pltpu.CompilerParams(
            vmem_limit_bytes=held + 12 * 1024 * 1024
        ),
        cost_estimate=pl.CostEstimate(flops=flops, bytes_accessed=held, transcendentals=0),
        name=name,
    )(*operands)


def ordered(values, order):
    first = [values[place] for place in order if place < len(values)]
    return first + [v for place, v in enumerate(values) if place not in order]


def per_device(devices, query_rows, key_rows, value_rows, grad_out, doc_lengths):
    tokens, query_width = query_rows.shape
    shared_heads = key_rows.shape[1] // HD
    length = tokens * devices
    reach = min(devices - 1, (length // 2 - 1 + tokens - 1) // tokens)
    blocks = reach + 1
    window = blocks * tokens
    low = jnp.bfloat16

    (kv,) = call(
        join_kernel,
        "join",
        [((tokens, 2 * shared_heads * HD), low)],
        [pltpu.SemaphoreType.DMA((2 * shared_heads,))],
        0,
        key_rows,
        value_rows,
        fetched=True,
    )
    kv_blocks = {0: kv}
    for back in ordered(list(range(blocks)), IN_ORDER)[1:]:
        kv_blocks[back] = lax.ppermute(
            kv, "ulysses", [(d, d + back) for d in range(devices - back)]
        )
    late = list(kv_blocks)[1]
    early = [0] + [back for back in kv_blocks if back not in (0, late)]
    places = early + [late]
    window_early = len(early) * tokens

    group_width = query_width // shared_heads
    columns = group_width // HD * tokens
    product = 2 * window * columns * HD
    attention, grad_queries, totals, far = [], [], [], []
    for shared in range(shared_heads):
        own_queries = query_rows[:, block(shared, group_width)]
        own_grads = grad_out[:, block(shared, group_width)]
        own_kv = [kv_blocks[back][:, block(shared, 2 * HD)] for back in places]
        queries, queries_t, grads_t, bias = call(
            functools.partial(prepare_kernel, reach),
            "prepare",
            [
                ((columns, HD), low),
                ((HD + tokens, columns), low),
                ((HD, columns), low),
                ((window, tokens), low),
            ],
            [
                pltpu.SMEM(doc_lengths.shape, jnp.int32),
                pltpu.VMEM((tokens, group_width), low),
                pltpu.VMEM((tokens, group_width), low),
                pltpu.SemaphoreType.DMA((3,)),
            ],
            product // 4,
            doc_lengths,
            own_queries,
            own_grads,
            fetched=True,
        )
        weights, stats, early_out_t = call(
            functools.partial(early_kernel, early),
            "early",
            [
                ((window_early, columns), low),
                ((2, columns), jnp.float32),
                ((HD, columns), jnp.float32),
            ],
            [pltpu.VMEM((window_early, columns), jnp.float32)],
            2 * product,
            queries_t,
            bias,
            *own_kv[:-1],
        )
        _, scores_grad, out_t, scaled_grads_t, *own_far = call(
            functools.partial(late_kernel, early, late),
            "late",
            [((tokens, columns), low), ((window, columns), low)]
            + [((HD, columns), low)] * 2
            + [((tokens, 2 * HD), low)] * reach,
            [],
            3 * product,
            queries,
            queries_t,
            grads_t,
            bias,
            *own_kv,
            weights,
            stats,
            early_out_t,
        )
        own_out, own_query_grad, own_total = call(
            near_kernel,
            "near",
            [((tokens, group_width), low)] * 2 + [((tokens, 2 * HD), jnp.float32)],
            [],
            2 * product,
            queries,
            weights,
            scores_grad,
            out_t,
            scaled_grads_t,
            *own_kv,
        )
        attention.append(own_out)
        grad_queries.append(own_query_grad)
        totals.append(own_total)
        far.append(own_far)

    def side_by_side(parts):
        return parts[0] if len(parts) == 1 else jnp.concatenate(parts, axis=1)

    far_places = [late] + early[1:]
    total = side_by_side(totals)
    for back in ordered(list(range(blocks)), OUT_ORDER)[1:]:
        terms = side_by_side([own[far_places.index(back)] for own in far])
        terms = lax.ppermute(terms, "ulysses", [(d, d - back) for d in range(back, devices)])
        total = total + terms.astype(jnp.float32)
    total = total.astype(low)
    grad_keys = side_by_side([total[:, block(2 * g, HD)] for g in range(shared_heads)])
    grad_values = side_by_side([total[:, block(2 * g + 1, HD)] for g in range(shared_heads)])
    return (side_by_side(attention), side_by_side(grad_queries), grad_keys, grad_values)


def solution(mesh):
    rows = P(("dp", "ulysses"), None)
    return jax.shard_map(
        functools.partial(per_device, mesh.shape["ulysses"]),
        mesh=mesh,
        in_specs=(rows, rows, rows, rows, P()),
        out_specs=(rows, rows, rows, rows),
        check_vma=False,
    )
```

```python
import functools
import math

import jax
import jax.numpy as jnp
from jax import lax
from jax.experimental import pallas as pl
from jax.experimental.pallas import tpu as pltpu
from jax.sharding import PartitionSpec as P

HD = 128
PAIR = 2
masked_score = -1e30
IN_ORDER = (0, 2, 1, 4, 3)
OUT_ORDER = (0, 3, 4, 1, 2)
score_scale = 1.0 / math.sqrt(HD)
exponent_scale = score_scale * math.log2(math.e)

NN = (((1,), (0,)), ((), ()))
NT = (((1,), (1,)), ((), ()))


def dot(a, b, dims=NN):
    return lax.dot_general(a, b, dims, preferred_element_type=jnp.float32)


def block(index, size):
    return slice(index * size, (index + 1) * size)


def fetch_kernel(doc_hbm, key_hbm, value_hbm, query_hbm, grad_hbm, *refs):
    kv_ref, query_ref, grad_ref, first_key_ref, doc_ref, sems = refs
    pairs = [(doc_hbm, doc_ref)]
    for shared in range(key_hbm.shape[1] // HD):
        for part, ref in enumerate((key_hbm, value_hbm)):
            pairs.append(
                (ref.at[:, pl.ds(shared * HD, HD)], kv_ref.at[:, pl.ds((2 * shared + part) * HD, HD)])
            )
    pairs += [(query_hbm, query_ref), (grad_hbm, grad_ref)]
    copies = [pltpu.make_async_copy(src, dst, sems.at[i]) for i, (src, dst) in enumerate(pairs)]
    for copy in copies:
        copy.start()
    tokens = query_hbm.shape[0]
    row = lax.axis_index("dp")
    place = lax.axis_index("ulysses")
    query_pos = place * tokens + lax.broadcasted_iota(jnp.int32, (1, tokens), 1)
    first_key = jnp.zeros((1, tokens), jnp.int32)
    copies[0].wait()
    doc_end = jnp.int32(0)
    for doc in range(doc_ref.shape[1]):
        doc_end = doc_end + doc_ref[row, doc]
        first_key = jnp.where(doc_end <= query_pos, doc_end, first_key)
    first_key_ref[...] = first_key
    for copy in copies[1:]:
        copy.wait()


def prepare_kernel(reach, first_key_ref, query_ref, grad_ref, *refs):
    query_rows_ref, grad_rows_ref, query_t_ref, grad_t_ref, bias_ref = refs
    tokens = query_ref.shape[0]
    place = lax.axis_index("ulysses")
    inner = lax.broadcasted_iota(jnp.int32, (tokens, tokens), 0)
    lanes = lax.broadcasted_iota(jnp.int32, (tokens, tokens), 1)
    first_key = first_key_ref[...] - place * tokens
    for back in range(reach + 1):
        key_pos = inner - back * tokens
        allowed = (key_pos >= first_key) & (key_pos <= lanes)
        bias_ref[block(back, tokens), :] = jnp.where(allowed, 0.0, masked_score).astype(
            jnp.bfloat16
        )
    identity = jnp.where(inner == lanes, 1.0, 0.0).astype(jnp.bfloat16)
    for head in range(query_ref.shape[1] // HD):
        own = block(head, tokens)
        queries = query_ref[:, block(head, HD)]
        grads = grad_ref[:, block(head, HD)]
        query_rows_ref[own, :] = queries
        grad_rows_ref[own, :] = grads
        query_t_ref[:HD, own] = queries.T
        query_t_ref[HD:, own] = identity
        grad_t_ref[:, own] = grads.T


def gradient_terms(weights, scores_grad, queries, grads):
    key_terms = dot(scores_grad, queries) * score_scale
    value_terms = dot(weights, grads)
    return jnp.concatenate([key_terms, value_terms], axis=1)


def parts(columns, tokens):
    width = min(columns, PAIR * tokens)
    return [slice(start, start + width) for start in range(0, columns, width)]


def biased_keys(kv_refs, bias_ref, places):
    tokens = kv_refs[0].shape[0]
    keys = jnp.concatenate([ref[:, :HD] for ref in kv_refs], axis=0)
    bias = jnp.concatenate([bias_ref[block(back, tokens), :] for back in places], axis=0)
    return jnp.concatenate([keys, bias], axis=1)


def early_kernel(early, query_t_ref, grad_t_ref, bias_ref, *refs):
    kv_refs = refs[: len(early)]
    weights_ref, grad_weights_ref, stats_ref, out_t_ref, scores_ref = refs[len(early) :]
    tokens = kv_refs[0].shape[0]
    columns = parts(query_t_ref.shape[1], tokens)
    keys = biased_keys(kv_refs, bias_ref, early)
    values = jnp.concatenate([ref[:, HD:] for ref in kv_refs], axis=0)
    values_t = values.T
    for part in columns:
        scores_ref[:, part] = dot(keys, query_t_ref[:, part])
    for part in columns:
        grad_weights_ref[:, part] = dot(values, grad_t_ref[:, part])
        top = jnp.max(scores_ref[:, part], axis=0, keepdims=True) * exponent_scale
        weights = jnp.exp2(scores_ref[:, part] * exponent_scale - top)
        stats_ref[0:1, part] = top
        stats_ref[1:2, part] = jnp.sum(weights, axis=0, keepdims=True)
        weights_ref[:, part] = weights.astype(jnp.bfloat16)
    for part in columns:
        out_t_ref[:, part] = dot(values_t, weights_ref[:, part])


def late_kernel(early, late, query_ref, grad_ref, query_t_ref, grad_t_ref, bias_ref, *refs):
    late_kv_ref, early_weights_ref, grad_weights_ref, stats_ref, early_out_t_ref = refs[:5]
    weights_ref, scores_grad_ref, out_t_ref, *term_refs = refs[5:]
    tokens = late_kv_ref.shape[0]
    columns = parts(query_t_ref.shape[1], tokens)
    early_rows = slice(0, len(early) * tokens)
    late_rows = block(len(early), tokens)
    keys = biased_keys([late_kv_ref], bias_ref, [late])
    values = late_kv_ref[:, HD:]
    values_t = values.T
    scores = [dot(keys, query_t_ref[:, part]) for part in columns]
    grad_weights = [dot(values, grad_t_ref[:, part]) for part in columns]
    weights, inverses, rescales = [], [], []
    for part, own in zip(columns, scores):
        early_top = stats_ref[0:1, part]
        top = jnp.maximum(early_top, jnp.max(own, axis=0, keepdims=True) * exponent_scale)
        rescale = jnp.exp2(early_top - top)
        own = jnp.exp2(own * exponent_scale - top)
        total = rescale * stats_ref[1:2, part] + jnp.sum(own, axis=0, keepdims=True)
        inverse = 1.0 / total
        weights.append(own * inverse)
        rescales.append(rescale * inverse)
        weights_ref[late_rows, part] = weights[-1].astype(jnp.bfloat16)
    row_dots = []
    for part, rescale in zip(columns, rescales):
        out_t = early_out_t_ref[:, part] * rescale + dot(values_t, weights_ref[late_rows, part])
        out_t = out_t.astype(jnp.bfloat16)
        out_t_ref[:, part] = out_t
        out_t = out_t.astype(jnp.float32) * grad_t_ref[:, part].astype(jnp.float32)
        row_dots.append(jnp.sum(out_t, axis=0, keepdims=True))
    for part, rescale, own, own_grad, dots in zip(
        columns, rescales, weights, grad_weights, row_dots
    ):
        scores_grad_ref[late_rows, part] = (own * (own_grad - dots)).astype(jnp.bfloat16)
        own = early_weights_ref[:, part].astype(jnp.float32) * rescale
        weights_ref[early_rows, part] = own.astype(jnp.bfloat16)
        scores_grad_ref[early_rows, part] = (own * (grad_weights_ref[:, part] - dots)).astype(
            jnp.bfloat16
        )
    terms = gradient_terms(
        weights_ref[tokens:, :], scores_grad_ref[tokens:, :], query_ref[...], grad_ref[...]
    ).astype(jnp.bfloat16)
    for place, ref in enumerate(term_refs):
        ref[...] = terms[block(place, tokens)]


def near_kernel(query_ref, grad_ref, weights_ref, scores_grad_ref, out_t_ref, *refs):
    *kv_refs, out_ref, query_grad_ref, near_ref = refs
    tokens = kv_refs[0].shape[0]
    near_ref[...] = gradient_terms(
        weights_ref[:tokens, :], scores_grad_ref[:tokens, :], query_ref[...], grad_ref[...]
    )
    keys_t = jnp.concatenate([ref[:, :HD] for ref in kv_refs], axis=0).T
    query_grad_t = (dot(keys_t, scores_grad_ref[...]) * score_scale).astype(jnp.bfloat16)
    for head in range(out_ref.shape[1] // HD):
        own = block(head, tokens)
        query_grad_ref[:, block(head, HD)] = query_grad_t[:, own].T
        out_ref[:, block(head, HD)] = out_t_ref[:, own].T


def call(body, name, outs, scratch, flops, *operands, fetched=False):
    vmem = pl.BlockSpec(memory_space=pltpu.VMEM)
    if fetched:
        operands = [pltpu.with_memory_space_constraint(a, pltpu.HBM) for a in operands]
    held = sum(math.prod(a.shape) * a.dtype.itemsize for a in operands)
    held += sum(math.prod(shape) * dtype.dtype.itemsize for shape, dtype in outs)
    held += sum(math.prod(s.shape) * 4 for s in scratch if hasattr(s, "shape"))
    return pl.pallas_call(
        body,
        out_shape=[jax.ShapeDtypeStruct(shape, dtype) for shape, dtype in outs],
        in_specs=[pl.BlockSpec(memory_space=pltpu.HBM) if fetched else vmem] * len(operands),
        out_specs=[vmem] * len(outs),
        scratch_shapes=scratch,
        compiler_params=pltpu.CompilerParams(
            vmem_limit_bytes=held + 12 * 1024 * 1024
        ),
        cost_estimate=pl.CostEstimate(flops=flops, bytes_accessed=held, transcendentals=0),
        name=name,
    )(*operands)


def ordered(values, order):
    first = [values[place] for place in order if place < len(values)]
    return first + [v for place, v in enumerate(values) if place not in order]


def per_device(devices, query_rows, key_rows, value_rows, grad_out, doc_lengths):
    tokens, query_width = query_rows.shape
    shared_heads = key_rows.shape[1] // HD
    length = tokens * devices
    reach = min(devices - 1, (length // 2 - 1 + tokens - 1) // tokens)
    blocks = reach + 1
    window = blocks * tokens
    low = jnp.bfloat16

    kv, query_rows, grad_out, first_key = call(
        fetch_kernel,
        "fetch",
        [
            ((tokens, 2 * shared_heads * HD), low),
            (query_rows.shape, low),
            (grad_out.shape, low),
            ((1, tokens), jnp.int32),
        ],
        [
            pltpu.SMEM(doc_lengths.shape, jnp.int32),
            pltpu.SemaphoreType.DMA((2 * shared_heads + 3,)),
        ],
        0,
        doc_lengths,
        key_rows,
        value_rows,
        query_rows,
        grad_out,
        fetched=True,
    )
    kv_blocks = {0: kv}
    for back in ordered(list(range(blocks)), IN_ORDER)[1:]:
        kv_blocks[back] = lax.ppermute(
            kv, "ulysses", [(d, d + back) for d in range(devices - back)]
        )
    late = list(kv_blocks)[1]
    early = [0] + [back for back in kv_blocks if back not in (0, late)]
    places = early + [late]
    window_early = len(early) * tokens

    group_width = query_width // shared_heads
    columns = group_width // HD * tokens
    product = 2 * window * columns * HD
    attention, grad_queries, totals, far = [], [], [], []
    for shared in range(shared_heads):
        own_queries = query_rows[:, block(shared, group_width)]
        own_grads = grad_out[:, block(shared, group_width)]
        own_kv = [kv_blocks[back][:, block(shared, 2 * HD)] for back in places]
        queries, grads, queries_t, grads_t, bias = call(
            functools.partial(prepare_kernel, reach),
            "prepare",
            [
                ((columns, HD), low),
                ((columns, HD), low),
                ((HD + tokens, columns), low),
                ((HD, columns), low),
                ((window, tokens), low),
            ],
            [],
            product // 4,
            first_key,
            own_queries,
            own_grads,
        )
        weights, grad_weights, stats, early_out_t = call(
            functools.partial(early_kernel, early),
            "early",
            [
                ((window_early, columns), low),
                ((window_early, columns), jnp.float32),
                ((2, columns), jnp.float32),
                ((HD, columns), jnp.float32),
            ],
            [pltpu.VMEM((window_early, columns), jnp.float32)],
            3 * product,
            queries_t,
            grads_t,
            bias,
            *own_kv[:-1],
        )
        weights, scores_grad, out_t, *own_far = call(
            functools.partial(late_kernel, early, late),
            "late",
            [((window, columns), low), ((window, columns), low), ((HD, columns), low)]
            + [((tokens, 2 * HD), low)] * reach,
            [],
            2 * product,
            queries,
            grads,
            queries_t,
            grads_t,
            bias,
            own_kv[-1],
            weights,
            grad_weights,
            stats,
            early_out_t,
        )
        own_out, own_query_grad, own_total = call(
            near_kernel,
            "near",
            [((tokens, group_width), low)] * 2 + [((tokens, 2 * HD), jnp.float32)],
            [],
            2 * product,
            queries,
            grads,
            weights,
            scores_grad,
            out_t,
            *own_kv,
        )
        attention.append(own_out)
        grad_queries.append(own_query_grad)
        totals.append(own_total)
        far.append(own_far)

    def side_by_side(parts):
        return parts[0] if len(parts) == 1 else jnp.concatenate(parts, axis=1)

    far_places = places[1:]
    total = side_by_side(totals)
    for back in ordered(list(range(blocks)), OUT_ORDER)[1:]:
        terms = side_by_side([own[far_places.index(back)] for own in far])
        terms = lax.ppermute(terms, "ulysses", [(d, d - back) for d in range(back, devices)])
        total = total + terms.astype(jnp.float32)
    total = total.astype(low)
    grad_keys = side_by_side([total[:, block(2 * g, HD)] for g in range(shared_heads)])
    grad_values = side_by_side([total[:, block(2 * g + 1, HD)] for g in range(shared_heads)])
    return (side_by_side(attention), side_by_side(grad_queries), grad_keys, grad_values)


def solution(mesh):
    rows = P(("dp", "ulysses"), None)
    return jax.shard_map(
        functools.partial(per_device, mesh.shape["ulysses"]),
        mesh=mesh,
        in_specs=(rows, rows, rows, rows, P()),
        out_specs=(rows, rows, rows, rows),
        check_vma=False,
    )
```

```python
import functools
import math

import jax
import jax.numpy as jnp
from jax import lax
from jax.experimental import pallas as pl
from jax.experimental.pallas import tpu as pltpu
from jax.sharding import PartitionSpec as P

HD = 128
PAIR = 2
masked_score = -1e30
IN_ORDER = (0, 2, 1, 4, 3)
OUT_ORDER = (0, 4, 3, 1, 2)
score_scale = 1.0 / math.sqrt(HD)
exponent_scale = score_scale * math.log2(math.e)

NN = (((1,), (0,)), ((), ()))
NT = (((1,), (1,)), ((), ()))


def dot(a, b, dims=NN):
    return lax.dot_general(a, b, dims, preferred_element_type=jnp.float32)


def block(index, size):
    return slice(index * size, (index + 1) * size)


def fetch_kernel(doc_hbm, key_hbm, value_hbm, kv_ref, first_key_ref, doc_ref, sems):
    pairs = [(doc_hbm, doc_ref)]
    for shared in range(key_hbm.shape[1] // HD):
        for part, ref in enumerate((key_hbm, value_hbm)):
            pairs.append(
                (ref.at[:, pl.ds(shared * HD, HD)], kv_ref.at[:, pl.ds((2 * shared + part) * HD, HD)])
            )
    copies = [pltpu.make_async_copy(src, dst, sems.at[i]) for i, (src, dst) in enumerate(pairs)]
    for copy in copies:
        copy.start()
    tokens = key_hbm.shape[0]
    row = lax.axis_index("dp")
    place = lax.axis_index("ulysses")
    query_pos = place * tokens + lax.broadcasted_iota(jnp.int32, (1, tokens), 1)
    first_key = jnp.zeros((1, tokens), jnp.int32)
    copies[0].wait()
    doc_end = jnp.int32(0)
    for doc in range(doc_ref.shape[1]):
        doc_end = doc_end + doc_ref[row, doc]
        first_key = jnp.where(doc_end <= query_pos, doc_end, first_key)
    first_key_ref[...] = first_key
    for copy in copies[1:]:
        copy.wait()


def prepare_kernel(reach, first_key_ref, query_ref, grad_ref, *refs):
    query_rows_ref, grad_rows_ref, query_t_ref, grad_t_ref, bias_ref = refs
    tokens = query_ref.shape[0]
    place = lax.axis_index("ulysses")
    inner = lax.broadcasted_iota(jnp.int32, (tokens, tokens), 0)
    lanes = lax.broadcasted_iota(jnp.int32, (tokens, tokens), 1)
    first_key = first_key_ref[...] - place * tokens
    for back in range(reach + 1):
        key_pos = inner - back * tokens
        allowed = (key_pos >= first_key) & (key_pos <= lanes)
        bias_ref[block(back, tokens), :] = jnp.where(allowed, 0.0, masked_score).astype(
            jnp.bfloat16
        )
    identity = jnp.where(inner == lanes, 1.0, 0.0).astype(jnp.bfloat16)
    for head in range(query_ref.shape[1] // HD):
        own = block(head, tokens)
        queries = query_ref[:, block(head, HD)]
        grads = grad_ref[:, block(head, HD)]
        query_rows_ref[own, :] = queries
        grad_rows_ref[own, :] = grads
        query_t_ref[:HD, own] = queries.T
        query_t_ref[HD:, own] = identity
        grad_t_ref[:, own] = grads.T


def gradient_terms(weights, scores_grad, queries, grads):
    key_terms = dot(scores_grad, queries) * score_scale
    value_terms = dot(weights, grads)
    return jnp.concatenate([key_terms, value_terms], axis=1)


def parts(columns, tokens):
    width = min(columns, PAIR * tokens)
    return [slice(start, start + width) for start in range(0, columns, width)]


def biased_keys(kv_refs, bias_ref, places):
    tokens = kv_refs[0].shape[0]
    keys = jnp.concatenate([ref[:, :HD] for ref in kv_refs], axis=0)
    bias = jnp.concatenate([bias_ref[block(back, tokens), :] for back in places], axis=0)
    return jnp.concatenate([keys, bias], axis=1)


def early_kernel(early, query_t_ref, grad_t_ref, bias_ref, *refs):
    kv_refs = refs[: len(early)]
    weights_ref, grad_weights_ref, stats_ref, out_t_ref, scores_ref = refs[len(early) :]
    tokens = kv_refs[0].shape[0]
    columns = parts(query_t_ref.shape[1], tokens)
    keys = biased_keys(kv_refs, bias_ref, early)
    values = jnp.concatenate([ref[:, HD:] for ref in kv_refs], axis=0)
    values_t = values.T
    for part in columns:
        scores_ref[:, part] = dot(keys, query_t_ref[:, part])
    for part in columns:
        grad_weights_ref[:, part] = dot(values, grad_t_ref[:, part])
        top = jnp.max(scores_ref[:, part], axis=0, keepdims=True) * exponent_scale
        weights = jnp.exp2(scores_ref[:, part] * exponent_scale - top)
        stats_ref[0:1, part] = top
        stats_ref[1:2, part] = jnp.sum(weights, axis=0, keepdims=True)
        weights_ref[:, part] = weights.astype(jnp.bfloat16)
    for part in columns:
        out_t_ref[:, part] = dot(values_t, weights_ref[:, part])


def late_kernel(early, late, query_ref, grad_ref, query_t_ref, grad_t_ref, bias_ref, *refs):
    late_kv_ref, early_weights_ref, grad_weights_ref, stats_ref, early_out_t_ref = refs[:5]
    weights_ref, scores_grad_ref, out_t_ref, *term_refs = refs[5:]
    tokens = late_kv_ref.shape[0]
    columns = parts(query_t_ref.shape[1], tokens)
    early_rows = slice(0, len(early) * tokens)
    late_rows = block(len(early), tokens)
    keys = biased_keys([late_kv_ref], bias_ref, [late])
    values = late_kv_ref[:, HD:]
    values_t = values.T
    scores = [dot(keys, query_t_ref[:, part]) for part in columns]
    grad_weights = [dot(values, grad_t_ref[:, part]) for part in columns]
    weights, inverses, rescales = [], [], []
    for part, own in zip(columns, scores):
        early_top = stats_ref[0:1, part]
        top = jnp.maximum(early_top, jnp.max(own, axis=0, keepdims=True) * exponent_scale)
        rescale = jnp.exp2(early_top - top)
        own = jnp.exp2(own * exponent_scale - top)
        total = rescale * stats_ref[1:2, part] + jnp.sum(own, axis=0, keepdims=True)
        inverse = 1.0 / total
        weights.append(own * inverse)
        rescales.append(rescale * inverse)
        weights_ref[late_rows, part] = weights[-1].astype(jnp.bfloat16)
    row_dots = []
    for part, rescale in zip(columns, rescales):
        out_t = early_out_t_ref[:, part] * rescale + dot(values_t, weights_ref[late_rows, part])
        out_t = out_t.astype(jnp.bfloat16)
        out_t_ref[:, part] = out_t
        out_t = out_t.astype(jnp.float32) * grad_t_ref[:, part].astype(jnp.float32)
        row_dots.append(jnp.sum(out_t, axis=0, keepdims=True))
    for part, rescale, own, own_grad, dots in zip(
        columns, rescales, weights, grad_weights, row_dots
    ):
        scores_grad_ref[late_rows, part] = (own * (own_grad - dots)).astype(jnp.bfloat16)
        own = early_weights_ref[:, part].astype(jnp.float32) * rescale
        weights_ref[early_rows, part] = own.astype(jnp.bfloat16)
        scores_grad_ref[early_rows, part] = (own * (grad_weights_ref[:, part] - dots)).astype(
            jnp.bfloat16
        )
    terms = gradient_terms(
        weights_ref[tokens:, :], scores_grad_ref[tokens:, :], query_ref[...], grad_ref[...]
    ).astype(jnp.bfloat16)
    for place, ref in enumerate(term_refs):
        ref[...] = terms[block(place, tokens)]


def near_kernel(query_ref, grad_ref, weights_ref, scores_grad_ref, out_t_ref, *refs):
    *kv_refs, out_ref, query_grad_ref, near_ref = refs
    tokens = kv_refs[0].shape[0]
    near_ref[...] = gradient_terms(
        weights_ref[:tokens, :], scores_grad_ref[:tokens, :], query_ref[...], grad_ref[...]
    )
    keys_t = jnp.concatenate([ref[:, :HD] for ref in kv_refs], axis=0).T
    query_grad_t = (dot(keys_t, scores_grad_ref[...]) * score_scale).astype(jnp.bfloat16)
    for head in range(out_ref.shape[1] // HD):
        own = block(head, tokens)
        query_grad_ref[:, block(head, HD)] = query_grad_t[:, own].T
        out_ref[:, block(head, HD)] = out_t_ref[:, own].T


def call(body, name, outs, scratch, flops, *operands, fetched=False):
    vmem = pl.BlockSpec(memory_space=pltpu.VMEM)
    if fetched:
        operands = [pltpu.with_memory_space_constraint(a, pltpu.HBM) for a in operands]
    held = sum(math.prod(a.shape) * a.dtype.itemsize for a in operands)
    held += sum(math.prod(shape) * dtype.dtype.itemsize for shape, dtype in outs)
    held += sum(math.prod(s.shape) * 4 for s in scratch if hasattr(s, "shape"))
    return pl.pallas_call(
        body,
        out_shape=[jax.ShapeDtypeStruct(shape, dtype) for shape, dtype in outs],
        in_specs=[pl.BlockSpec(memory_space=pltpu.HBM) if fetched else vmem] * len(operands),
        out_specs=[vmem] * len(outs),
        scratch_shapes=scratch,
        compiler_params=pltpu.CompilerParams(
            vmem_limit_bytes=held + 12 * 1024 * 1024
        ),
        cost_estimate=pl.CostEstimate(flops=flops, bytes_accessed=held, transcendentals=0),
        name=name,
    )(*operands)


def ordered(values, order):
    first = [values[place] for place in order if place < len(values)]
    return first + [v for place, v in enumerate(values) if place not in order]


def per_device(devices, query_rows, key_rows, value_rows, grad_out, doc_lengths):
    tokens, query_width = query_rows.shape
    shared_heads = key_rows.shape[1] // HD
    length = tokens * devices
    reach = min(devices - 1, (length // 2 - 1 + tokens - 1) // tokens)
    blocks = reach + 1
    window = blocks * tokens
    low = jnp.bfloat16

    group_width = query_width // shared_heads
    columns = group_width // HD * tokens
    product = 2 * window * columns * HD
    kv, first_key = call(
        fetch_kernel,
        "fetch",
        [
            ((tokens, 2 * shared_heads * HD), low),
            ((1, tokens), jnp.int32),
        ],
        [
            pltpu.SMEM(doc_lengths.shape, jnp.int32),
            pltpu.SemaphoreType.DMA((2 * shared_heads + 1,)),
        ],
        16 * product,
        doc_lengths,
        key_rows,
        value_rows,
        fetched=True,
    )
    kv_blocks = {0: kv}
    for back in ordered(list(range(blocks)), IN_ORDER)[1:]:
        kv_blocks[back] = lax.ppermute(
            kv, "ulysses", [(d, d + back) for d in range(devices - back)]
        )
    late = list(kv_blocks)[1]
    early = [0] + [back for back in kv_blocks if back not in (0, late)]
    places = early + [late]
    window_early = len(early) * tokens

    attention, grad_queries, totals, far = [], [], [], []
    for shared in range(shared_heads):
        own_queries = query_rows[:, block(shared, group_width)]
        own_grads = grad_out[:, block(shared, group_width)]
        own_kv = [kv_blocks[back][:, block(shared, 2 * HD)] for back in places]
        queries, grads, queries_t, grads_t, bias = call(
            functools.partial(prepare_kernel, reach),
            "prepare",
            [
                ((columns, HD), low),
                ((columns, HD), low),
                ((HD + tokens, columns), low),
                ((HD, columns), low),
                ((window, tokens), low),
            ],
            [],
            product // 4,
            first_key,
            own_queries,
            own_grads,
        )
        weights, grad_weights, stats, early_out_t = call(
            functools.partial(early_kernel, early),
            "early",
            [
                ((window_early, columns), low),
                ((window_early, columns), jnp.float32),
                ((2, columns), jnp.float32),
                ((HD, columns), jnp.float32),
            ],
            [pltpu.VMEM((window_early, columns), jnp.float32)],
            3 * product,
            queries_t,
            grads_t,
            bias,
            *own_kv[:-1],
        )
        weights, scores_grad, out_t, *own_far = call(
            functools.partial(late_kernel, early, late),
            "late",
            [((window, columns), low), ((window, columns), low), ((HD, columns), low)]
            + [((tokens, 2 * HD), low)] * reach,
            [],
            2 * product,
            queries,
            grads,
            queries_t,
            grads_t,
            bias,
            own_kv[-1],
            weights,
            grad_weights,
            stats,
            early_out_t,
        )
        own_out, own_query_grad, own_total = call(
            near_kernel,
            "near",
            [((tokens, group_width), low)] * 2 + [((tokens, 2 * HD), jnp.float32)],
            [],
            2 * product,
            queries,
            grads,
            weights,
            scores_grad,
            out_t,
            *own_kv,
        )
        attention.append(own_out)
        grad_queries.append(own_query_grad)
        totals.append(own_total)
        far.append(own_far)

    def side_by_side(parts):
        return parts[0] if len(parts) == 1 else jnp.concatenate(parts, axis=1)

    far_places = places[1:]
    total = side_by_side(totals)
    for back in ordered(list(range(blocks)), OUT_ORDER)[1:]:
        terms = side_by_side([own[far_places.index(back)] for own in far])
        terms = lax.ppermute(terms, "ulysses", [(d, d - back) for d in range(back, devices)])
        total = total + terms.astype(jnp.float32)
    total = total.astype(low)
    grad_keys = side_by_side([total[:, block(2 * g, HD)] for g in range(shared_heads)])
    grad_values = side_by_side([total[:, block(2 * g + 1, HD)] for g in range(shared_heads)])
    return (side_by_side(attention), side_by_side(grad_queries), grad_keys, grad_values)


def solution(mesh):
    rows = P(("dp", "ulysses"), None)
    return jax.shard_map(
        functools.partial(per_device, mesh.shape["ulysses"]),
        mesh=mesh,
        in_specs=(rows, rows, rows, rows, P()),
        out_specs=(rows, rows, rows, rows),
        check_vma=False,
    )
```

```python
import functools
import math

import jax
import jax.numpy as jnp
from jax import lax
from jax.experimental import pallas as pl
from jax.experimental.pallas import tpu as pltpu
from jax.sharding import PartitionSpec as P

HD = 128
PAIR = 2
masked_score = -1e30
IN_ORDER = (0, 2, 1, 4, 3)
OUT_ORDER = (0, 4, 3, 1, 2)
score_scale = 1.0 / math.sqrt(HD)
exponent_scale = score_scale * math.log2(math.e)

NN = (((1,), (0,)), ((), ()))
NT = (((1,), (1,)), ((), ()))


def dot(a, b, dims=NN):
    return lax.dot_general(a, b, dims, preferred_element_type=jnp.float32)


def block(index, size):
    return slice(index * size, (index + 1) * size)


def fetch_kernel(doc_hbm, key_hbm, value_hbm, kv_ref, first_key_ref, doc_ref, sems):
    pairs = [(doc_hbm, doc_ref)]
    for shared in range(key_hbm.shape[1] // HD):
        for part, ref in enumerate((key_hbm, value_hbm)):
            pairs.append(
                (ref.at[:, pl.ds(shared * HD, HD)], kv_ref.at[:, pl.ds((2 * shared + part) * HD, HD)])
            )
    copies = [pltpu.make_async_copy(src, dst, sems.at[i]) for i, (src, dst) in enumerate(pairs)]
    for copy in copies:
        copy.start()
    tokens = key_hbm.shape[0]
    row = lax.axis_index("dp")
    place = lax.axis_index("ulysses")
    query_pos = place * tokens + lax.broadcasted_iota(jnp.int32, (1, tokens), 1)
    first_key = jnp.zeros((1, tokens), jnp.int32)
    copies[0].wait()
    doc_end = jnp.int32(0)
    for doc in range(doc_ref.shape[1]):
        doc_end = doc_end + doc_ref[row, doc]
        first_key = jnp.where(doc_end <= query_pos, doc_end, first_key)
    first_key_ref[...] = first_key
    for copy in copies[1:]:
        copy.wait()


def prepare_kernel(reach, first_key_ref, query_ref, grad_ref, *refs):
    query_rows_ref, grad_rows_ref, query_t_ref, grad_t_ref, bias_ref = refs
    tokens = query_ref.shape[0]
    place = lax.axis_index("ulysses")
    inner = lax.broadcasted_iota(jnp.int32, (tokens, tokens), 0)
    lanes = lax.broadcasted_iota(jnp.int32, (tokens, tokens), 1)
    first_key = first_key_ref[...] - place * tokens
    for back in range(reach + 1):
        key_pos = inner - back * tokens
        allowed = (key_pos >= first_key) & (key_pos <= lanes)
        bias_ref[block(back, tokens), :] = jnp.where(allowed, 0.0, masked_score).astype(
            jnp.bfloat16
        )
    identity = jnp.where(inner == lanes, 1.0, 0.0).astype(jnp.bfloat16)
    for head in range(query_ref.shape[1] // HD):
        own = block(head, tokens)
        queries = query_ref[:, block(head, HD)]
        grads = grad_ref[:, block(head, HD)]
        query_rows_ref[own, :] = queries
        grad_rows_ref[own, :] = grads
        query_t_ref[:HD, own] = queries.T
        query_t_ref[HD:, own] = identity
        grad_t_ref[:, own] = grads.T


def gradient_terms(weights, scores_grad, queries, grads):
    key_terms = dot(scores_grad, queries) * score_scale
    value_terms = dot(weights, grads)
    return jnp.concatenate([key_terms, value_terms], axis=1)


def parts(columns, tokens):
    width = min(columns, PAIR * tokens)
    return [slice(start, start + width) for start in range(0, columns, width)]


def biased_keys(kv_refs, bias_ref, places):
    tokens = kv_refs[0].shape[0]
    keys = jnp.concatenate([ref[:, :HD] for ref in kv_refs], axis=0)
    bias = jnp.concatenate([bias_ref[block(back, tokens), :] for back in places], axis=0)
    return jnp.concatenate([keys, bias], axis=1)


def early_kernel(early, query_t_ref, grad_t_ref, bias_ref, *refs):
    kv_refs = refs[: len(early)]
    weights_ref, grad_weights_ref, stats_ref, out_t_ref, scores_ref = refs[len(early) :]
    tokens = kv_refs[0].shape[0]
    columns = parts(query_t_ref.shape[1], tokens)
    keys = biased_keys(kv_refs, bias_ref, early)
    values = jnp.concatenate([ref[:, HD:] for ref in kv_refs], axis=0)
    values_t = values.T
    for part in columns:
        scores_ref[:, part] = dot(keys, query_t_ref[:, part])
    for part in columns:
        grad_weights_ref[:, part] = dot(values, grad_t_ref[:, part])
        top = jnp.max(scores_ref[:, part], axis=0, keepdims=True) * exponent_scale
        weights = jnp.exp2(scores_ref[:, part] * exponent_scale - top)
        stats_ref[0:1, part] = top
        stats_ref[1:2, part] = jnp.sum(weights, axis=0, keepdims=True)
        stats_ref[2:3, part] = jnp.sum(weights * grad_weights_ref[:, part], axis=0, keepdims=True)
        weights_ref[:, part] = weights.astype(jnp.bfloat16)
    for part in columns:
        out_t_ref[:, part] = dot(values_t, weights_ref[:, part])


def late_kernel(early, late, query_ref, grad_ref, query_t_ref, grad_t_ref, bias_ref, *refs):
    late_kv_ref, early_weights_ref, grad_weights_ref, stats_ref = refs[:4]
    weights_ref, scores_grad_ref, rescale_ref, *term_refs = refs[4:]
    tokens = late_kv_ref.shape[0]
    columns = parts(query_t_ref.shape[1], tokens)
    early_rows = slice(0, len(early) * tokens)
    late_rows = block(len(early), tokens)
    keys = biased_keys([late_kv_ref], bias_ref, [late])
    values = late_kv_ref[:, HD:]
    scores = [dot(keys, query_t_ref[:, part]) for part in columns]
    grad_weights = [dot(values, grad_t_ref[:, part]) for part in columns]
    for part, own, own_grad in zip(columns, scores, grad_weights):
        early_top = stats_ref[0:1, part]
        top = jnp.maximum(early_top, jnp.max(own, axis=0, keepdims=True) * exponent_scale)
        rescale = jnp.exp2(early_top - top)
        own = jnp.exp2(own * exponent_scale - top)
        total = rescale * stats_ref[1:2, part] + jnp.sum(own, axis=0, keepdims=True)
        inverse = 1.0 / total
        own = own * inverse
        rescale = rescale * inverse
        row_dots = rescale * stats_ref[2:3, part] + jnp.sum(own * own_grad, axis=0, keepdims=True)
        rescale_ref[:, part] = rescale
        weights_ref[late_rows, part] = own.astype(jnp.bfloat16)
        scores_grad_ref[late_rows, part] = (own * (own_grad - row_dots)).astype(jnp.bfloat16)
        own = early_weights_ref[:, part].astype(jnp.float32) * rescale
        weights_ref[early_rows, part] = own.astype(jnp.bfloat16)
        scores_grad_ref[early_rows, part] = (
            own * (grad_weights_ref[:, part] - row_dots)
        ).astype(jnp.bfloat16)
    terms = gradient_terms(
        weights_ref[tokens:, :], scores_grad_ref[tokens:, :], query_ref[...], grad_ref[...]
    ).astype(jnp.bfloat16)
    for place, ref in enumerate(term_refs):
        ref[...] = terms[block(place, tokens)]


def near_kernel(query_ref, grad_ref, weights_ref, scores_grad_ref, rescale_ref, *refs):
    early_out_t_ref, *kv_refs, out_ref, query_grad_ref, near_ref = refs
    tokens = kv_refs[0].shape[0]
    late_out_t = dot(kv_refs[-1][:, HD:].T, weights_ref[-tokens:, :])
    out_t = (early_out_t_ref[...] * rescale_ref[...] + late_out_t).astype(jnp.bfloat16)
    near_ref[...] = gradient_terms(
        weights_ref[:tokens, :], scores_grad_ref[:tokens, :], query_ref[...], grad_ref[...]
    )
    keys_t = jnp.concatenate([ref[:, :HD] for ref in kv_refs], axis=0).T
    query_grad_t = (dot(keys_t, scores_grad_ref[...]) * score_scale).astype(jnp.bfloat16)
    for head in range(out_ref.shape[1] // HD):
        own = block(head, tokens)
        query_grad_ref[:, block(head, HD)] = query_grad_t[:, own].T
        out_ref[:, block(head, HD)] = out_t[:, own].T


def call(body, name, outs, scratch, flops, *operands, fetched=False):
    vmem = pl.BlockSpec(memory_space=pltpu.VMEM)
    if fetched:
        operands = [pltpu.with_memory_space_constraint(a, pltpu.HBM) for a in operands]
    held = sum(math.prod(a.shape) * a.dtype.itemsize for a in operands)
    held += sum(math.prod(shape) * dtype.dtype.itemsize for shape, dtype in outs)
    held += sum(math.prod(s.shape) * 4 for s in scratch if hasattr(s, "shape"))
    return pl.pallas_call(
        body,
        out_shape=[jax.ShapeDtypeStruct(shape, dtype) for shape, dtype in outs],
        in_specs=[pl.BlockSpec(memory_space=pltpu.HBM) if fetched else vmem] * len(operands),
        out_specs=[vmem] * len(outs),
        scratch_shapes=scratch,
        compiler_params=pltpu.CompilerParams(
            vmem_limit_bytes=held + 12 * 1024 * 1024
        ),
        cost_estimate=pl.CostEstimate(flops=flops, bytes_accessed=held, transcendentals=0),
        name=name,
    )(*operands)


def ordered(values, order):
    first = [values[place] for place in order if place < len(values)]
    return first + [v for place, v in enumerate(values) if place not in order]


def per_device(devices, query_rows, key_rows, value_rows, grad_out, doc_lengths):
    tokens, query_width = query_rows.shape
    shared_heads = key_rows.shape[1] // HD
    length = tokens * devices
    reach = min(devices - 1, (length // 2 - 1 + tokens - 1) // tokens)
    blocks = reach + 1
    window = blocks * tokens
    low = jnp.bfloat16

    group_width = query_width // shared_heads
    columns = group_width // HD * tokens
    product = 2 * window * columns * HD
    kv, first_key = call(
        fetch_kernel,
        "fetch",
        [
            ((tokens, 2 * shared_heads * HD), low),
            ((1, tokens), jnp.int32),
        ],
        [
            pltpu.SMEM(doc_lengths.shape, jnp.int32),
            pltpu.SemaphoreType.DMA((2 * shared_heads + 1,)),
        ],
        16 * product,
        doc_lengths,
        key_rows,
        value_rows,
        fetched=True,
    )
    kv_blocks = {0: kv}
    for back in ordered(list(range(blocks)), IN_ORDER)[1:]:
        kv_blocks[back] = lax.ppermute(
            kv, "ulysses", [(d, d + back) for d in range(devices - back)]
        )
    late = list(kv_blocks)[1]
    early = [0] + [back for back in kv_blocks if back not in (0, late)]
    places = early + [late]
    window_early = len(early) * tokens

    attention, grad_queries, totals, far = [], [], [], []
    for shared in range(shared_heads):
        own_queries = query_rows[:, block(shared, group_width)]
        own_grads = grad_out[:, block(shared, group_width)]
        own_kv = [kv_blocks[back][:, block(shared, 2 * HD)] for back in places]
        queries, grads, queries_t, grads_t, bias = call(
            functools.partial(prepare_kernel, reach),
            "prepare",
            [
                ((columns, HD), low),
                ((columns, HD), low),
                ((HD + tokens, columns), low),
                ((HD, columns), low),
                ((window, tokens), low),
            ],
            [],
            product // 4,
            first_key,
            own_queries,
            own_grads,
        )
        weights, grad_weights, stats, early_out_t = call(
            functools.partial(early_kernel, early),
            "early",
            [
                ((window_early, columns), low),
                ((window_early, columns), jnp.float32),
                ((3, columns), jnp.float32),
                ((HD, columns), jnp.float32),
            ],
            [pltpu.VMEM((window_early, columns), jnp.float32)],
            3 * product,
            queries_t,
            grads_t,
            bias,
            *own_kv[:-1],
        )
        weights, scores_grad, rescale, *own_far = call(
            functools.partial(late_kernel, early, late),
            "late",
            [((window, columns), low), ((window, columns), low), ((1, columns), jnp.float32)]
            + [((tokens, 2 * HD), low)] * reach,
            [],
            2 * product,
            queries,
            grads,
            queries_t,
            grads_t,
            bias,
            own_kv[-1],
            weights,
            grad_weights,
            stats,
        )
        own_out, own_query_grad, own_total = call(
            near_kernel,
            "near",
            [((tokens, group_width), low)] * 2 + [((tokens, 2 * HD), jnp.float32)],
            [],
            2 * product,
            queries,
            grads,
            weights,
            scores_grad,
            rescale,
            early_out_t,
            *own_kv,
        )
        attention.append(own_out)
        grad_queries.append(own_query_grad)
        totals.append(own_total)
        far.append(own_far)

    def side_by_side(parts):
        return parts[0] if len(parts) == 1 else jnp.concatenate(parts, axis=1)

    far_places = places[1:]
    total = side_by_side(totals)
    for back in ordered(list(range(blocks)), OUT_ORDER)[1:]:
        terms = side_by_side([own[far_places.index(back)] for own in far])
        terms = lax.ppermute(terms, "ulysses", [(d, d - back) for d in range(back, devices)])
        total = total + terms.astype(jnp.float32)
    total = total.astype(low)
    grad_keys = side_by_side([total[:, block(2 * g, HD)] for g in range(shared_heads)])
    grad_values = side_by_side([total[:, block(2 * g + 1, HD)] for g in range(shared_heads)])
    return (side_by_side(attention), side_by_side(grad_queries), grad_keys, grad_values)


def solution(mesh):
    rows = P(("dp", "ulysses"), None)
    return jax.shard_map(
        functools.partial(per_device, mesh.shape["ulysses"]),
        mesh=mesh,
        in_specs=(rows, rows, rows, rows, P()),
        out_specs=(rows, rows, rows, rows),
        check_vma=False,
    )
```

```python
import functools
import math

import jax
import jax.numpy as jnp
from jax import lax
from jax.experimental import pallas as pl
from jax.experimental.pallas import tpu as pltpu
from jax.sharding import PartitionSpec as P

HD = 128
PAIR = 2
masked_score = -1e30
IN_ORDER = (0, 2, 4, 3, 1)
OUT_ORDER = (0, 4, 2, 3, 1)
score_scale = 1.0 / math.sqrt(HD)
exponent_scale = score_scale * math.log2(math.e)

NN = (((1,), (0,)), ((), ()))
NT = (((1,), (1,)), ((), ()))


def dot(a, b, dims=NN):
    return lax.dot_general(a, b, dims, preferred_element_type=jnp.float32)


def block(index, size):
    return slice(index * size, (index + 1) * size)


def fetch_kernel(doc_hbm, key_hbm, value_hbm, kv_ref, first_key_ref, doc_ref, sems):
    pairs = [(doc_hbm, doc_ref)]
    for shared in range(key_hbm.shape[1] // HD):
        for part, ref in enumerate((key_hbm, value_hbm)):
            pairs.append(
                (ref.at[:, pl.ds(shared * HD, HD)], kv_ref.at[:, pl.ds((2 * shared + part) * HD, HD)])
            )
    copies = [pltpu.make_async_copy(src, dst, sems.at[i]) for i, (src, dst) in enumerate(pairs)]
    for copy in copies:
        copy.start()
    tokens = key_hbm.shape[0]
    row = lax.axis_index("dp")
    place = lax.axis_index("ulysses")
    query_pos = place * tokens + lax.broadcasted_iota(jnp.int32, (1, tokens), 1)
    first_key = jnp.zeros((1, tokens), jnp.int32)
    copies[0].wait()
    doc_end = jnp.int32(0)
    for doc in range(doc_ref.shape[1]):
        doc_end = doc_end + doc_ref[row, doc]
        first_key = jnp.where(doc_end <= query_pos, doc_end, first_key)
    first_key_ref[...] = first_key
    for copy in copies[1:]:
        copy.wait()


def prepare_kernel(reach, first_key_ref, query_ref, grad_ref, *refs):
    query_rows_ref, grad_rows_ref, query_t_ref, grad_t_ref, bias_ref = refs
    tokens = query_ref.shape[0]
    place = lax.axis_index("ulysses")
    inner = lax.broadcasted_iota(jnp.int32, (tokens, tokens), 0)
    lanes = lax.broadcasted_iota(jnp.int32, (tokens, tokens), 1)
    first_key = first_key_ref[...] - place * tokens
    for back in range(reach + 1):
        key_pos = inner - back * tokens
        allowed = (key_pos >= first_key) & (key_pos <= lanes)
        bias_ref[block(back, tokens), :] = jnp.where(allowed, 0.0, masked_score).astype(
            jnp.bfloat16
        )
    identity = jnp.where(inner == lanes, 1.0, 0.0).astype(jnp.bfloat16)
    for head in range(query_ref.shape[1] // HD):
        own = block(head, tokens)
        queries = query_ref[:, block(head, HD)]
        grads = grad_ref[:, block(head, HD)]
        query_rows_ref[own, :] = queries
        grad_rows_ref[own, :] = grads
        query_t_ref[:HD, own] = queries.T
        query_t_ref[HD:, own] = identity
        grad_t_ref[:, own] = grads.T


def gradient_terms(weights, scores_grad, queries, grads):
    key_terms = dot(scores_grad, queries) * score_scale
    value_terms = dot(weights, grads)
    return jnp.concatenate([key_terms, value_terms], axis=1)


def parts(columns, tokens):
    width = min(columns, PAIR * tokens)
    return [slice(start, start + width) for start in range(0, columns, width)]


def biased_keys(kv_refs, bias_ref, places):
    tokens = kv_refs[0].shape[0]
    keys = jnp.concatenate([ref[:, :HD] for ref in kv_refs], axis=0)
    bias = jnp.concatenate([bias_ref[block(back, tokens), :] for back in places], axis=0)
    return jnp.concatenate([keys, bias], axis=1)


def early_kernel(early, query_t_ref, grad_t_ref, bias_ref, *refs):
    *kv_refs, _, last_kv_ref = refs[: len(early) + 1]
    kv_refs.append(last_kv_ref)
    weights_ref, grad_weights_ref, stats_ref, out_t_ref, scores_ref = refs[len(early) + 1 :]
    tokens = kv_refs[0].shape[0]
    columns = parts(query_t_ref.shape[1], tokens)
    keys = biased_keys(kv_refs, bias_ref, early)
    values = jnp.concatenate([ref[:, HD:] for ref in kv_refs], axis=0)
    values_t = values.T
    for part in columns:
        scores_ref[:, part] = dot(keys, query_t_ref[:, part])
    for part in columns:
        grad_weights_ref[:, part] = dot(values, grad_t_ref[:, part])
        top = jnp.max(scores_ref[:, part], axis=0, keepdims=True) * exponent_scale
        weights = jnp.exp2(scores_ref[:, part] * exponent_scale - top)
        stats_ref[0:1, part] = top
        stats_ref[1:2, part] = jnp.sum(weights, axis=0, keepdims=True)
        stats_ref[2:3, part] = jnp.sum(weights * grad_weights_ref[:, part], axis=0, keepdims=True)
        weights_ref[:, part] = weights.astype(jnp.bfloat16)
    for part in columns:
        out_t_ref[:, part] = dot(values_t, weights_ref[:, part])


def late_kernel(early, late, query_ref, grad_ref, query_t_ref, grad_t_ref, bias_ref, *refs):
    early_weights_ref, grad_weights_ref, stats_ref, kv_ref, more_kv_ref = refs[:5]
    weights_ref, scores_grad_ref, rescale_ref, *term_refs = refs[5:]
    late_kv = kv_ref[...] + more_kv_ref[...]
    tokens = late_kv.shape[0]
    columns = parts(query_t_ref.shape[1], tokens)
    early_rows = slice(0, len(early) * tokens)
    late_rows = block(len(early), tokens)
    keys = biased_keys([late_kv], bias_ref, [late])
    values = late_kv[:, HD:]
    scores = [dot(keys, query_t_ref[:, part]) for part in columns]
    grad_weights = [dot(values, grad_t_ref[:, part]) for part in columns]
    for part, own, own_grad in zip(columns, scores, grad_weights):
        early_top = stats_ref[0:1, part]
        top = jnp.maximum(early_top, jnp.max(own, axis=0, keepdims=True) * exponent_scale)
        rescale = jnp.exp2(early_top - top)
        own = jnp.exp2(own * exponent_scale - top)
        total = rescale * stats_ref[1:2, part] + jnp.sum(own, axis=0, keepdims=True)
        inverse = 1.0 / total
        own = own * inverse
        rescale = rescale * inverse
        row_dots = rescale * stats_ref[2:3, part] + jnp.sum(own * own_grad, axis=0, keepdims=True)
        rescale_ref[:, part] = rescale
        weights_ref[late_rows, part] = own.astype(jnp.bfloat16)
        scores_grad_ref[late_rows, part] = (own * (own_grad - row_dots)).astype(jnp.bfloat16)
        own = early_weights_ref[:, part].astype(jnp.float32) * rescale
        weights_ref[early_rows, part] = own.astype(jnp.bfloat16)
        scores_grad_ref[early_rows, part] = (
            own * (grad_weights_ref[:, part] - row_dots)
        ).astype(jnp.bfloat16)
    terms = gradient_terms(
        weights_ref[tokens:, :], scores_grad_ref[tokens:, :], query_ref[...], grad_ref[...]
    ).astype(jnp.bfloat16)
    for place, ref in enumerate(term_refs):
        ref[...] = terms[block(place, tokens)]


def near_kernel(query_ref, grad_ref, weights_ref, scores_grad_ref, rescale_ref, *refs):
    early_out_t_ref, *kv_refs, out_ref, query_grad_ref, near_ref = refs
    *kv_refs, late_kv_ref, more_kv_ref = kv_refs
    tokens = late_kv_ref.shape[0]
    late_kv = late_kv_ref[...] + more_kv_ref[...]
    late_out_t = dot(late_kv[:, HD:].T, weights_ref[-tokens:, :])
    out_t = (early_out_t_ref[...] * rescale_ref[...] + late_out_t).astype(jnp.bfloat16)
    near_ref[...] = gradient_terms(
        weights_ref[:tokens, :], scores_grad_ref[:tokens, :], query_ref[...], grad_ref[...]
    )
    keys_t = jnp.concatenate([rows[:, :HD] for rows in [*kv_refs, late_kv]], axis=0).T
    query_grad_t = (dot(keys_t, scores_grad_ref[...]) * score_scale).astype(jnp.bfloat16)
    for head in range(out_ref.shape[1] // HD):
        own = block(head, tokens)
        query_grad_ref[:, block(head, HD)] = query_grad_t[:, own].T
        out_ref[:, block(head, HD)] = out_t[:, own].T


def call(body, name, outs, scratch, flops, *operands, fetched=False):
    vmem = pl.BlockSpec(memory_space=pltpu.VMEM)
    if fetched:
        operands = [pltpu.with_memory_space_constraint(a, pltpu.HBM) for a in operands]
    held = sum(math.prod(a.shape) * a.dtype.itemsize for a in operands)
    held += sum(math.prod(shape) * dtype.dtype.itemsize for shape, dtype in outs)
    held += sum(math.prod(s.shape) * 4 for s in scratch if hasattr(s, "shape"))
    return pl.pallas_call(
        body,
        out_shape=[jax.ShapeDtypeStruct(shape, dtype) for shape, dtype in outs],
        in_specs=[pl.BlockSpec(memory_space=pltpu.HBM) if fetched else vmem] * len(operands),
        out_specs=[vmem] * len(outs),
        scratch_shapes=scratch,
        compiler_params=pltpu.CompilerParams(
            vmem_limit_bytes=held + 12 * 1024 * 1024
        ),
        cost_estimate=pl.CostEstimate(flops=flops, bytes_accessed=held, transcendentals=0),
        name=name,
    )(*operands)


def ordered(values, order):
    first = [values[place] for place in order if place < len(values)]
    return first + [v for place, v in enumerate(values) if place not in order]


def per_device(devices, query_rows, key_rows, value_rows, grad_out, doc_lengths):
    tokens, query_width = query_rows.shape
    shared_heads = key_rows.shape[1] // HD
    length = tokens * devices
    reach = min(devices - 1, (length // 2 - 1 + tokens - 1) // tokens)
    blocks = reach + 1
    window = blocks * tokens
    low = jnp.bfloat16

    group_width = query_width // shared_heads
    columns = group_width // HD * tokens
    product = 2 * window * columns * HD
    kv, first_key = call(
        fetch_kernel,
        "fetch",
        [
            ((tokens, 2 * shared_heads * HD), low),
            ((1, tokens), jnp.int32),
        ],
        [
            pltpu.SMEM(doc_lengths.shape, jnp.int32),
            pltpu.SemaphoreType.DMA((2 * shared_heads + 1,)),
        ],
        16 * product,
        doc_lengths,
        key_rows,
        value_rows,
        fetched=True,
    )
    def forward(back, first, last):
        return lax.ppermute(kv, "ulysses", [(d - back, d) for d in range(max(first, back), last)])

    kv_blocks = {0: kv}
    for back in ordered(list(range(blocks)), IN_ORDER)[1:]:
        if len(kv_blocks) == 1:
            late_kv = [forward(back, reach, devices), forward(back, 0, reach)]
            kv_blocks[back] = None
        else:
            kv_blocks[back] = forward(back, 0, devices)
    late = list(kv_blocks)[1]
    early = [0] + [back for back in kv_blocks if back not in (0, late)]
    places = early + [late]
    window_early = len(early) * tokens

    attention, grad_queries, totals, far = [], [], [], []
    for shared in range(shared_heads):
        own_queries = query_rows[:, block(shared, group_width)]
        own_grads = grad_out[:, block(shared, group_width)]
        if attention:
            own_queries, attention[-1] = lax.optimization_barrier((own_queries, attention[-1]))
        own_kv = [
            rows[:, block(shared, 2 * HD)]
            for rows in [kv_blocks[back] for back in early] + late_kv
        ]
        queries, grads, queries_t, grads_t, bias = call(
            functools.partial(prepare_kernel, reach),
            "prepare",
            [
                ((columns, HD), low),
                ((columns, HD), low),
                ((HD + tokens, columns), low),
                ((HD, columns), low),
                ((window, tokens), low),
            ],
            [],
            product // 4,
            first_key,
            own_queries,
            own_grads,
        )
        weights, grad_weights, stats, early_out_t = call(
            functools.partial(early_kernel, early),
            "early",
            [
                ((window_early, columns), low),
                ((window_early, columns), jnp.float32),
                ((3, columns), jnp.float32),
                ((HD, columns), jnp.float32),
            ],
            [pltpu.VMEM((window_early, columns), jnp.float32)],
            3 * product,
            queries_t,
            grads_t,
            bias,
            *own_kv[: len(early) - 1],
            own_kv[-1],
            own_kv[len(early) - 1],
        )
        weights, scores_grad, rescale, *own_far = call(
            functools.partial(late_kernel, early, late),
            "late",
            [((window, columns), low), ((window, columns), low), ((1, columns), jnp.float32)]
            + [((tokens, 2 * HD), low)] * reach,
            [],
            2 * product,
            queries,
            grads,
            queries_t,
            grads_t,
            bias,
            weights,
            grad_weights,
            stats,
            *own_kv[len(early) :],
        )
        own_out, own_query_grad, own_total = call(
            near_kernel,
            "near",
            [((tokens, group_width), low)] * 2 + [((tokens, 2 * HD), jnp.float32)],
            [],
            2 * product,
            queries,
            grads,
            weights,
            scores_grad,
            rescale,
            early_out_t,
            *own_kv,
        )
        attention.append(own_out)
        grad_queries.append(own_query_grad)
        totals.append(own_total)
        far.append(own_far)

    def side_by_side(parts):
        return parts[0] if len(parts) == 1 else jnp.concatenate(parts, axis=1)

    far_places = places[1:]
    total = side_by_side(totals)
    for back in ordered(list(range(blocks)), OUT_ORDER)[1:]:
        terms = side_by_side([own[far_places.index(back)] for own in far])
        terms = lax.ppermute(terms, "ulysses", [(d, d - back) for d in range(back, devices)])
        total = total + terms.astype(jnp.float32)
    total = total.astype(low)
    grad_keys = side_by_side([total[:, block(2 * g, HD)] for g in range(shared_heads)])
    grad_values = side_by_side([total[:, block(2 * g + 1, HD)] for g in range(shared_heads)])
    return (side_by_side(attention), side_by_side(grad_queries), grad_keys, grad_values)


def solution(mesh):
    rows = P(("dp", "ulysses"), None)
    return jax.shard_map(
        functools.partial(per_device, mesh.shape["ulysses"]),
        mesh=mesh,
        in_specs=(rows, rows, rows, rows, P()),
        out_specs=(rows, rows, rows, rows),
        check_vma=False,
    )
```

```python
import functools
import math

import jax
import jax.numpy as jnp
from jax import lax
from jax.experimental import pallas as pl
from jax.experimental.pallas import tpu as pltpu
from jax.sharding import PartitionSpec as P

HD = 128
PAIR = 2
masked_score = -1e30
IN_ORDER = (0, 2, 1, 4, 3)
OUT_ORDER = (0, 4, 3, 2, 1)
score_scale = 1.0 / math.sqrt(HD)
exponent_scale = score_scale * math.log2(math.e)

NN = (((1,), (0,)), ((), ()))
NT = (((1,), (1,)), ((), ()))


def dot(a, b, dims=NN):
    return lax.dot_general(a, b, dims, preferred_element_type=jnp.float32)


def block(index, size):
    return slice(index * size, (index + 1) * size)


def fetch_kernel(doc_hbm, key_hbm, value_hbm, kv_ref, first_key_ref, doc_ref, sems):
    pairs = [(doc_hbm, doc_ref)]
    for shared in range(key_hbm.shape[1] // HD):
        for part, ref in enumerate((key_hbm, value_hbm)):
            pairs.append(
                (ref.at[:, pl.ds(shared * HD, HD)], kv_ref.at[:, pl.ds((2 * shared + part) * HD, HD)])
            )
    copies = [pltpu.make_async_copy(src, dst, sems.at[i]) for i, (src, dst) in enumerate(pairs)]
    for copy in copies:
        copy.start()
    tokens = key_hbm.shape[0]
    row = lax.axis_index("dp")
    place = lax.axis_index("ulysses")
    query_pos = place * tokens + lax.broadcasted_iota(jnp.int32, (1, tokens), 1)
    first_key = jnp.zeros((1, tokens), jnp.int32)
    copies[0].wait()
    doc_end = jnp.int32(0)
    for doc in range(doc_ref.shape[1]):
        doc_end = doc_end + doc_ref[row, doc]
        first_key = jnp.where(doc_end <= query_pos, doc_end, first_key)
    first_key_ref[...] = first_key
    for copy in copies[1:]:
        copy.wait()


def prepare_kernel(reach, first_key_ref, query_ref, grad_ref, *refs):
    query_rows_ref, grad_rows_ref, query_t_ref, grad_t_ref, bias_ref = refs
    tokens = query_ref.shape[0]
    place = lax.axis_index("ulysses")
    inner = lax.broadcasted_iota(jnp.int32, (tokens, tokens), 0)
    lanes = lax.broadcasted_iota(jnp.int32, (tokens, tokens), 1)
    first_key = first_key_ref[...] - place * tokens
    for back in range(reach + 1):
        key_pos = inner - back * tokens
        allowed = (key_pos >= first_key) & (key_pos <= lanes)
        bias_ref[block(back, tokens), :] = jnp.where(allowed, 0.0, masked_score).astype(
            jnp.bfloat16
        )
    identity = jnp.where(inner == lanes, 1.0, 0.0).astype(jnp.bfloat16)
    for head in range(query_ref.shape[1] // HD):
        own = block(head, tokens)
        queries = query_ref[:, block(head, HD)]
        grads = grad_ref[:, block(head, HD)]
        query_rows_ref[own, :] = queries
        grad_rows_ref[own, :] = grads
        query_t_ref[:HD, own] = queries.T
        query_t_ref[HD:, own] = identity
        grad_t_ref[:, own] = grads.T


def gradient_terms(weights, scores_grad, queries, grads):
    key_terms = dot(scores_grad, queries) * score_scale
    value_terms = dot(weights, grads)
    return jnp.concatenate([key_terms, value_terms], axis=1)


def parts(columns, tokens):
    width = min(columns, PAIR * tokens)
    return [slice(start, start + width) for start in range(0, columns, width)]


def joined(early, kv_refs):
    *kv_blocks, more = [ref[...] for ref in kv_refs]
    kv_blocks[early.index(1)] += more
    return kv_blocks


def biased_keys(kv_blocks, bias_ref, places):
    tokens = kv_blocks[0].shape[0]
    keys = jnp.concatenate([rows[:, :HD] for rows in kv_blocks], axis=0)
    bias = jnp.concatenate([bias_ref[block(back, tokens), :] for back in places], axis=0)
    return jnp.concatenate([keys, bias], axis=1)


def early_kernel(early, query_t_ref, grad_t_ref, bias_ref, *refs):
    *kv_refs, weights_ref, grad_weights_ref, stats_ref, out_t_ref, scores_ref = refs
    kv_blocks = joined(early, kv_refs)
    tokens = kv_blocks[0].shape[0]
    columns = parts(query_t_ref.shape[1], tokens)
    keys = biased_keys(kv_blocks, bias_ref, early)
    values = jnp.concatenate([rows[:, HD:] for rows in kv_blocks], axis=0)
    values_t = values.T
    for part in columns:
        scores_ref[:, part] = dot(keys, query_t_ref[:, part])
    for part in columns:
        grad_weights_ref[:, part] = dot(values, grad_t_ref[:, part])
        top = jnp.max(scores_ref[:, part], axis=0, keepdims=True) * exponent_scale
        weights = jnp.exp2(scores_ref[:, part] * exponent_scale - top)
        stats_ref[0:1, part] = top
        stats_ref[1:2, part] = jnp.sum(weights, axis=0, keepdims=True)
        stats_ref[2:3, part] = jnp.sum(weights * grad_weights_ref[:, part], axis=0, keepdims=True)
        weights_ref[:, part] = weights.astype(jnp.bfloat16)
    for part in columns:
        out_t_ref[:, part] = dot(values_t, weights_ref[:, part])


def late_kernel(early, late, query_ref, grad_ref, query_t_ref, grad_t_ref, bias_ref, *refs):
    late_kv_ref, early_weights_ref, grad_weights_ref, stats_ref = refs[:4]
    weights_ref, scores_grad_ref, rescale_ref, *term_refs = refs[4:]
    tokens = late_kv_ref.shape[0]
    columns = parts(query_t_ref.shape[1], tokens)
    early_rows = slice(0, len(early) * tokens)
    late_rows = block(len(early), tokens)
    keys = biased_keys([late_kv_ref[...]], bias_ref, [late])
    values = late_kv_ref[:, HD:]
    scores = [dot(keys, query_t_ref[:, part]) for part in columns]
    grad_weights = [dot(values, grad_t_ref[:, part]) for part in columns]
    for part, own, own_grad in zip(columns, scores, grad_weights):
        early_top = stats_ref[0:1, part]
        top = jnp.maximum(early_top, jnp.max(own, axis=0, keepdims=True) * exponent_scale)
        rescale = jnp.exp2(early_top - top)
        own = jnp.exp2(own * exponent_scale - top)
        total = rescale * stats_ref[1:2, part] + jnp.sum(own, axis=0, keepdims=True)
        inverse = 1.0 / total
        own = own * inverse
        rescale = rescale * inverse
        row_dots = rescale * stats_ref[2:3, part] + jnp.sum(own * own_grad, axis=0, keepdims=True)
        rescale_ref[:, part] = rescale
        weights_ref[late_rows, part] = own.astype(jnp.bfloat16)
        scores_grad_ref[late_rows, part] = (own * (own_grad - row_dots)).astype(jnp.bfloat16)
        own = early_weights_ref[:, part].astype(jnp.float32) * rescale
        weights_ref[early_rows, part] = own.astype(jnp.bfloat16)
        scores_grad_ref[early_rows, part] = (
            own * (grad_weights_ref[:, part] - row_dots)
        ).astype(jnp.bfloat16)
    terms = gradient_terms(
        weights_ref[tokens:, :], scores_grad_ref[tokens:, :], query_ref[...], grad_ref[...]
    ).astype(jnp.bfloat16)
    for place, ref in enumerate(term_refs):
        ref[...] = terms[block(place, tokens)]


def near_kernel(early, query_ref, grad_ref, weights_ref, scores_grad_ref, rescale_ref, *refs):
    early_out_t_ref, late_kv_ref, *kv_refs, out_ref, query_grad_ref, near_ref = refs
    tokens = late_kv_ref.shape[0]
    late_out_t = dot(late_kv_ref[:, HD:].T, weights_ref[-tokens:, :])
    out_t = (early_out_t_ref[...] * rescale_ref[...] + late_out_t).astype(jnp.bfloat16)
    near_ref[...] = gradient_terms(
        weights_ref[:tokens, :], scores_grad_ref[:tokens, :], query_ref[...], grad_ref[...]
    )
    kv_blocks = joined(early, kv_refs) + [late_kv_ref[...]]
    keys_t = jnp.concatenate([rows[:, :HD] for rows in kv_blocks], axis=0).T
    query_grad_t = (dot(keys_t, scores_grad_ref[...]) * score_scale).astype(jnp.bfloat16)
    for head in range(out_ref.shape[1] // HD):
        own = block(head, tokens)
        query_grad_ref[:, block(head, HD)] = query_grad_t[:, own].T
        out_ref[:, block(head, HD)] = out_t[:, own].T


def call(body, name, outs, scratch, flops, *operands, fetched=False):
    vmem = pl.BlockSpec(memory_space=pltpu.VMEM)
    if fetched:
        operands = [pltpu.with_memory_space_constraint(a, pltpu.HBM) for a in operands]
    held = sum(math.prod(a.shape) * a.dtype.itemsize for a in operands)
    held += sum(math.prod(shape) * dtype.dtype.itemsize for shape, dtype in outs)
    held += sum(math.prod(s.shape) * 4 for s in scratch if hasattr(s, "shape"))
    return pl.pallas_call(
        body,
        out_shape=[jax.ShapeDtypeStruct(shape, dtype) for shape, dtype in outs],
        in_specs=[pl.BlockSpec(memory_space=pltpu.HBM) if fetched else vmem] * len(operands),
        out_specs=[vmem] * len(outs),
        scratch_shapes=scratch,
        compiler_params=pltpu.CompilerParams(
            vmem_limit_bytes=held + 12 * 1024 * 1024
        ),
        cost_estimate=pl.CostEstimate(flops=flops, bytes_accessed=held, transcendentals=0),
        name=name,
    )(*operands)


def ordered(values, order):
    first = [values[place] for place in order if place < len(values)]
    return first + [v for place, v in enumerate(values) if place not in order]


def per_device(devices, query_rows, key_rows, value_rows, grad_out, doc_lengths):
    tokens, query_width = query_rows.shape
    shared_heads = key_rows.shape[1] // HD
    length = tokens * devices
    reach = min(devices - 1, (length // 2 - 1 + tokens - 1) // tokens)
    blocks = reach + 1
    window = blocks * tokens
    low = jnp.bfloat16

    group_width = query_width // shared_heads
    columns = group_width // HD * tokens
    product = 2 * window * columns * HD
    kv, first_key = call(
        fetch_kernel,
        "fetch",
        [
            ((tokens, 2 * shared_heads * HD), low),
            ((1, tokens), jnp.int32),
        ],
        [
            pltpu.SMEM(doc_lengths.shape, jnp.int32),
            pltpu.SemaphoreType.DMA((2 * shared_heads + 1,)),
        ],
        16 * product,
        doc_lengths,
        key_rows,
        value_rows,
        fetched=True,
    )
    def forward(back, first, last):
        return lax.ppermute(kv, "ulysses", [(d - back, d) for d in range(max(first, back), last)])

    previous = [forward(1, reach + 1, devices), forward(1, 0, reach + 1)]
    kv_blocks = {0: kv}
    for back in ordered(list(range(blocks)), IN_ORDER)[1:]:
        kv_blocks[back] = previous[0] if back == 1 else forward(back, 0, devices)
    late = list(kv_blocks)[1]
    early = [0] + [back for back in kv_blocks if back not in (0, late)]
    places = early + [late]
    window_early = len(early) * tokens

    attention, grad_queries, totals, far = [], [], [], []
    for shared in range(shared_heads):
        own_queries = query_rows[:, block(shared, group_width)]
        own_grads = grad_out[:, block(shared, group_width)]
        if attention:
            own_queries, attention[-1] = lax.optimization_barrier((own_queries, attention[-1]))
        own_kv = [
            rows[:, block(shared, 2 * HD)]
            for rows in [kv_blocks[back] for back in places] + previous[1:]
        ]
        early_kv = own_kv[:-2] + own_kv[-1:]
        queries, grads, queries_t, grads_t, bias = call(
            functools.partial(prepare_kernel, reach),
            "prepare",
            [
                ((columns, HD), low),
                ((columns, HD), low),
                ((HD + tokens, columns), low),
                ((HD, columns), low),
                ((window, tokens), low),
            ],
            [],
            product // 4,
            first_key,
            own_queries,
            own_grads,
        )
        weights, grad_weights, stats, early_out_t = call(
            functools.partial(early_kernel, early),
            "early",
            [
                ((window_early, columns), low),
                ((window_early, columns), jnp.float32),
                ((3, columns), jnp.float32),
                ((HD, columns), jnp.float32),
            ],
            [pltpu.VMEM((window_early, columns), jnp.float32)],
            3 * product,
            queries_t,
            grads_t,
            bias,
            *early_kv,
        )
        weights, scores_grad, rescale, *own_far = call(
            functools.partial(late_kernel, early, late),
            "late",
            [((window, columns), low), ((window, columns), low), ((1, columns), jnp.float32)]
            + [((tokens, 2 * HD), low)] * reach,
            [],
            2 * product,
            queries,
            grads,
            queries_t,
            grads_t,
            bias,
            own_kv[-2],
            weights,
            grad_weights,
            stats,
        )
        own_out, own_query_grad, own_total = call(
            functools.partial(near_kernel, early),
            "near",
            [((tokens, group_width), low)] * 2 + [((tokens, 2 * HD), jnp.float32)],
            [],
            2 * product,
            queries,
            grads,
            weights,
            scores_grad,
            rescale,
            early_out_t,
            own_kv[-2],
            *early_kv,
        )
        attention.append(own_out)
        grad_queries.append(own_query_grad)
        totals.append(own_total)
        far.append(own_far)

    def side_by_side(parts):
        return parts[0] if len(parts) == 1 else jnp.concatenate(parts, axis=1)

    far_places = places[1:]
    total = side_by_side(totals)
    for back in ordered(list(range(blocks)), OUT_ORDER)[1:]:
        terms = side_by_side([own[far_places.index(back)] for own in far])
        terms = lax.ppermute(terms, "ulysses", [(d, d - back) for d in range(back, devices)])
        total = total + terms.astype(jnp.float32)
    total = total.astype(low)
    grad_keys = side_by_side([total[:, block(2 * g, HD)] for g in range(shared_heads)])
    grad_values = side_by_side([total[:, block(2 * g + 1, HD)] for g in range(shared_heads)])
    return (side_by_side(attention), side_by_side(grad_queries), grad_keys, grad_values)


def solution(mesh):
    rows = P(("dp", "ulysses"), None)
    return jax.shard_map(
        functools.partial(per_device, mesh.shape["ulysses"]),
        mesh=mesh,
        in_specs=(rows, rows, rows, rows, P()),
        out_specs=(rows, rows, rows, rows),
        check_vma=False,
    )
```

```python
import functools
import math

import jax
import jax.numpy as jnp
from jax import lax
from jax.experimental import pallas as pl
from jax.experimental.pallas import tpu as pltpu
from jax.sharding import PartitionSpec as P

HD = 128
PAIR = 2
masked_score = -1e30
IN_ORDER = (0, 2, 1, 4, 3)
OUT_ORDER = (0, 4, 3, 2, 1)
score_scale = 1.0 / math.sqrt(HD)
exponent_scale = score_scale * math.log2(math.e)

NN = (((1,), (0,)), ((), ()))
NT = (((1,), (1,)), ((), ()))


def dot(a, b, dims=NN):
    return lax.dot_general(a, b, dims, preferred_element_type=jnp.float32)


def block(index, size):
    return slice(index * size, (index + 1) * size)


def fetch_kernel(doc_hbm, key_hbm, value_hbm, kv_ref, first_key_ref, doc_ref, sems):
    pairs = [(doc_hbm, doc_ref)]
    for shared in range(key_hbm.shape[1] // HD):
        for part, ref in enumerate((key_hbm, value_hbm)):
            pairs.append(
                (ref.at[:, pl.ds(shared * HD, HD)], kv_ref.at[:, pl.ds((2 * shared + part) * HD, HD)])
            )
    copies = [pltpu.make_async_copy(src, dst, sems.at[i]) for i, (src, dst) in enumerate(pairs)]
    for copy in copies:
        copy.start()
    tokens = key_hbm.shape[0]
    row = lax.axis_index("dp")
    place = lax.axis_index("ulysses")
    query_pos = place * tokens + lax.broadcasted_iota(jnp.int32, (1, tokens), 1)
    first_key = jnp.zeros((1, tokens), jnp.int32)
    copies[0].wait()
    doc_end = jnp.int32(0)
    for doc in range(doc_ref.shape[1]):
        doc_end = doc_end + doc_ref[row, doc]
        first_key = jnp.where(doc_end <= query_pos, doc_end, first_key)
    first_key_ref[...] = first_key
    for copy in copies[1:]:
        copy.wait()


def prepare_kernel(reach, first_key_ref, query_ref, grad_ref, *refs):
    query_rows_ref, grad_rows_ref, query_t_ref, grad_t_ref, bias_ref = refs
    tokens = query_ref.shape[0]
    place = lax.axis_index("ulysses")
    inner = lax.broadcasted_iota(jnp.int32, (tokens, tokens), 0)
    lanes = lax.broadcasted_iota(jnp.int32, (tokens, tokens), 1)
    first_key = first_key_ref[...] - place * tokens
    for back in range(reach + 1):
        key_pos = inner - back * tokens
        allowed = (key_pos >= first_key) & (key_pos <= lanes)
        bias_ref[block(back, tokens), :] = jnp.where(allowed, 0.0, masked_score).astype(
            jnp.bfloat16
        )
    identity = jnp.where(inner == lanes, 1.0, 0.0).astype(jnp.bfloat16)
    for head in range(query_ref.shape[1] // HD):
        own = block(head, tokens)
        queries = query_ref[:, block(head, HD)]
        grads = grad_ref[:, block(head, HD)]
        query_rows_ref[own, :] = queries
        grad_rows_ref[own, :] = grads
        query_t_ref[:HD, own] = queries.T
        query_t_ref[HD:, own] = identity
        grad_t_ref[:, own] = grads.T


def gradient_terms(weights, scores_grad, queries, grads):
    key_terms = dot(scores_grad, queries) * score_scale
    value_terms = dot(weights, grads)
    return jnp.concatenate([key_terms, value_terms], axis=1)


def parts(columns, tokens):
    width = min(columns, PAIR * tokens)
    return [slice(start, start + width) for start in range(0, columns, width)]


def joined(early, kv_refs):
    *kv_blocks, more = [ref[...] for ref in kv_refs]
    kv_blocks[early.index(1)] += more
    return kv_blocks


def biased_keys(kv_blocks, bias_ref, places):
    tokens = kv_blocks[0].shape[0]
    keys = jnp.concatenate([rows[:, :HD] for rows in kv_blocks], axis=0)
    bias = jnp.concatenate([bias_ref[block(back, tokens), :] for back in places], axis=0)
    return jnp.concatenate([keys, bias], axis=1)


def early_kernel(early, query_t_ref, grad_t_ref, bias_ref, *refs):
    *kv_refs, weights_ref, grad_weights_ref, stats_ref, out_t_ref, scores_ref = refs
    kv_blocks = joined(early, kv_refs)
    tokens = kv_blocks[0].shape[0]
    columns = parts(query_t_ref.shape[1], tokens)
    keys = biased_keys(kv_blocks, bias_ref, early)
    values = jnp.concatenate([rows[:, HD:] for rows in kv_blocks], axis=0)
    values_t = values.T
    for part in columns:
        scores_ref[:, part] = dot(keys, query_t_ref[:, part])
    for part in columns:
        grad_weights_ref[:, part] = dot(values, grad_t_ref[:, part])
        top = jnp.max(scores_ref[:, part], axis=0, keepdims=True) * exponent_scale
        weights = jnp.exp2(scores_ref[:, part] * exponent_scale - top)
        stats_ref[0:1, part] = top
        stats_ref[1:2, part] = jnp.sum(weights, axis=0, keepdims=True)
        stats_ref[2:3, part] = jnp.sum(weights * grad_weights_ref[:, part], axis=0, keepdims=True)
        weights_ref[:, part] = weights.astype(jnp.bfloat16)
    for part in columns:
        out_t_ref[:, part] = dot(values_t, weights_ref[:, part])


def late_kernel(early, late, query_ref, grad_ref, query_t_ref, grad_t_ref, bias_ref, *refs):
    late_kv_ref, early_weights_ref, grad_weights_ref, stats_ref = refs[:4]
    weights_ref, scores_grad_ref, rescale_ref, *term_refs = refs[4:]
    tokens = late_kv_ref.shape[0]
    columns = parts(query_t_ref.shape[1], tokens)
    early_rows = slice(0, len(early) * tokens)
    late_rows = block(len(early), tokens)
    keys = biased_keys([late_kv_ref[...]], bias_ref, [late])
    values = late_kv_ref[:, HD:]
    scores = [dot(keys, query_t_ref[:, part]) for part in columns]
    grad_weights = [dot(values, grad_t_ref[:, part]) for part in columns]
    key_terms = value_terms = jnp.zeros((len(early) * tokens, HD), jnp.float32)
    for part, own, own_grad in zip(columns, scores, grad_weights):
        early_top = stats_ref[0:1, part]
        top = jnp.maximum(early_top, jnp.max(own, axis=0, keepdims=True) * exponent_scale)
        rescale = jnp.exp2(early_top - top)
        own = jnp.exp2(own * exponent_scale - top)
        total = rescale * stats_ref[1:2, part] + jnp.sum(own, axis=0, keepdims=True)
        inverse = 1.0 / total
        own = own * inverse
        rescale = rescale * inverse
        row_dots = rescale * stats_ref[2:3, part] + jnp.sum(own * own_grad, axis=0, keepdims=True)
        rescale_ref[:, part] = rescale
        weights_ref[late_rows, part] = own.astype(jnp.bfloat16)
        scores_grad_ref[late_rows, part] = (own * (own_grad - row_dots)).astype(jnp.bfloat16)
        own = early_weights_ref[:, part].astype(jnp.float32) * rescale
        weights_ref[early_rows, part] = own.astype(jnp.bfloat16)
        scores_grad_ref[early_rows, part] = (
            own * (grad_weights_ref[:, part] - row_dots)
        ).astype(jnp.bfloat16)
        key_terms += dot(scores_grad_ref[tokens:, part], query_ref[part, :])
        value_terms += dot(weights_ref[tokens:, part], grad_ref[part, :])
    key_terms = (key_terms * score_scale).astype(jnp.bfloat16)
    value_terms = value_terms.astype(jnp.bfloat16)
    for place, ref in enumerate(term_refs):
        ref[:, :HD] = key_terms[block(place, tokens)]
        ref[:, HD:] = value_terms[block(place, tokens)]


def near_kernel(early, query_ref, grad_ref, weights_ref, scores_grad_ref, rescale_ref, *refs):
    early_out_t_ref, late_kv_ref, *kv_refs, out_ref, query_grad_ref, near_ref = refs
    tokens = late_kv_ref.shape[0]
    late_out_t = dot(late_kv_ref[:, HD:].T, weights_ref[-tokens:, :])
    out_t = (early_out_t_ref[...] * rescale_ref[...] + late_out_t).astype(jnp.bfloat16)
    near_ref[...] = gradient_terms(
        weights_ref[:tokens, :], scores_grad_ref[:tokens, :], query_ref[...], grad_ref[...]
    )
    kv_blocks = joined(early, kv_refs) + [late_kv_ref[...]]
    keys_t = jnp.concatenate([rows[:, :HD] for rows in kv_blocks], axis=0).T
    query_grad_t = (dot(keys_t, scores_grad_ref[...]) * score_scale).astype(jnp.bfloat16)
    for head in range(out_ref.shape[1] // HD):
        own = block(head, tokens)
        query_grad_ref[:, block(head, HD)] = query_grad_t[:, own].T
        out_ref[:, block(head, HD)] = out_t[:, own].T


def call(body, name, outs, scratch, flops, *operands, fetched=False):
    vmem = pl.BlockSpec(memory_space=pltpu.VMEM)
    if fetched:
        operands = [pltpu.with_memory_space_constraint(a, pltpu.HBM) for a in operands]
    held = sum(math.prod(a.shape) * a.dtype.itemsize for a in operands)
    held += sum(math.prod(shape) * dtype.dtype.itemsize for shape, dtype in outs)
    held += sum(math.prod(s.shape) * 4 for s in scratch if hasattr(s, "shape"))
    return pl.pallas_call(
        body,
        out_shape=[jax.ShapeDtypeStruct(shape, dtype) for shape, dtype in outs],
        in_specs=[pl.BlockSpec(memory_space=pltpu.HBM) if fetched else vmem] * len(operands),
        out_specs=[vmem] * len(outs),
        scratch_shapes=scratch,
        compiler_params=pltpu.CompilerParams(
            vmem_limit_bytes=held + 12 * 1024 * 1024
        ),
        cost_estimate=pl.CostEstimate(flops=flops, bytes_accessed=held, transcendentals=0),
        name=name,
    )(*operands)


def ordered(values, order):
    first = [values[place] for place in order if place < len(values)]
    return first + [v for place, v in enumerate(values) if place not in order]


def per_device(devices, query_rows, key_rows, value_rows, grad_out, doc_lengths):
    tokens, query_width = query_rows.shape
    shared_heads = key_rows.shape[1] // HD
    length = tokens * devices
    reach = min(devices - 1, (length // 2 - 1 + tokens - 1) // tokens)
    blocks = reach + 1
    window = blocks * tokens
    low = jnp.bfloat16

    group_width = query_width // shared_heads
    columns = group_width // HD * tokens
    product = 2 * window * columns * HD
    kv, first_key = call(
        fetch_kernel,
        "fetch",
        [
            ((tokens, 2 * shared_heads * HD), low),
            ((1, tokens), jnp.int32),
        ],
        [
            pltpu.SMEM(doc_lengths.shape, jnp.int32),
            pltpu.SemaphoreType.DMA((2 * shared_heads + 1,)),
        ],
        16 * product,
        doc_lengths,
        key_rows,
        value_rows,
        fetched=True,
    )
    def forward(back, first, last):
        return lax.ppermute(kv, "ulysses", [(d - back, d) for d in range(max(first, back), last)])

    previous = [forward(1, reach + 1, devices), forward(1, 0, reach + 1)]
    kv_blocks = {0: kv}
    for back in ordered(list(range(blocks)), IN_ORDER)[1:]:
        kv_blocks[back] = previous[0] if back == 1 else forward(back, 0, devices)
    late = list(kv_blocks)[1]
    early = [0] + [back for back in kv_blocks if back not in (0, late)]
    places = early + [late]
    window_early = len(early) * tokens

    attention, grad_queries, totals, far = [], [], [], []
    for shared in range(shared_heads):
        own_queries = query_rows[:, block(shared, group_width)]
        own_grads = grad_out[:, block(shared, group_width)]
        if attention:
            own_queries, attention[-1] = lax.optimization_barrier((own_queries, attention[-1]))
        own_kv = [
            rows[:, block(shared, 2 * HD)]
            for rows in [kv_blocks[back] for back in places] + previous[1:]
        ]
        early_kv = own_kv[:-2] + own_kv[-1:]
        queries, grads, queries_t, grads_t, bias = call(
            functools.partial(prepare_kernel, reach),
            "prepare",
            [
                ((columns, HD), low),
                ((columns, HD), low),
                ((HD + tokens, columns), low),
                ((HD, columns), low),
                ((window, tokens), low),
            ],
            [],
            product // 4,
            first_key,
            own_queries,
            own_grads,
        )
        weights, grad_weights, stats, early_out_t = call(
            functools.partial(early_kernel, early),
            "early",
            [
                ((window_early, columns), low),
                ((window_early, columns), jnp.float32),
                ((3, columns), jnp.float32),
                ((HD, columns), jnp.float32),
            ],
            [pltpu.VMEM((window_early, columns), jnp.float32)],
            3 * product,
            queries_t,
            grads_t,
            bias,
            *early_kv,
        )
        weights, scores_grad, rescale, *own_far = call(
            functools.partial(late_kernel, early, late),
            "late",
            [((window, columns), low), ((window, columns), low), ((1, columns), jnp.float32)]
            + [((tokens, 2 * HD), low)] * reach,
            [],
            2 * product,
            queries,
            grads,
            queries_t,
            grads_t,
            bias,
            own_kv[-2],
            weights,
            grad_weights,
            stats,
        )
        own_out, own_query_grad, own_total = call(
            functools.partial(near_kernel, early),
            "near",
            [((tokens, group_width), low)] * 2 + [((tokens, 2 * HD), jnp.float32)],
            [],
            2 * product,
            queries,
            grads,
            weights,
            scores_grad,
            rescale,
            early_out_t,
            own_kv[-2],
            *early_kv,
        )
        attention.append(own_out)
        grad_queries.append(own_query_grad)
        totals.append(own_total)
        far.append(own_far)

    def side_by_side(parts):
        return parts[0] if len(parts) == 1 else jnp.concatenate(parts, axis=1)

    far_places = places[1:]
    total = side_by_side(totals)
    for back in ordered(list(range(blocks)), OUT_ORDER)[1:]:
        terms = side_by_side([own[far_places.index(back)] for own in far])
        terms = lax.ppermute(terms, "ulysses", [(d, d - back) for d in range(back, devices)])
        total = total + terms.astype(jnp.float32)
    total = total.astype(low)
    grad_keys = side_by_side([total[:, block(2 * g, HD)] for g in range(shared_heads)])
    grad_values = side_by_side([total[:, block(2 * g + 1, HD)] for g in range(shared_heads)])
    return (side_by_side(attention), side_by_side(grad_queries), grad_keys, grad_values)


def solution(mesh):
    rows = P(("dp", "ulysses"), None)
    return jax.shard_map(
        functools.partial(per_device, mesh.shape["ulysses"]),
        mesh=mesh,
        in_specs=(rows, rows, rows, rows, P()),
        out_specs=(rows, rows, rows, rows),
        check_vma=False,
    )
```

```python
import functools
import math

import jax
import jax.numpy as jnp
from jax import lax
from jax.experimental import pallas as pl
from jax.experimental.pallas import tpu as pltpu
from jax.sharding import PartitionSpec as P

HD = 128
PAIR = 2
masked_score = -1e30
IN_ORDER = (0, 2, 1, 4, 3)
OUT_ORDER = (0, 4, 3, 2, 1)
score_scale = 1.0 / math.sqrt(HD)
exponent_scale = score_scale * math.log2(math.e)

NN = (((1,), (0,)), ((), ()))
NT = (((1,), (1,)), ((), ()))


def dot(a, b, dims=NN):
    return lax.dot_general(a, b, dims, preferred_element_type=jnp.float32)


def block(index, size):
    return slice(index * size, (index + 1) * size)


def fetch_kernel(doc_hbm, key_hbm, value_hbm, kv_ref, first_key_ref, doc_ref, sems):
    pairs = [(doc_hbm, doc_ref)]
    for shared in range(key_hbm.shape[1] // HD):
        for part, ref in enumerate((key_hbm, value_hbm)):
            pairs.append(
                (ref.at[:, pl.ds(shared * HD, HD)], kv_ref.at[:, pl.ds((2 * shared + part) * HD, HD)])
            )
    copies = [pltpu.make_async_copy(src, dst, sems.at[i]) for i, (src, dst) in enumerate(pairs)]
    for copy in copies:
        copy.start()
    tokens = key_hbm.shape[0]
    row = lax.axis_index("dp")
    place = lax.axis_index("ulysses")
    query_pos = place * tokens + lax.broadcasted_iota(jnp.int32, (1, tokens), 1)
    first_key = jnp.zeros((1, tokens), jnp.int32)
    copies[0].wait()
    doc_end = jnp.int32(0)
    for doc in range(doc_ref.shape[1]):
        doc_end = doc_end + doc_ref[row, doc]
        first_key = jnp.where(doc_end <= query_pos, doc_end, first_key)
    first_key_ref[...] = first_key
    for copy in copies[1:]:
        copy.wait()


def prepare_kernel(reach, first_key_ref, query_ref, grad_ref, *refs):
    query_rows_ref, grad_rows_ref, query_t_ref, grad_t_ref, bias_ref = refs
    tokens = query_ref.shape[0]
    place = lax.axis_index("ulysses")
    inner = lax.broadcasted_iota(jnp.int32, (tokens, tokens), 0)
    lanes = lax.broadcasted_iota(jnp.int32, (tokens, tokens), 1)
    first_key = first_key_ref[...] - place * tokens
    for back in range(reach + 1):
        key_pos = inner - back * tokens
        allowed = (key_pos >= first_key) & (key_pos <= lanes)
        bias_ref[block(back, tokens), :] = jnp.where(allowed, 0.0, masked_score).astype(
            jnp.bfloat16
        )
    identity = jnp.where(inner == lanes, 1.0, 0.0).astype(jnp.bfloat16)
    for head in range(query_ref.shape[1] // HD):
        own = block(head, tokens)
        queries = query_ref[:, block(head, HD)]
        grads = grad_ref[:, block(head, HD)]
        query_rows_ref[own, :] = queries
        grad_rows_ref[own, :] = grads
        query_t_ref[:HD, own] = queries.T
        query_t_ref[HD:, own] = identity
        grad_t_ref[:, own] = grads.T


def gradient_terms(weights, scores_grad, queries, grads):
    key_terms = dot(scores_grad, queries) * score_scale
    value_terms = dot(weights, grads)
    return jnp.concatenate([key_terms, value_terms], axis=1)


def parts(columns, tokens):
    width = min(columns, PAIR * tokens)
    return [slice(start, start + width) for start in range(0, columns, width)]


def joined(early, kv_refs):
    *kv_blocks, more = [ref[...] for ref in kv_refs]
    kv_blocks[early.index(1)] += more
    return [kv_blocks[early.index(back)] for back in sorted(early)]


def biased_keys(kv_blocks, bias_ref, places):
    tokens = kv_blocks[0].shape[0]
    keys = jnp.concatenate([rows[:, :HD] for rows in kv_blocks], axis=0)
    bias = jnp.concatenate([bias_ref[block(back, tokens), :] for back in places], axis=0)
    return jnp.concatenate([keys, bias], axis=1)


def early_kernel(early, query_t_ref, grad_t_ref, bias_ref, *refs):
    *kv_refs, weights_ref, grad_weights_ref, stats_ref, out_t_ref, scores_ref = refs
    kv_blocks = joined(early, kv_refs)
    tokens = kv_blocks[0].shape[0]
    columns = parts(query_t_ref.shape[1], tokens)
    keys = biased_keys(kv_blocks, bias_ref, sorted(early))
    values = jnp.concatenate([rows[:, HD:] for rows in kv_blocks], axis=0)
    values_t = values.T
    for part in columns:
        scores_ref[:, part] = dot(keys, query_t_ref[:, part])
    for part in columns:
        grad_weights_ref[:, part] = dot(values, grad_t_ref[:, part])
        top = jnp.max(scores_ref[:, part], axis=0, keepdims=True) * exponent_scale
        weights = jnp.exp2(scores_ref[:, part] * exponent_scale - top)
        stats_ref[0:1, part] = top
        stats_ref[1:2, part] = jnp.sum(weights, axis=0, keepdims=True)
        stats_ref[2:3, part] = jnp.sum(weights * grad_weights_ref[:, part], axis=0, keepdims=True)
        weights_ref[:, part] = weights.astype(jnp.bfloat16)
    for part in columns:
        out_t_ref[:, part] = dot(values_t, weights_ref[:, part])


def late_kernel(early, late, query_ref, grad_ref, query_t_ref, grad_t_ref, bias_ref, *refs):
    late_kv_ref, early_weights_ref, grad_weights_ref, stats_ref = refs[:4]
    weights_ref, scores_grad_ref, rescale_ref, late_term_ref, *term_refs = refs[4:]
    tokens = late_kv_ref.shape[0]
    columns = parts(query_t_ref.shape[1], tokens)
    late_rows = block(len(early), tokens)
    place = lax.axis_index("ulysses")

    def with_blocks(count):
        early_rows = slice(0, count * tokens)
        far_rows = slice(tokens, count * tokens)
        keys = biased_keys([late_kv_ref[...]], bias_ref, [late])
        values = late_kv_ref[:, HD:]
        scores = [dot(keys, query_t_ref[:, part]) for part in columns]
        grad_weights = [dot(values, grad_t_ref[:, part]) for part in columns]
        key_terms = value_terms = jnp.zeros((count * tokens, HD), jnp.float32)
        for part, own, own_grad in zip(columns, scores, grad_weights):
            early_top = stats_ref[0:1, part]
            top = jnp.maximum(early_top, jnp.max(own, axis=0, keepdims=True) * exponent_scale)
            rescale = jnp.exp2(early_top - top)
            own = jnp.exp2(own * exponent_scale - top)
            total = rescale * stats_ref[1:2, part] + jnp.sum(own, axis=0, keepdims=True)
            inverse = 1.0 / total
            own = own * inverse
            rescale = rescale * inverse
            row_dots = rescale * stats_ref[2:3, part]
            row_dots += jnp.sum(own * own_grad, axis=0, keepdims=True)
            rescale_ref[:, part] = rescale
            weights_ref[late_rows, part] = own.astype(jnp.bfloat16)
            scores_grad_ref[late_rows, part] = (own * (own_grad - row_dots)).astype(jnp.bfloat16)
            own = early_weights_ref[early_rows, part].astype(jnp.float32) * rescale
            weights_ref[early_rows, part] = own.astype(jnp.bfloat16)
            scores_grad_ref[early_rows, part] = (
                own * (grad_weights_ref[early_rows, part] - row_dots)
            ).astype(jnp.bfloat16)
            low_grad = [scores_grad_ref[rows, part] for rows in (late_rows, far_rows)]
            low = [weights_ref[rows, part] for rows in (late_rows, far_rows)]
            key_terms += dot(jnp.concatenate(low_grad, axis=0), query_ref[part, :])
            value_terms += dot(jnp.concatenate(low, axis=0), grad_ref[part, :])
        missing = len(early) - count
        if missing:
            scores_grad_ref[count * tokens : len(early) * tokens, :] = jnp.zeros(
                (missing * tokens, scores_grad_ref.shape[1]), jnp.bfloat16
            )
        terms = jnp.concatenate([key_terms * score_scale, value_terms], axis=1)
        terms = terms.astype(jnp.bfloat16)
        for index, ref in enumerate([late_term_ref, *term_refs]):
            if index < count:
                ref[...] = terms[block(index, tokens)]
            else:
                ref[...] = jnp.zeros_like(ref)

    exist = [sum(back <= reach for back in early) for reach in (late, max(early) - 1, max(early))]
    pl.when(place <= late)(lambda: with_blocks(exist[0]))
    pl.when((place > late) & (place < max(early)))(lambda: with_blocks(exist[1]))
    pl.when(place >= max(early))(lambda: with_blocks(exist[2]))


def near_kernel(early, query_ref, grad_ref, weights_ref, scores_grad_ref, rescale_ref, *refs):
    early_out_t_ref, late_kv_ref, *kv_refs, out_ref, query_grad_ref, near_ref = refs
    tokens = late_kv_ref.shape[0]
    late_out_t = dot(late_kv_ref[:, HD:].T, weights_ref[-tokens:, :])
    out_t = (early_out_t_ref[...] * rescale_ref[...] + late_out_t).astype(jnp.bfloat16)
    near_ref[...] = gradient_terms(
        weights_ref[:tokens, :], scores_grad_ref[:tokens, :], query_ref[...], grad_ref[...]
    )
    kv_blocks = joined(early, kv_refs) + [late_kv_ref[...]]
    keys_t = jnp.concatenate([rows[:, :HD] for rows in kv_blocks], axis=0).T
    query_grad_t = (dot(keys_t, scores_grad_ref[...]) * score_scale).astype(jnp.bfloat16)
    for head in range(out_ref.shape[1] // HD):
        own = block(head, tokens)
        query_grad_ref[:, block(head, HD)] = query_grad_t[:, own].T
        out_ref[:, block(head, HD)] = out_t[:, own].T


def call(body, name, outs, scratch, flops, *operands, fetched=False):
    vmem = pl.BlockSpec(memory_space=pltpu.VMEM)
    if fetched:
        operands = [pltpu.with_memory_space_constraint(a, pltpu.HBM) for a in operands]
    held = sum(math.prod(a.shape) * a.dtype.itemsize for a in operands)
    held += sum(math.prod(shape) * dtype.dtype.itemsize for shape, dtype in outs)
    held += sum(math.prod(s.shape) * 4 for s in scratch if hasattr(s, "shape"))
    return pl.pallas_call(
        body,
        out_shape=[jax.ShapeDtypeStruct(shape, dtype) for shape, dtype in outs],
        in_specs=[pl.BlockSpec(memory_space=pltpu.HBM) if fetched else vmem] * len(operands),
        out_specs=[vmem] * len(outs),
        scratch_shapes=scratch,
        compiler_params=pltpu.CompilerParams(
            vmem_limit_bytes=held + 12 * 1024 * 1024
        ),
        cost_estimate=pl.CostEstimate(flops=flops, bytes_accessed=held, transcendentals=0),
        name=name,
    )(*operands)


def ordered(values, order):
    first = [values[place] for place in order if place < len(values)]
    return first + [v for place, v in enumerate(values) if place not in order]


def per_device(devices, query_rows, key_rows, value_rows, grad_out, doc_lengths):
    tokens, query_width = query_rows.shape
    shared_heads = key_rows.shape[1] // HD
    length = tokens * devices
    reach = min(devices - 1, (length // 2 - 1 + tokens - 1) // tokens)
    blocks = reach + 1
    window = blocks * tokens
    low = jnp.bfloat16

    group_width = query_width // shared_heads
    columns = group_width // HD * tokens
    product = 2 * window * columns * HD
    kv, first_key = call(
        fetch_kernel,
        "fetch",
        [
            ((tokens, 2 * shared_heads * HD), low),
            ((1, tokens), jnp.int32),
        ],
        [
            pltpu.SMEM(doc_lengths.shape, jnp.int32),
            pltpu.SemaphoreType.DMA((2 * shared_heads + 1,)),
        ],
        16 * product,
        doc_lengths,
        key_rows,
        value_rows,
        fetched=True,
    )
    def forward(back, first, last):
        return lax.ppermute(kv, "ulysses", [(d - back, d) for d in range(max(first, back), last)])

    previous = [forward(1, reach + 1, devices), forward(1, 0, reach + 1)]
    kv_blocks = {0: kv}
    for back in ordered(list(range(blocks)), IN_ORDER)[1:]:
        kv_blocks[back] = previous[0] if back == 1 else forward(back, 0, devices)
    late = list(kv_blocks)[1]
    early = [0] + [back for back in kv_blocks if back not in (0, late)]
    places = early + [late]
    window_early = len(early) * tokens

    attention, grad_queries, totals, far = [], [], [], []
    for shared in range(shared_heads):
        own_queries = query_rows[:, block(shared, group_width)]
        own_grads = grad_out[:, block(shared, group_width)]
        if attention:
            own_queries, attention[-1] = lax.optimization_barrier((own_queries, attention[-1]))
        own_kv = [
            rows[:, block(shared, 2 * HD)]
            for rows in [kv_blocks[back] for back in places] + previous[1:]
        ]
        early_kv = own_kv[:-2] + own_kv[-1:]
        queries, grads, queries_t, grads_t, bias = call(
            functools.partial(prepare_kernel, reach),
            "prepare",
            [
                ((columns, HD), low),
                ((columns, HD), low),
                ((HD + tokens, columns), low),
                ((HD, columns), low),
                ((window, tokens), low),
            ],
            [],
            product // 4,
            first_key,
            own_queries,
            own_grads,
        )
        weights, grad_weights, stats, early_out_t = call(
            functools.partial(early_kernel, early),
            "early",
            [
                ((window_early, columns), low),
                ((window_early, columns), jnp.float32),
                ((3, columns), jnp.float32),
                ((HD, columns), jnp.float32),
            ],
            [pltpu.VMEM((window_early, columns), jnp.float32)],
            3 * product,
            queries_t,
            grads_t,
            bias,
            *early_kv,
        )
        weights, scores_grad, rescale, *own_far = call(
            functools.partial(late_kernel, early, late),
            "late",
            [((window, columns), low), ((window, columns), low), ((1, columns), jnp.float32)]
            + [((tokens, 2 * HD), low)] * reach,
            [],
            2 * product,
            queries,
            grads,
            queries_t,
            grads_t,
            bias,
            own_kv[-2],
            weights,
            grad_weights,
            stats,
        )
        own_out, own_query_grad, own_total = call(
            functools.partial(near_kernel, early),
            "near",
            [((tokens, group_width), low)] * 2 + [((tokens, 2 * HD), jnp.float32)],
            [],
            2 * product,
            queries,
            grads,
            weights,
            scores_grad,
            rescale,
            early_out_t,
            own_kv[-2],
            *early_kv,
        )
        attention.append(own_out)
        grad_queries.append(own_query_grad)
        totals.append(own_total)
        far.append(own_far)

    def side_by_side(parts):
        return parts[0] if len(parts) == 1 else jnp.concatenate(parts, axis=1)

    far_places = [late] + sorted(early)[1:]
    total = side_by_side(totals)
    for back in ordered(list(range(blocks)), OUT_ORDER)[1:]:
        terms = side_by_side([own[far_places.index(back)] for own in far])
        terms = lax.ppermute(terms, "ulysses", [(d, d - back) for d in range(back, devices)])
        total = total + terms.astype(jnp.float32)
    total = total.astype(low)
    grad_keys = side_by_side([total[:, block(2 * g, HD)] for g in range(shared_heads)])
    grad_values = side_by_side([total[:, block(2 * g + 1, HD)] for g in range(shared_heads)])
    return (side_by_side(attention), side_by_side(grad_queries), grad_keys, grad_values)


def solution(mesh):
    rows = P(("dp", "ulysses"), None)
    return jax.shard_map(
        functools.partial(per_device, mesh.shape["ulysses"]),
        mesh=mesh,
        in_specs=(rows, rows, rows, rows, P()),
        out_specs=(rows, rows, rows, rows),
        check_vma=False,
    )
```

```python
import functools
import math

import jax
import jax.numpy as jnp
from jax import lax
from jax.experimental import pallas as pl
from jax.experimental.pallas import tpu as pltpu
from jax.sharding import PartitionSpec as P

HD = 128
PAIR = 2
masked_score = -1e30
IN_ORDER = (0, 2, 1, 4, 3)
OUT_ORDER = (0, 4, 3, 2, 1)
score_scale = 1.0 / math.sqrt(HD)
exponent_scale = score_scale * math.log2(math.e)

NN = (((1,), (0,)), ((), ()))
NT = (((1,), (1,)), ((), ()))


def dot(a, b, dims=NN):
    return lax.dot_general(a, b, dims, preferred_element_type=jnp.float32)


def block(index, size):
    return slice(index * size, (index + 1) * size)


def fetch_kernel(doc_hbm, key_hbm, value_hbm, kv_ref, first_key_ref, doc_ref, sems):
    pairs = [(doc_hbm, doc_ref)]
    for shared in range(key_hbm.shape[1] // HD):
        for part, ref in enumerate((key_hbm, value_hbm)):
            pairs.append(
                (ref.at[:, pl.ds(shared * HD, HD)], kv_ref.at[:, pl.ds((2 * shared + part) * HD, HD)])
            )
    copies = [pltpu.make_async_copy(src, dst, sems.at[i]) for i, (src, dst) in enumerate(pairs)]
    for copy in copies:
        copy.start()
    tokens = key_hbm.shape[0]
    row = lax.axis_index("dp")
    place = lax.axis_index("ulysses")
    query_pos = place * tokens + lax.broadcasted_iota(jnp.int32, (1, tokens), 1)
    first_key = jnp.zeros((1, tokens), jnp.int32)
    copies[0].wait()
    doc_end = jnp.int32(0)
    for doc in range(doc_ref.shape[1]):
        doc_end = doc_end + doc_ref[row, doc]
        first_key = jnp.where(doc_end <= query_pos, doc_end, first_key)
    first_key_ref[...] = first_key
    for copy in copies[1:]:
        copy.wait()


def prepare_kernel(reach, first_key_ref, query_ref, grad_ref, *refs):
    query_rows_ref, grad_rows_ref, query_t_ref, grad_t_ref, bias_ref = refs
    tokens = query_ref.shape[0]
    place = lax.axis_index("ulysses")
    inner = lax.broadcasted_iota(jnp.int32, (tokens, tokens), 0)
    lanes = lax.broadcasted_iota(jnp.int32, (tokens, tokens), 1)
    first_key = first_key_ref[...] - place * tokens
    for back in range(reach + 1):
        key_pos = inner - back * tokens
        allowed = (key_pos >= first_key) & (key_pos <= lanes)
        bias_ref[block(back, tokens), :] = jnp.where(allowed, 0.0, masked_score).astype(
            jnp.bfloat16
        )
    identity = jnp.where(inner == lanes, 1.0, 0.0).astype(jnp.bfloat16)
    for head in range(query_ref.shape[1] // HD):
        own = block(head, tokens)
        queries = query_ref[:, block(head, HD)]
        grads = grad_ref[:, block(head, HD)]
        query_rows_ref[own, :] = queries
        grad_rows_ref[own, :] = grads
        query_t_ref[:HD, own] = queries.T
        query_t_ref[HD:, own] = identity
        grad_t_ref[:, own] = grads.T


def gradient_terms(weights, scores_grad, queries, grads):
    key_terms = dot(scores_grad, queries) * score_scale
    value_terms = dot(weights, grads)
    return jnp.concatenate([key_terms, value_terms], axis=1)


def parts(columns, tokens):
    width = min(columns, PAIR * tokens)
    return [slice(start, start + width) for start in range(0, columns, width)]


def joined(early, kv_refs):
    *kv_blocks, more = [ref[...] for ref in kv_refs]
    kv_blocks[early.index(1)] += more
    return [kv_blocks[early.index(back)] for back in sorted(early)]


def biased_keys(kv_blocks, bias_ref, places):
    tokens = kv_blocks[0].shape[0]
    keys = jnp.concatenate([rows[:, :HD] for rows in kv_blocks], axis=0)
    bias = jnp.concatenate([bias_ref[block(back, tokens), :] for back in places], axis=0)
    return jnp.concatenate([keys, bias], axis=1)


def early_kernel(early, query_t_ref, grad_t_ref, bias_ref, *refs):
    *kv_refs, weights_ref, grad_weights_ref, stats_ref, out_t_ref, scores_ref = refs
    kv_blocks = joined(early, kv_refs)
    tokens = kv_blocks[0].shape[0]
    columns = parts(query_t_ref.shape[1], tokens)
    keys = biased_keys(kv_blocks, bias_ref, sorted(early))
    values = jnp.concatenate([rows[:, HD:] for rows in kv_blocks], axis=0)
    values_t = values.T
    for part in columns:
        scores_ref[:, part] = dot(keys, query_t_ref[:, part])
    for part in columns:
        grad_weights_ref[:, part] = dot(values, grad_t_ref[:, part])
        top = jnp.max(scores_ref[:, part], axis=0, keepdims=True) * exponent_scale
        weights = jnp.exp2(scores_ref[:, part] * exponent_scale - top)
        stats_ref[0:1, part] = top
        stats_ref[1:2, part] = jnp.sum(weights, axis=0, keepdims=True)
        stats_ref[2:3, part] = jnp.sum(weights * grad_weights_ref[:, part], axis=0, keepdims=True)
        weights_ref[:, part] = weights.astype(jnp.bfloat16)
    for part in columns:
        out_t_ref[:, part] = dot(values_t, weights_ref[:, part])


def late_kernel(early, late, query_ref, grad_ref, query_t_ref, grad_t_ref, bias_ref, *refs):
    late_kv_ref, early_weights_ref, grad_weights_ref, stats_ref = refs[:4]
    weights_ref, scores_grad_ref, rescale_ref, late_term_ref, *term_refs, again_ref = refs[4:]
    tokens = late_kv_ref.shape[0]
    columns = parts(query_t_ref.shape[1], tokens)
    late_rows = block(len(early), tokens)
    place = lax.axis_index("ulysses")

    def with_blocks(count):
        early_rows = slice(0, count * tokens)
        far_rows = slice(tokens, count * tokens)
        keys = biased_keys([late_kv_ref[...]], bias_ref, [late])
        values = late_kv_ref[:, HD:]
        scores = [dot(keys, query_t_ref[:, part]) for part in columns]
        grad_weights = [dot(values, grad_t_ref[:, part]) for part in columns]
        key_terms = value_terms = jnp.zeros((count * tokens, HD), jnp.float32)
        for part, own, own_grad in zip(columns, scores, grad_weights):
            early_top = stats_ref[0:1, part]
            top = jnp.maximum(early_top, jnp.max(own, axis=0, keepdims=True) * exponent_scale)
            rescale = jnp.exp2(early_top - top)
            own = jnp.exp2(own * exponent_scale - top)
            total = rescale * stats_ref[1:2, part] + jnp.sum(own, axis=0, keepdims=True)
            inverse = 1.0 / total
            own = own * inverse
            rescale = rescale * inverse
            row_dots = rescale * stats_ref[2:3, part]
            row_dots += jnp.sum(own * own_grad, axis=0, keepdims=True)
            rescale_ref[:, part] = rescale
            weights_ref[late_rows, part] = own.astype(jnp.bfloat16)
            scores_grad_ref[late_rows, part] = (own * (own_grad - row_dots)).astype(jnp.bfloat16)
            own = early_weights_ref[early_rows, part].astype(jnp.float32) * rescale
            weights_ref[early_rows, part] = own.astype(jnp.bfloat16)
            scores_grad_ref[early_rows, part] = (
                own * (grad_weights_ref[early_rows, part] - row_dots)
            ).astype(jnp.bfloat16)
            low_grad = [scores_grad_ref[rows, part] for rows in (late_rows, far_rows)]
            low = [weights_ref[rows, part] for rows in (late_rows, far_rows)]
            key_terms += dot(jnp.concatenate(low_grad, axis=0), query_ref[part, :])
            value_terms += dot(jnp.concatenate(low, axis=0), grad_ref[part, :])
        missing = len(early) - count
        if missing:
            scores_grad_ref[count * tokens : len(early) * tokens, :] = jnp.zeros(
                (missing * tokens, scores_grad_ref.shape[1]), jnp.bfloat16
            )
        terms = jnp.concatenate([key_terms * score_scale, value_terms], axis=1)
        terms = terms.astype(jnp.bfloat16)
        for index, ref in enumerate([late_term_ref, *term_refs]):
            if index < count:
                ref[...] = terms[block(index, tokens)]
            else:
                ref[...] = jnp.zeros_like(ref)
        again_ref[...] = terms[block(1, tokens)]

    exist = [sum(back <= reach for back in early) for reach in (late, max(early) - 1, max(early))]
    pl.when(place <= late)(lambda: with_blocks(exist[0]))
    pl.when((place > late) & (place < max(early)))(lambda: with_blocks(exist[1]))
    pl.when(place >= max(early))(lambda: with_blocks(exist[2]))


def near_kernel(early, query_ref, grad_ref, weights_ref, scores_grad_ref, rescale_ref, *refs):
    early_out_t_ref, late_kv_ref, *kv_refs, out_ref, query_grad_ref, near_ref = refs
    tokens = late_kv_ref.shape[0]
    late_out_t = dot(late_kv_ref[:, HD:].T, weights_ref[-tokens:, :])
    out_t = (early_out_t_ref[...] * rescale_ref[...] + late_out_t).astype(jnp.bfloat16)
    near_ref[...] = gradient_terms(
        weights_ref[:tokens, :], scores_grad_ref[:tokens, :], query_ref[...], grad_ref[...]
    )
    kv_blocks = joined(early, kv_refs) + [late_kv_ref[...]]
    keys_t = jnp.concatenate([rows[:, :HD] for rows in kv_blocks], axis=0).T
    query_grad_t = (dot(keys_t, scores_grad_ref[...]) * score_scale).astype(jnp.bfloat16)
    for head in range(out_ref.shape[1] // HD):
        own = block(head, tokens)
        query_grad_ref[:, block(head, HD)] = query_grad_t[:, own].T
        out_ref[:, block(head, HD)] = out_t[:, own].T


def call(body, name, outs, scratch, flops, *operands, fetched=False):
    vmem = pl.BlockSpec(memory_space=pltpu.VMEM)
    if fetched:
        operands = [pltpu.with_memory_space_constraint(a, pltpu.HBM) for a in operands]
    held = sum(math.prod(a.shape) * a.dtype.itemsize for a in operands)
    held += sum(math.prod(shape) * dtype.dtype.itemsize for shape, dtype in outs)
    held += sum(math.prod(s.shape) * 4 for s in scratch if hasattr(s, "shape"))
    return pl.pallas_call(
        body,
        out_shape=[jax.ShapeDtypeStruct(shape, dtype) for shape, dtype in outs],
        in_specs=[pl.BlockSpec(memory_space=pltpu.HBM) if fetched else vmem] * len(operands),
        out_specs=[vmem] * len(outs),
        scratch_shapes=scratch,
        compiler_params=pltpu.CompilerParams(
            vmem_limit_bytes=held + 12 * 1024 * 1024
        ),
        cost_estimate=pl.CostEstimate(flops=flops, bytes_accessed=held, transcendentals=0),
        name=name,
    )(*operands)


def ordered(values, order):
    first = [values[place] for place in order if place < len(values)]
    return first + [v for place, v in enumerate(values) if place not in order]


def per_device(devices, query_rows, key_rows, value_rows, grad_out, doc_lengths):
    tokens, query_width = query_rows.shape
    shared_heads = key_rows.shape[1] // HD
    length = tokens * devices
    reach = min(devices - 1, (length // 2 - 1 + tokens - 1) // tokens)
    blocks = reach + 1
    window = blocks * tokens
    low = jnp.bfloat16

    group_width = query_width // shared_heads
    columns = group_width // HD * tokens
    product = 2 * window * columns * HD
    kv, first_key = call(
        fetch_kernel,
        "fetch",
        [
            ((tokens, 2 * shared_heads * HD), low),
            ((1, tokens), jnp.int32),
        ],
        [
            pltpu.SMEM(doc_lengths.shape, jnp.int32),
            pltpu.SemaphoreType.DMA((2 * shared_heads + 1,)),
        ],
        16 * product,
        doc_lengths,
        key_rows,
        value_rows,
        fetched=True,
    )
    def forward(back, first, last):
        return lax.ppermute(kv, "ulysses", [(d - back, d) for d in range(max(first, back), last)])

    previous = [forward(1, reach + 1, devices), forward(1, 0, reach + 1)]
    kv_blocks = {0: kv}
    for back in ordered(list(range(blocks)), IN_ORDER)[1:]:
        kv_blocks[back] = previous[0] if back == 1 else forward(back, 0, devices)
    late = list(kv_blocks)[1]
    early = [0] + [back for back in kv_blocks if back not in (0, late)]
    places = early + [late]
    window_early = len(early) * tokens

    attention, grad_queries, totals, far = [], [], [], []
    for shared in range(shared_heads):
        own_queries = query_rows[:, block(shared, group_width)]
        own_grads = grad_out[:, block(shared, group_width)]
        if attention:
            own_queries, attention[-1] = lax.optimization_barrier((own_queries, attention[-1]))
        own_kv = [
            rows[:, block(shared, 2 * HD)]
            for rows in [kv_blocks[back] for back in places] + previous[1:]
        ]
        early_kv = own_kv[:-2] + own_kv[-1:]
        queries, grads, queries_t, grads_t, bias = call(
            functools.partial(prepare_kernel, reach),
            "prepare",
            [
                ((columns, HD), low),
                ((columns, HD), low),
                ((HD + tokens, columns), low),
                ((HD, columns), low),
                ((window, tokens), low),
            ],
            [],
            product // 4,
            first_key,
            own_queries,
            own_grads,
        )
        weights, grad_weights, stats, early_out_t = call(
            functools.partial(early_kernel, early),
            "early",
            [
                ((window_early, columns), low),
                ((window_early, columns), jnp.float32),
                ((3, columns), jnp.float32),
                ((HD, columns), jnp.float32),
            ],
            [pltpu.VMEM((window_early, columns), jnp.float32)],
            3 * product,
            queries_t,
            grads_t,
            bias,
            *early_kv,
        )
        weights, scores_grad, rescale, *own_far = call(
            functools.partial(late_kernel, early, late),
            "late",
            [((window, columns), low), ((window, columns), low), ((1, columns), jnp.float32)]
            + [((tokens, 2 * HD), low)] * (reach + 1),
            [],
            2 * product,
            queries,
            grads,
            queries_t,
            grads_t,
            bias,
            own_kv[-2],
            weights,
            grad_weights,
            stats,
        )
        own_out, own_query_grad, own_total = call(
            functools.partial(near_kernel, early),
            "near",
            [((tokens, group_width), low)] * 2 + [((tokens, 2 * HD), jnp.float32)],
            [],
            2 * product,
            queries,
            grads,
            weights,
            scores_grad,
            rescale,
            early_out_t,
            own_kv[-2],
            *early_kv,
        )
        attention.append(own_out)
        grad_queries.append(own_query_grad)
        totals.append(own_total)
        far.append(own_far)

    def side_by_side(parts):
        return parts[0] if len(parts) == 1 else jnp.concatenate(parts, axis=1)

    far_places = [late] + sorted(early)[1:]
    total = side_by_side(totals)
    returns = [(back, 0, devices) for back in ordered(list(range(blocks)), OUT_ORDER)[1:]]
    returns[-2:] = [(1, reach + 1, devices), returns[-2], (1, 0, reach + 1)]
    for back, first, last in returns:
        index = reach if last == reach + 1 else far_places.index(back)
        terms = side_by_side([own[index] for own in far])
        terms = lax.ppermute(
            terms, "ulysses", [(d + back, d) for d in range(first, min(last, devices - back))]
        )
        total = total + terms.astype(jnp.float32)
    total = total.astype(low)
    grad_keys = side_by_side([total[:, block(2 * g, HD)] for g in range(shared_heads)])
    grad_values = side_by_side([total[:, block(2 * g + 1, HD)] for g in range(shared_heads)])
    return (side_by_side(attention), side_by_side(grad_queries), grad_keys, grad_values)


def solution(mesh):
    rows = P(("dp", "ulysses"), None)
    return jax.shard_map(
        functools.partial(per_device, mesh.shape["ulysses"]),
        mesh=mesh,
        in_specs=(rows, rows, rows, rows, P()),
        out_specs=(rows, rows, rows, rows),
        check_vma=False,
    )
```

```python
import functools
import math

import jax
import jax.numpy as jnp
from jax import lax
from jax.experimental import pallas as pl
from jax.experimental.pallas import tpu as pltpu
from jax.sharding import PartitionSpec as P

HD = 128
PAIR = 2
masked_score = -1e30
IN_ORDER = (0, 2, 1, 4, 3)
OUT_ORDER = (0, 4, 3, 2, 1)
score_scale = 1.0 / math.sqrt(HD)
exponent_scale = score_scale * math.log2(math.e)

NN = (((1,), (0,)), ((), ()))
NT = (((1,), (1,)), ((), ()))


def dot(a, b, dims=NN):
    return lax.dot_general(a, b, dims, preferred_element_type=jnp.float32)


def block(index, size):
    return slice(index * size, (index + 1) * size)


def fetch_kernel(doc_hbm, key_hbm, value_hbm, kv_ref, first_key_ref, doc_ref, sems):
    pairs = [(doc_hbm, doc_ref)]
    for shared in range(key_hbm.shape[1] // HD):
        for part, ref in enumerate((key_hbm, value_hbm)):
            pairs.append(
                (ref.at[:, pl.ds(shared * HD, HD)], kv_ref.at[:, pl.ds((2 * shared + part) * HD, HD)])
            )
    copies = [pltpu.make_async_copy(src, dst, sems.at[i]) for i, (src, dst) in enumerate(pairs)]
    for copy in copies:
        copy.start()
    tokens = key_hbm.shape[0]
    row = lax.axis_index("dp")
    place = lax.axis_index("ulysses")
    query_pos = place * tokens + lax.broadcasted_iota(jnp.int32, (1, tokens), 1)
    first_key = jnp.zeros((1, tokens), jnp.int32)
    copies[0].wait()
    doc_end = jnp.int32(0)
    for doc in range(doc_ref.shape[1]):
        doc_end = doc_end + doc_ref[row, doc]
        first_key = jnp.where(doc_end <= query_pos, doc_end, first_key)
    first_key_ref[...] = first_key
    for copy in copies[1:]:
        copy.wait()


def prepare_kernel(reach, first_key_ref, query_ref, grad_ref, *refs):
    query_rows_ref, grad_rows_ref, query_t_ref, grad_t_ref, bias_ref = refs
    tokens = query_ref.shape[0]
    place = lax.axis_index("ulysses")
    inner = lax.broadcasted_iota(jnp.int32, (tokens, tokens), 0)
    lanes = lax.broadcasted_iota(jnp.int32, (tokens, tokens), 1)
    first_key = first_key_ref[...] - place * tokens
    for back in range(reach + 1):
        key_pos = inner - back * tokens
        allowed = (key_pos >= first_key) & (key_pos <= lanes)
        bias_ref[block(back, tokens), :] = jnp.where(allowed, 0.0, masked_score).astype(
            jnp.bfloat16
        )
    identity = jnp.where(inner == lanes, 1.0, 0.0).astype(jnp.bfloat16)
    for head in range(query_ref.shape[1] // HD):
        own = block(head, tokens)
        queries = query_ref[:, block(head, HD)]
        grads = grad_ref[:, block(head, HD)]
        query_rows_ref[own, :] = queries
        grad_rows_ref[own, :] = grads
        query_t_ref[:HD, own] = queries.T
        query_t_ref[HD:, own] = identity
        grad_t_ref[:, own] = grads.T


def gradient_terms(weights, scores_grad, queries, grads):
    key_terms = dot(scores_grad, queries) * score_scale
    value_terms = dot(weights, grads)
    return jnp.concatenate([key_terms, value_terms], axis=1)


def parts(columns, tokens):
    width = min(columns, PAIR * tokens)
    return [slice(start, start + width) for start in range(0, columns, width)]


def joined(early, kv_refs):
    *kv_blocks, more = [ref[...] for ref in kv_refs]
    kv_blocks[early.index(1)] += more
    return [kv_blocks[early.index(back)] for back in sorted(early)]


def biased_keys(kv_blocks, bias_ref, places):
    tokens = kv_blocks[0].shape[0]
    keys = jnp.concatenate([rows[:, :HD] for rows in kv_blocks], axis=0)
    bias = jnp.concatenate([bias_ref[block(back, tokens), :] for back in places], axis=0)
    return jnp.concatenate([keys, bias], axis=1)


def early_kernel(early, late, query_t_ref, grad_t_ref, bias_ref, *refs):
    *kv_refs, weights_ref, grad_weights_ref, stats_ref, out_t_ref, scores_ref = refs
    tokens = kv_refs[0].shape[0]
    columns = parts(query_t_ref.shape[1], tokens)
    place = lax.axis_index("ulysses")

    def with_blocks(count):
        rows = slice(0, count * tokens)
        kv_blocks = joined(early, kv_refs)[:count]
        keys = biased_keys(kv_blocks, bias_ref, sorted(early)[:count])
        values = jnp.concatenate([own[:, HD:] for own in kv_blocks], axis=0)
        values_t = values.T
        for part in columns:
            scores_ref[rows, part] = dot(keys, query_t_ref[:, part])
        for part in columns:
            grad_weights = dot(values, grad_t_ref[:, part])
            grad_weights_ref[rows, part] = grad_weights
            top = jnp.max(scores_ref[rows, part], axis=0, keepdims=True) * exponent_scale
            weights = jnp.exp2(scores_ref[rows, part] * exponent_scale - top)
            stats_ref[0:1, part] = top
            stats_ref[1:2, part] = jnp.sum(weights, axis=0, keepdims=True)
            stats_ref[2:3, part] = jnp.sum(weights * grad_weights, axis=0, keepdims=True)
            weights_ref[rows, part] = weights.astype(jnp.bfloat16)
        for part in columns:
            out_t_ref[:, part] = dot(values_t, weights_ref[rows, part])

    pl.when(place <= late)(lambda: with_blocks(sum(back <= late for back in early)))
    pl.when(place > late)(lambda: with_blocks(len(early)))


def late_kernel(early, late, query_ref, grad_ref, query_t_ref, grad_t_ref, bias_ref, *refs):
    late_kv_ref, early_weights_ref, grad_weights_ref, stats_ref = refs[:4]
    weights_ref, scores_grad_ref, rescale_ref, late_term_ref, *term_refs, again_ref = refs[4:]
    tokens = late_kv_ref.shape[0]
    columns = parts(query_t_ref.shape[1], tokens)
    late_rows = block(len(early), tokens)
    place = lax.axis_index("ulysses")

    def with_blocks(count):
        early_rows = slice(0, count * tokens)
        far_rows = slice(tokens, count * tokens)
        keys = biased_keys([late_kv_ref[...]], bias_ref, [late])
        values = late_kv_ref[:, HD:]
        scores = [dot(keys, query_t_ref[:, part]) for part in columns]
        grad_weights = [dot(values, grad_t_ref[:, part]) for part in columns]
        key_terms = value_terms = jnp.zeros((count * tokens, HD), jnp.float32)
        for part, own, own_grad in zip(columns, scores, grad_weights):
            early_top = stats_ref[0:1, part]
            top = jnp.maximum(early_top, jnp.max(own, axis=0, keepdims=True) * exponent_scale)
            rescale = jnp.exp2(early_top - top)
            own = jnp.exp2(own * exponent_scale - top)
            total = rescale * stats_ref[1:2, part] + jnp.sum(own, axis=0, keepdims=True)
            inverse = 1.0 / total
            own = own * inverse
            rescale = rescale * inverse
            row_dots = rescale * stats_ref[2:3, part]
            row_dots += jnp.sum(own * own_grad, axis=0, keepdims=True)
            rescale_ref[:, part] = rescale
            weights_ref[late_rows, part] = own.astype(jnp.bfloat16)
            scores_grad_ref[late_rows, part] = (own * (own_grad - row_dots)).astype(jnp.bfloat16)
            own = early_weights_ref[early_rows, part].astype(jnp.float32) * rescale
            weights_ref[early_rows, part] = own.astype(jnp.bfloat16)
            scores_grad_ref[early_rows, part] = (
                own * (grad_weights_ref[early_rows, part] - row_dots)
            ).astype(jnp.bfloat16)
            low_grad = [scores_grad_ref[rows, part] for rows in (late_rows, far_rows)]
            low = [weights_ref[rows, part] for rows in (late_rows, far_rows)]
            key_terms += dot(jnp.concatenate(low_grad, axis=0), query_ref[part, :])
            value_terms += dot(jnp.concatenate(low, axis=0), grad_ref[part, :])
        missing = len(early) - count
        if missing:
            scores_grad_ref[count * tokens : len(early) * tokens, :] = jnp.zeros(
                (missing * tokens, scores_grad_ref.shape[1]), jnp.bfloat16
            )
        terms = jnp.concatenate([key_terms * score_scale, value_terms], axis=1)
        terms = terms.astype(jnp.bfloat16)
        for index, ref in enumerate([late_term_ref, *term_refs]):
            if index < count:
                ref[...] = terms[block(index, tokens)]
            else:
                ref[...] = jnp.zeros_like(ref)
        again_ref[...] = terms[block(1, tokens)]

    exist = [sum(back <= reach for back in early) for reach in (late, max(early) - 1, max(early))]
    pl.when(place <= late)(lambda: with_blocks(exist[0]))
    pl.when((place > late) & (place < max(early)))(lambda: with_blocks(exist[1]))
    pl.when(place >= max(early))(lambda: with_blocks(exist[2]))


def near_kernel(early, query_ref, grad_ref, weights_ref, scores_grad_ref, rescale_ref, *refs):
    early_out_t_ref, late_kv_ref, *kv_refs, out_ref, query_grad_ref, near_ref = refs
    tokens = late_kv_ref.shape[0]
    late_out_t = dot(late_kv_ref[:, HD:].T, weights_ref[-tokens:, :])
    out_t = (early_out_t_ref[...] * rescale_ref[...] + late_out_t).astype(jnp.bfloat16)
    near_ref[...] = gradient_terms(
        weights_ref[:tokens, :], scores_grad_ref[:tokens, :], query_ref[...], grad_ref[...]
    )
    kv_blocks = joined(early, kv_refs) + [late_kv_ref[...]]
    keys_t = jnp.concatenate([rows[:, :HD] for rows in kv_blocks], axis=0).T
    query_grad_t = (dot(keys_t, scores_grad_ref[...]) * score_scale).astype(jnp.bfloat16)
    for head in range(out_ref.shape[1] // HD):
        own = block(head, tokens)
        query_grad_ref[:, block(head, HD)] = query_grad_t[:, own].T
        out_ref[:, block(head, HD)] = out_t[:, own].T


def call(body, name, outs, scratch, flops, *operands, fetched=False):
    vmem = pl.BlockSpec(memory_space=pltpu.VMEM)
    if fetched:
        operands = [pltpu.with_memory_space_constraint(a, pltpu.HBM) for a in operands]
    held = sum(math.prod(a.shape) * a.dtype.itemsize for a in operands)
    held += sum(math.prod(shape) * dtype.dtype.itemsize for shape, dtype in outs)
    held += sum(math.prod(s.shape) * 4 for s in scratch if hasattr(s, "shape"))
    return pl.pallas_call(
        body,
        out_shape=[jax.ShapeDtypeStruct(shape, dtype) for shape, dtype in outs],
        in_specs=[pl.BlockSpec(memory_space=pltpu.HBM) if fetched else vmem] * len(operands),
        out_specs=[vmem] * len(outs),
        scratch_shapes=scratch,
        compiler_params=pltpu.CompilerParams(
            vmem_limit_bytes=held + 12 * 1024 * 1024
        ),
        cost_estimate=pl.CostEstimate(flops=flops, bytes_accessed=held, transcendentals=0),
        name=name,
    )(*operands)


def ordered(values, order):
    first = [values[place] for place in order if place < len(values)]
    return first + [v for place, v in enumerate(values) if place not in order]


def per_device(devices, query_rows, key_rows, value_rows, grad_out, doc_lengths):
    tokens, query_width = query_rows.shape
    shared_heads = key_rows.shape[1] // HD
    length = tokens * devices
    reach = min(devices - 1, (length // 2 - 1 + tokens - 1) // tokens)
    blocks = reach + 1
    window = blocks * tokens
    low = jnp.bfloat16

    group_width = query_width // shared_heads
    columns = group_width // HD * tokens
    product = 2 * window * columns * HD
    kv, first_key = call(
        fetch_kernel,
        "fetch",
        [
            ((tokens, 2 * shared_heads * HD), low),
            ((1, tokens), jnp.int32),
        ],
        [
            pltpu.SMEM(doc_lengths.shape, jnp.int32),
            pltpu.SemaphoreType.DMA((2 * shared_heads + 1,)),
        ],
        16 * product,
        doc_lengths,
        key_rows,
        value_rows,
        fetched=True,
    )
    def forward(back, first, last):
        return lax.ppermute(kv, "ulysses", [(d - back, d) for d in range(max(first, back), last)])

    previous = [forward(1, reach + 1, devices), forward(1, 0, reach + 1)]
    kv_blocks = {0: kv}
    for back in ordered(list(range(blocks)), IN_ORDER)[1:]:
        kv_blocks[back] = previous[0] if back == 1 else forward(back, 0, devices)
    late = list(kv_blocks)[1]
    early = [0] + [back for back in kv_blocks if back not in (0, late)]
    places = early + [late]
    window_early = len(early) * tokens

    attention, grad_queries, totals, far = [], [], [], []
    for shared in range(shared_heads):
        own_queries = query_rows[:, block(shared, group_width)]
        own_grads = grad_out[:, block(shared, group_width)]
        if attention:
            own_queries, attention[-1] = lax.optimization_barrier((own_queries, attention[-1]))
        own_kv = [
            rows[:, block(shared, 2 * HD)]
            for rows in [kv_blocks[back] for back in places] + previous[1:]
        ]
        early_kv = own_kv[:-2] + own_kv[-1:]
        queries, grads, queries_t, grads_t, bias = call(
            functools.partial(prepare_kernel, reach),
            "prepare",
            [
                ((columns, HD), low),
                ((columns, HD), low),
                ((HD + tokens, columns), low),
                ((HD, columns), low),
                ((window, tokens), low),
            ],
            [],
            product // 4,
            first_key,
            own_queries,
            own_grads,
        )
        weights, grad_weights, stats, early_out_t = call(
            functools.partial(early_kernel, early, late),
            "early",
            [
                ((window_early, columns), low),
                ((window_early, columns), jnp.float32),
                ((3, columns), jnp.float32),
                ((HD, columns), jnp.float32),
            ],
            [pltpu.VMEM((window_early, columns), jnp.float32)],
            3 * product,
            queries_t,
            grads_t,
            bias,
            *early_kv,
        )
        weights, scores_grad, rescale, *own_far = call(
            functools.partial(late_kernel, early, late),
            "late",
            [((window, columns), low), ((window, columns), low), ((1, columns), jnp.float32)]
            + [((tokens, 2 * HD), low)] * (reach + 1),
            [],
            2 * product,
            queries,
            grads,
            queries_t,
            grads_t,
            bias,
            own_kv[-2],
            weights,
            grad_weights,
            stats,
        )
        own_out, own_query_grad, own_total = call(
            functools.partial(near_kernel, early),
            "near",
            [((tokens, group_width), low)] * 2 + [((tokens, 2 * HD), jnp.float32)],
            [],
            2 * product,
            queries,
            grads,
            weights,
            scores_grad,
            rescale,
            early_out_t,
            own_kv[-2],
            *early_kv,
        )
        attention.append(own_out)
        grad_queries.append(own_query_grad)
        totals.append(own_total)
        far.append(own_far)

    def side_by_side(parts):
        return parts[0] if len(parts) == 1 else jnp.concatenate(parts, axis=1)

    far_places = [late] + sorted(early)[1:]
    total = side_by_side(totals)
    returns = [(back, 0, devices) for back in ordered(list(range(blocks)), OUT_ORDER)[1:]]
    returns[-2:] = [(1, reach + 1, devices), returns[-2], (1, 0, reach + 1)]
    for back, first, last in returns:
        index = reach if last == reach + 1 else far_places.index(back)
        terms = side_by_side([own[index] for own in far])
        terms = lax.ppermute(
            terms, "ulysses", [(d + back, d) for d in range(first, min(last, devices - back))]
        )
        total = total + terms.astype(jnp.float32)
    total = total.astype(low)
    grad_keys = side_by_side([total[:, block(2 * g, HD)] for g in range(shared_heads)])
    grad_values = side_by_side([total[:, block(2 * g + 1, HD)] for g in range(shared_heads)])
    return (side_by_side(attention), side_by_side(grad_queries), grad_keys, grad_values)


def solution(mesh):
    rows = P(("dp", "ulysses"), None)
    return jax.shard_map(
        functools.partial(per_device, mesh.shape["ulysses"]),
        mesh=mesh,
        in_specs=(rows, rows, rows, rows, P()),
        out_specs=(rows, rows, rows, rows),
        check_vma=False,
    )
```

```python
import functools
import math

import jax
import jax.numpy as jnp
from jax import lax
from jax.experimental import pallas as pl
from jax.experimental.pallas import tpu as pltpu
from jax.sharding import PartitionSpec as P

HD = 128
PAIR = 2
masked_score = -1e30
IN_ORDER = (0, 2, 1, 4, 3)
OUT_ORDER = (0, 4, 3, 2, 1)
score_scale = 1.0 / math.sqrt(HD)
exponent_scale = score_scale * math.log2(math.e)

NN = (((1,), (0,)), ((), ()))
NT = (((1,), (1,)), ((), ()))


def dot(a, b, dims=NN):
    return lax.dot_general(a, b, dims, preferred_element_type=jnp.float32)


def block(index, size):
    return slice(index * size, (index + 1) * size)


def fetch_kernel(doc_hbm, key_hbm, value_hbm, kv_ref, first_key_ref, doc_ref, sems):
    pairs = [(doc_hbm, doc_ref)]
    for shared in range(key_hbm.shape[1] // HD):
        for part, ref in enumerate((key_hbm, value_hbm)):
            pairs.append(
                (ref.at[:, pl.ds(shared * HD, HD)], kv_ref.at[:, pl.ds((2 * shared + part) * HD, HD)])
            )
    copies = [pltpu.make_async_copy(src, dst, sems.at[i]) for i, (src, dst) in enumerate(pairs)]
    for copy in copies:
        copy.start()
    tokens = key_hbm.shape[0]
    row = lax.axis_index("dp")
    place = lax.axis_index("ulysses")
    query_pos = place * tokens + lax.broadcasted_iota(jnp.int32, (1, tokens), 1)
    first_key = jnp.zeros((1, tokens), jnp.int32)
    copies[0].wait()
    doc_end = jnp.int32(0)
    for doc in range(doc_ref.shape[1]):
        doc_end = doc_end + doc_ref[row, doc]
        first_key = jnp.where(doc_end <= query_pos, doc_end, first_key)
    first_key_ref[...] = first_key
    for copy in copies[1:]:
        copy.wait()


def prepare_kernel(reach, first_key_ref, query_ref, grad_ref, *refs):
    query_rows_ref, grad_rows_ref, query_t_ref, grad_t_ref, bias_ref = refs
    tokens = query_ref.shape[0]
    place = lax.axis_index("ulysses")
    inner = lax.broadcasted_iota(jnp.int32, (tokens, tokens), 0)
    lanes = lax.broadcasted_iota(jnp.int32, (tokens, tokens), 1)
    first_key = first_key_ref[...] - place * tokens
    for back in range(reach + 1):
        key_pos = inner - back * tokens
        allowed = (key_pos >= first_key) & (key_pos <= lanes)
        bias_ref[block(back, tokens), :] = jnp.where(allowed, 0.0, masked_score).astype(
            jnp.bfloat16
        )
    identity = jnp.where(inner == lanes, 1.0, 0.0).astype(jnp.bfloat16)
    for head in range(query_ref.shape[1] // HD):
        own = block(head, tokens)
        queries = query_ref[:, block(head, HD)]
        grads = grad_ref[:, block(head, HD)]
        query_rows_ref[own, :] = queries
        grad_rows_ref[own, :] = grads
        query_t_ref[:HD, own] = queries.T
        query_t_ref[HD:, own] = identity
        grad_t_ref[:, own] = grads.T


def gradient_terms(weights, scores_grad, queries, grads):
    key_terms = dot(scores_grad, queries) * score_scale
    value_terms = dot(weights, grads)
    return jnp.concatenate([key_terms, value_terms], axis=1)


def parts(columns, tokens):
    width = min(columns, PAIR * tokens)
    return [slice(start, start + width) for start in range(0, columns, width)]


def joined(early, kv_refs):
    *kv_blocks, more = [ref[...] for ref in kv_refs]
    kv_blocks[early.index(1)] += more
    return [kv_blocks[early.index(back)] for back in sorted(early)]


def biased_keys(kv_blocks, bias_ref, places):
    tokens = kv_blocks[0].shape[0]
    keys = jnp.concatenate([rows[:, :HD] for rows in kv_blocks], axis=0)
    bias = jnp.concatenate([bias_ref[block(back, tokens), :] for back in places], axis=0)
    return jnp.concatenate([keys, bias], axis=1)


def early_kernel(early, late, query_t_ref, grad_t_ref, bias_ref, *refs):
    *kv_refs, weights_ref, grad_weights_ref, stats_ref, out_t_ref, scores_ref = refs
    tokens = kv_refs[0].shape[0]
    columns = parts(query_t_ref.shape[1], tokens)
    place = lax.axis_index("ulysses")

    def with_blocks(count):
        rows = slice(0, count * tokens)
        kv_blocks = joined(early, kv_refs)[:count]
        keys = biased_keys(kv_blocks, bias_ref, sorted(early)[:count])
        values = jnp.concatenate([own[:, HD:] for own in kv_blocks], axis=0)
        values_t = values.T
        for part in columns:
            scores_ref[rows, part] = dot(keys, query_t_ref[:, part])
        for part in columns:
            grad_weights = dot(values, grad_t_ref[:, part])
            grad_weights_ref[rows, part] = grad_weights
            top = jnp.max(scores_ref[rows, part], axis=0, keepdims=True) * exponent_scale
            weights = jnp.exp2(scores_ref[rows, part] * exponent_scale - top)
            stats_ref[0:1, part] = top
            stats_ref[1:2, part] = jnp.sum(weights, axis=0, keepdims=True)
            stats_ref[2:3, part] = jnp.sum(weights * grad_weights, axis=0, keepdims=True)
            weights_ref[rows, part] = weights.astype(jnp.bfloat16)
        for part in columns:
            out_t_ref[:, part] = dot(values_t, weights_ref[rows, part])

    pl.when(place <= late)(lambda: with_blocks(sum(back <= late for back in early)))
    pl.when(place > late)(lambda: with_blocks(len(early)))


def late_kernel(early, late, query_ref, grad_ref, query_t_ref, grad_t_ref, bias_ref, *refs):
    late_kv_ref, early_weights_ref, grad_weights_ref, stats_ref = refs[:4]
    weights_ref, scores_grad_ref, rescale_ref, late_term_ref, *term_refs, again_ref = refs[4:]
    tokens = late_kv_ref.shape[0]
    columns = parts(query_t_ref.shape[1], tokens)
    late_rows = block(len(early), tokens)
    place = lax.axis_index("ulysses")

    def with_blocks(count, has_late=True):
        early_rows = slice(0, count * tokens)
        far_rows = slice(tokens, count * tokens)
        term_rows = ([late_rows] if has_late else []) + [far_rows]
        if has_late:
            keys = biased_keys([late_kv_ref[...]], bias_ref, [late])
            values = late_kv_ref[:, HD:]
            scores = [dot(keys, query_t_ref[:, part]) for part in columns]
            grad_weights = [dot(values, grad_t_ref[:, part]) for part in columns]
        else:
            for ref in (weights_ref, scores_grad_ref):
                ref[late_rows, :] = jnp.zeros((tokens, ref.shape[1]), jnp.bfloat16)
        key_terms = value_terms = jnp.zeros(((count - 1 + has_late) * tokens, HD), jnp.float32)
        for index, part in enumerate(columns):
            rescale = 1.0
            total = stats_ref[1:2, part]
            if has_late:
                own, own_grad = scores[index], grad_weights[index]
                early_top = stats_ref[0:1, part]
                top = jnp.maximum(early_top, jnp.max(own, axis=0, keepdims=True) * exponent_scale)
                rescale = jnp.exp2(early_top - top)
                own = jnp.exp2(own * exponent_scale - top)
                total = rescale * total + jnp.sum(own, axis=0, keepdims=True)
            inverse = 1.0 / total
            rescale = rescale * inverse
            row_dots = rescale * stats_ref[2:3, part]
            rescale_ref[:, part] = rescale
            if has_late:
                own = own * inverse
                row_dots += jnp.sum(own * own_grad, axis=0, keepdims=True)
                weights_ref[late_rows, part] = own.astype(jnp.bfloat16)
                scores_grad_ref[late_rows, part] = (own * (own_grad - row_dots)).astype(
                    jnp.bfloat16
                )
            own = early_weights_ref[early_rows, part].astype(jnp.float32) * rescale
            weights_ref[early_rows, part] = own.astype(jnp.bfloat16)
            scores_grad_ref[early_rows, part] = (
                own * (grad_weights_ref[early_rows, part] - row_dots)
            ).astype(jnp.bfloat16)
            low_grad = [scores_grad_ref[rows, part] for rows in term_rows]
            low = [weights_ref[rows, part] for rows in term_rows]
            key_terms += dot(jnp.concatenate(low_grad, axis=0), query_ref[part, :])
            value_terms += dot(jnp.concatenate(low, axis=0), grad_ref[part, :])
        missing = len(early) - count
        if missing:
            scores_grad_ref[count * tokens : len(early) * tokens, :] = jnp.zeros(
                (missing * tokens, scores_grad_ref.shape[1]), jnp.bfloat16
            )
        terms = jnp.concatenate([key_terms * score_scale, value_terms], axis=1)
        terms = terms.astype(jnp.bfloat16)
        existing = ([late_term_ref] if has_late else []) + term_refs[: count - 1]
        for index, ref in enumerate(existing):
            ref[...] = terms[block(index, tokens)]
        for ref in term_refs[count - 1 :] + ([] if has_late else [late_term_ref]):
            ref[...] = jnp.zeros_like(ref)
        again_ref[...] = term_refs[0][...]

    exist = [sum(back <= reach for back in early) for reach in (late, max(early) - 1, max(early))]
    pl.when(place < late)(lambda: with_blocks(exist[0], has_late=False))
    pl.when(place == late)(lambda: with_blocks(exist[0]))
    pl.when((place > late) & (place < max(early)))(lambda: with_blocks(exist[1]))
    pl.when(place >= max(early))(lambda: with_blocks(exist[2]))


def near_kernel(early, query_ref, grad_ref, weights_ref, scores_grad_ref, rescale_ref, *refs):
    early_out_t_ref, late_kv_ref, *kv_refs, out_ref, query_grad_ref, near_ref = refs
    tokens = late_kv_ref.shape[0]
    late_out_t = dot(late_kv_ref[:, HD:].T, weights_ref[-tokens:, :])
    out_t = (early_out_t_ref[...] * rescale_ref[...] + late_out_t).astype(jnp.bfloat16)
    near_ref[...] = gradient_terms(
        weights_ref[:tokens, :], scores_grad_ref[:tokens, :], query_ref[...], grad_ref[...]
    )
    kv_blocks = joined(early, kv_refs) + [late_kv_ref[...]]
    keys_t = jnp.concatenate([rows[:, :HD] for rows in kv_blocks], axis=0).T
    query_grad_t = (dot(keys_t, scores_grad_ref[...]) * score_scale).astype(jnp.bfloat16)
    for head in range(out_ref.shape[1] // HD):
        own = block(head, tokens)
        query_grad_ref[:, block(head, HD)] = query_grad_t[:, own].T
        out_ref[:, block(head, HD)] = out_t[:, own].T


def call(body, name, outs, scratch, flops, *operands, fetched=False):
    vmem = pl.BlockSpec(memory_space=pltpu.VMEM)
    if fetched:
        operands = [pltpu.with_memory_space_constraint(a, pltpu.HBM) for a in operands]
    held = sum(math.prod(a.shape) * a.dtype.itemsize for a in operands)
    held += sum(math.prod(shape) * dtype.dtype.itemsize for shape, dtype in outs)
    held += sum(math.prod(s.shape) * 4 for s in scratch if hasattr(s, "shape"))
    return pl.pallas_call(
        body,
        out_shape=[jax.ShapeDtypeStruct(shape, dtype) for shape, dtype in outs],
        in_specs=[pl.BlockSpec(memory_space=pltpu.HBM) if fetched else vmem] * len(operands),
        out_specs=[vmem] * len(outs),
        scratch_shapes=scratch,
        compiler_params=pltpu.CompilerParams(
            vmem_limit_bytes=held + 12 * 1024 * 1024
        ),
        cost_estimate=pl.CostEstimate(flops=flops, bytes_accessed=held, transcendentals=0),
        name=name,
    )(*operands)


def ordered(values, order):
    first = [values[place] for place in order if place < len(values)]
    return first + [v for place, v in enumerate(values) if place not in order]


def per_device(devices, query_rows, key_rows, value_rows, grad_out, doc_lengths):
    tokens, query_width = query_rows.shape
    shared_heads = key_rows.shape[1] // HD
    length = tokens * devices
    reach = min(devices - 1, (length // 2 - 1 + tokens - 1) // tokens)
    blocks = reach + 1
    window = blocks * tokens
    low = jnp.bfloat16

    group_width = query_width // shared_heads
    columns = group_width // HD * tokens
    product = 2 * window * columns * HD
    kv, first_key = call(
        fetch_kernel,
        "fetch",
        [
            ((tokens, 2 * shared_heads * HD), low),
            ((1, tokens), jnp.int32),
        ],
        [
            pltpu.SMEM(doc_lengths.shape, jnp.int32),
            pltpu.SemaphoreType.DMA((2 * shared_heads + 1,)),
        ],
        16 * product,
        doc_lengths,
        key_rows,
        value_rows,
        fetched=True,
    )
    def forward(back, first, last):
        return lax.ppermute(kv, "ulysses", [(d - back, d) for d in range(max(first, back), last)])

    previous = [forward(1, reach + 1, devices), forward(1, 0, reach + 1)]
    kv_blocks = {0: kv}
    for back in ordered(list(range(blocks)), IN_ORDER)[1:]:
        kv_blocks[back] = previous[0] if back == 1 else forward(back, 0, devices)
    late = list(kv_blocks)[1]
    early = [0] + [back for back in kv_blocks if back not in (0, late)]
    places = early + [late]
    window_early = len(early) * tokens

    attention, grad_queries, totals, far = [], [], [], []
    for shared in range(shared_heads):
        own_queries = query_rows[:, block(shared, group_width)]
        own_grads = grad_out[:, block(shared, group_width)]
        if attention:
            own_queries, attention[-1] = lax.optimization_barrier((own_queries, attention[-1]))
        own_kv = [
            rows[:, block(shared, 2 * HD)]
            for rows in [kv_blocks[back] for back in places] + previous[1:]
        ]
        early_kv = own_kv[:-2] + own_kv[-1:]
        queries, grads, queries_t, grads_t, bias = call(
            functools.partial(prepare_kernel, reach),
            "prepare",
            [
                ((columns, HD), low),
                ((columns, HD), low),
                ((HD + tokens, columns), low),
                ((HD, columns), low),
                ((window, tokens), low),
            ],
            [],
            product // 4,
            first_key,
            own_queries,
            own_grads,
        )
        weights, grad_weights, stats, early_out_t = call(
            functools.partial(early_kernel, early, late),
            "early",
            [
                ((window_early, columns), low),
                ((window_early, columns), jnp.float32),
                ((3, columns), jnp.float32),
                ((HD, columns), jnp.float32),
            ],
            [pltpu.VMEM((window_early, columns), jnp.float32)],
            3 * product,
            queries_t,
            grads_t,
            bias,
            *early_kv,
        )
        weights, scores_grad, rescale, *own_far = call(
            functools.partial(late_kernel, early, late),
            "late",
            [((window, columns), low), ((window, columns), low), ((1, columns), jnp.float32)]
            + [((tokens, 2 * HD), low)] * (reach + 1),
            [],
            2 * product,
            queries,
            grads,
            queries_t,
            grads_t,
            bias,
            own_kv[-2],
            weights,
            grad_weights,
            stats,
        )
        own_out, own_query_grad, own_total = call(
            functools.partial(near_kernel, early),
            "near",
            [((tokens, group_width), low)] * 2 + [((tokens, 2 * HD), jnp.float32)],
            [],
            2 * product,
            queries,
            grads,
            weights,
            scores_grad,
            rescale,
            early_out_t,
            own_kv[-2],
            *early_kv,
        )
        attention.append(own_out)
        grad_queries.append(own_query_grad)
        totals.append(own_total)
        far.append(own_far)

    def side_by_side(parts):
        return parts[0] if len(parts) == 1 else jnp.concatenate(parts, axis=1)

    far_places = [late] + sorted(early)[1:]
    total = side_by_side(totals)
    returns = [(back, 0, devices) for back in ordered(list(range(blocks)), OUT_ORDER)[1:]]
    returns[-2:] = [(1, reach + 1, devices), returns[-2], (1, 0, reach + 1)]
    for back, first, last in returns:
        index = reach if last == reach + 1 else far_places.index(back)
        terms = side_by_side([own[index] for own in far])
        terms = lax.ppermute(
            terms, "ulysses", [(d + back, d) for d in range(first, min(last, devices - back))]
        )
        total = total + terms.astype(jnp.float32)
    total = total.astype(low)
    grad_keys = side_by_side([total[:, block(2 * g, HD)] for g in range(shared_heads)])
    grad_values = side_by_side([total[:, block(2 * g + 1, HD)] for g in range(shared_heads)])
    return (side_by_side(attention), side_by_side(grad_queries), grad_keys, grad_values)


def solution(mesh):
    rows = P(("dp", "ulysses"), None)
    return jax.shard_map(
        functools.partial(per_device, mesh.shape["ulysses"]),
        mesh=mesh,
        in_specs=(rows, rows, rows, rows, P()),
        out_specs=(rows, rows, rows, rows),
        check_vma=False,
    )
```

```python
import functools
import math

import jax
import jax.numpy as jnp
from jax import lax
from jax.experimental import pallas as pl
from jax.experimental.pallas import tpu as pltpu
from jax.sharding import PartitionSpec as P

HD = 128
PAIR = 2
masked_score = -1e30
IN_ORDER = (0, 2, 1, 4, 3)
OUT_ORDER = (0, 4, 3, 2, 1)
score_scale = 1.0 / math.sqrt(HD)
exponent_scale = score_scale * math.log2(math.e)

NN = (((1,), (0,)), ((), ()))
NT = (((1,), (1,)), ((), ()))


def dot(a, b, dims=NN):
    return lax.dot_general(a, b, dims, preferred_element_type=jnp.float32)


def block(index, size):
    return slice(index * size, (index + 1) * size)


def fetch_kernel(doc_hbm, key_hbm, value_hbm, kv_ref, first_key_ref, doc_ref, sems):
    pairs = [(doc_hbm, doc_ref)]
    for shared in range(key_hbm.shape[1] // HD):
        for part, ref in enumerate((key_hbm, value_hbm)):
            pairs.append(
                (ref.at[:, pl.ds(shared * HD, HD)], kv_ref.at[:, pl.ds((2 * shared + part) * HD, HD)])
            )
    copies = [pltpu.make_async_copy(src, dst, sems.at[i]) for i, (src, dst) in enumerate(pairs)]
    for copy in copies:
        copy.start()
    tokens = key_hbm.shape[0]
    row = lax.axis_index("dp")
    place = lax.axis_index("ulysses")
    query_pos = place * tokens + lax.broadcasted_iota(jnp.int32, (1, tokens), 1)
    first_key = jnp.zeros((1, tokens), jnp.int32)
    copies[0].wait()
    doc_end = jnp.int32(0)
    for doc in range(doc_ref.shape[1]):
        doc_end = doc_end + doc_ref[row, doc]
        first_key = jnp.where(doc_end <= query_pos, doc_end, first_key)
    first_key_ref[...] = first_key
    for copy in copies[1:]:
        copy.wait()


def prepare_kernel(reach, first_key_ref, query_ref, grad_ref, *refs):
    query_rows_ref, grad_rows_ref, query_t_ref, grad_t_ref, bias_ref = refs
    tokens = query_ref.shape[0]
    place = lax.axis_index("ulysses")
    inner = lax.broadcasted_iota(jnp.int32, (tokens, tokens), 0)
    lanes = lax.broadcasted_iota(jnp.int32, (tokens, tokens), 1)
    first_key = first_key_ref[...] - place * tokens
    for back in range(reach + 1):
        key_pos = inner - back * tokens
        allowed = (key_pos >= first_key) & (key_pos <= lanes)
        bias_ref[block(back, tokens), :] = jnp.where(allowed, 0.0, masked_score).astype(
            jnp.bfloat16
        )
    identity = jnp.where(inner == lanes, 1.0, 0.0).astype(jnp.bfloat16)
    for head in range(query_ref.shape[1] // HD):
        own = block(head, tokens)
        queries = query_ref[:, block(head, HD)]
        grads = grad_ref[:, block(head, HD)]
        query_rows_ref[own, :] = queries
        grad_rows_ref[own, :] = grads
        query_t_ref[:HD, own] = queries.T
        query_t_ref[HD:, own] = identity
        grad_t_ref[:, own] = grads.T


def gradient_terms(weights, scores_grad, queries, grads):
    key_terms = dot(scores_grad, queries) * score_scale
    value_terms = dot(weights, grads)
    return jnp.concatenate([key_terms, value_terms], axis=1)


def parts(columns, tokens):
    width = min(columns, PAIR * tokens)
    return [slice(start, start + width) for start in range(0, columns, width)]


def joined(early, kv_refs):
    *kv_blocks, more = [ref[...] for ref in kv_refs]
    kv_blocks[early.index(1)] += more
    return [kv_blocks[early.index(back)] for back in sorted(early)]


def biased_keys(kv_blocks, bias_ref, places):
    tokens = kv_blocks[0].shape[0]
    keys = jnp.concatenate([rows[:, :HD] for rows in kv_blocks], axis=0)
    bias = jnp.concatenate([bias_ref[block(back, tokens), :] for back in places], axis=0)
    return jnp.concatenate([keys, bias], axis=1)


def early_kernel(early, late, query_t_ref, grad_t_ref, bias_ref, *refs):
    *kv_refs, weights_ref, grad_weights_ref, stats_ref, out_t_ref, scores_ref = refs
    del kv_refs[2]
    tokens = kv_refs[0].shape[0]
    columns = parts(query_t_ref.shape[1], tokens)
    place = lax.axis_index("ulysses")

    def with_blocks(count):
        rows = slice(0, count * tokens)
        kv_blocks = joined(early, kv_refs)[:count]
        keys = biased_keys(kv_blocks, bias_ref, sorted(early)[:count])
        values = jnp.concatenate([own[:, HD:] for own in kv_blocks], axis=0)
        values_t = values.T
        for part in columns:
            scores_ref[rows, part] = dot(keys, query_t_ref[:, part])
        for part in columns:
            grad_weights = dot(values, grad_t_ref[:, part])
            grad_weights_ref[rows, part] = grad_weights
            top = jnp.max(scores_ref[rows, part], axis=0, keepdims=True) * exponent_scale
            weights = jnp.exp2(scores_ref[rows, part] * exponent_scale - top)
            stats_ref[0:1, part] = top
            stats_ref[1:2, part] = jnp.sum(weights, axis=0, keepdims=True)
            stats_ref[2:3, part] = jnp.sum(weights * grad_weights, axis=0, keepdims=True)
            weights_ref[rows, part] = weights.astype(jnp.bfloat16)
        for part in columns:
            out_t_ref[:, part] = dot(values_t, weights_ref[rows, part])

    pl.when(place <= late)(lambda: with_blocks(sum(back <= late for back in early)))
    pl.when(place > late)(lambda: with_blocks(len(early)))


def late_kernel(early, late, query_ref, grad_ref, query_t_ref, grad_t_ref, bias_ref, *refs):
    early_weights_ref, grad_weights_ref, stats_ref, kv_ref, more_kv_ref = refs[:5]
    weights_ref, scores_grad_ref, rescale_ref, late_term_ref, *term_refs, again_ref = refs[5:]
    tokens = kv_ref.shape[0]
    columns = parts(query_t_ref.shape[1], tokens)
    late_rows = block(len(early), tokens)
    place = lax.axis_index("ulysses")

    def with_blocks(count, has_late=True):
        early_rows = slice(0, count * tokens)
        far_rows = slice(tokens, count * tokens)
        term_rows = ([late_rows] if has_late else []) + [far_rows]
        if has_late:
            late_kv = kv_ref[...] + more_kv_ref[...]
            keys = biased_keys([late_kv], bias_ref, [late])
            values = late_kv[:, HD:]
            scores = [dot(keys, query_t_ref[:, part]) for part in columns]
            grad_weights = [dot(values, grad_t_ref[:, part]) for part in columns]
        else:
            for ref in (weights_ref, scores_grad_ref):
                ref[late_rows, :] = jnp.zeros((tokens, ref.shape[1]), jnp.bfloat16)
        key_terms = value_terms = jnp.zeros(((count - 1 + has_late) * tokens, HD), jnp.float32)
        for index, part in enumerate(columns):
            rescale = 1.0
            total = stats_ref[1:2, part]
            if has_late:
                own, own_grad = scores[index], grad_weights[index]
                early_top = stats_ref[0:1, part]
                top = jnp.maximum(early_top, jnp.max(own, axis=0, keepdims=True) * exponent_scale)
                rescale = jnp.exp2(early_top - top)
                own = jnp.exp2(own * exponent_scale - top)
                total = rescale * total + jnp.sum(own, axis=0, keepdims=True)
            inverse = 1.0 / total
            rescale = rescale * inverse
            row_dots = rescale * stats_ref[2:3, part]
            rescale_ref[:, part] = rescale
            if has_late:
                own = own * inverse
                row_dots += jnp.sum(own * own_grad, axis=0, keepdims=True)
                weights_ref[late_rows, part] = own.astype(jnp.bfloat16)
                scores_grad_ref[late_rows, part] = (own * (own_grad - row_dots)).astype(
                    jnp.bfloat16
                )
            own = early_weights_ref[early_rows, part].astype(jnp.float32) * rescale
            weights_ref[early_rows, part] = own.astype(jnp.bfloat16)
            scores_grad_ref[early_rows, part] = (
                own * (grad_weights_ref[early_rows, part] - row_dots)
            ).astype(jnp.bfloat16)
            low_grad = [scores_grad_ref[rows, part] for rows in term_rows]
            low = [weights_ref[rows, part] for rows in term_rows]
            key_terms += dot(jnp.concatenate(low_grad, axis=0), query_ref[part, :])
            value_terms += dot(jnp.concatenate(low, axis=0), grad_ref[part, :])
        missing = len(early) - count
        if missing:
            scores_grad_ref[count * tokens : len(early) * tokens, :] = jnp.zeros(
                (missing * tokens, scores_grad_ref.shape[1]), jnp.bfloat16
            )
        terms = jnp.concatenate([key_terms * score_scale, value_terms], axis=1)
        terms = terms.astype(jnp.bfloat16)
        existing = ([late_term_ref] if has_late else []) + term_refs[: count - 1]
        for index, ref in enumerate(existing):
            ref[...] = terms[block(index, tokens)]
        for ref in term_refs[count - 1 :] + ([] if has_late else [late_term_ref]):
            ref[...] = jnp.zeros_like(ref)
        again_ref[...] = term_refs[0][...]

    exist = [sum(back <= reach for back in early) for reach in (late, max(early) - 1, max(early))]
    pl.when(place < late)(lambda: with_blocks(exist[0], has_late=False))
    pl.when(place == late)(lambda: with_blocks(exist[0]))
    pl.when((place > late) & (place < max(early)))(lambda: with_blocks(exist[1]))
    pl.when(place >= max(early))(lambda: with_blocks(exist[2]))


def near_kernel(early, query_ref, grad_ref, weights_ref, scores_grad_ref, rescale_ref, *refs):
    early_out_t_ref, kv_ref, more_kv_ref, *kv_refs, out_ref, query_grad_ref, near_ref = refs
    tokens = kv_ref.shape[0]
    late_kv = kv_ref[...] + more_kv_ref[...]
    late_out_t = dot(late_kv[:, HD:].T, weights_ref[-tokens:, :])
    out_t = (early_out_t_ref[...] * rescale_ref[...] + late_out_t).astype(jnp.bfloat16)
    near_ref[...] = gradient_terms(
        weights_ref[:tokens, :], scores_grad_ref[:tokens, :], query_ref[...], grad_ref[...]
    )
    kv_blocks = joined(early, kv_refs) + [late_kv]
    keys_t = jnp.concatenate([rows[:, :HD] for rows in kv_blocks], axis=0).T
    query_grad_t = (dot(keys_t, scores_grad_ref[...]) * score_scale).astype(jnp.bfloat16)
    for head in range(out_ref.shape[1] // HD):
        own = block(head, tokens)
        query_grad_ref[:, block(head, HD)] = query_grad_t[:, own].T
        out_ref[:, block(head, HD)] = out_t[:, own].T


def call(body, name, outs, scratch, flops, *operands, fetched=False):
    vmem = pl.BlockSpec(memory_space=pltpu.VMEM)
    if fetched:
        operands = [pltpu.with_memory_space_constraint(a, pltpu.HBM) for a in operands]
    held = sum(math.prod(a.shape) * a.dtype.itemsize for a in operands)
    held += sum(math.prod(shape) * dtype.dtype.itemsize for shape, dtype in outs)
    held += sum(math.prod(s.shape) * 4 for s in scratch if hasattr(s, "shape"))
    return pl.pallas_call(
        body,
        out_shape=[jax.ShapeDtypeStruct(shape, dtype) for shape, dtype in outs],
        in_specs=[pl.BlockSpec(memory_space=pltpu.HBM) if fetched else vmem] * len(operands),
        out_specs=[vmem] * len(outs),
        scratch_shapes=scratch,
        compiler_params=pltpu.CompilerParams(
            vmem_limit_bytes=held + 12 * 1024 * 1024
        ),
        cost_estimate=pl.CostEstimate(flops=flops, bytes_accessed=held, transcendentals=0),
        name=name,
    )(*operands)


def ordered(values, order):
    first = [values[place] for place in order if place < len(values)]
    return first + [v for place, v in enumerate(values) if place not in order]


def per_device(devices, query_rows, key_rows, value_rows, grad_out, doc_lengths):
    tokens, query_width = query_rows.shape
    shared_heads = key_rows.shape[1] // HD
    length = tokens * devices
    reach = min(devices - 1, (length // 2 - 1 + tokens - 1) // tokens)
    blocks = reach + 1
    window = blocks * tokens
    low = jnp.bfloat16

    group_width = query_width // shared_heads
    columns = group_width // HD * tokens
    product = 2 * window * columns * HD
    kv, first_key = call(
        fetch_kernel,
        "fetch",
        [
            ((tokens, 2 * shared_heads * HD), low),
            ((1, tokens), jnp.int32),
        ],
        [
            pltpu.SMEM(doc_lengths.shape, jnp.int32),
            pltpu.SemaphoreType.DMA((2 * shared_heads + 1,)),
        ],
        16 * product,
        doc_lengths,
        key_rows,
        value_rows,
        fetched=True,
    )
    def forward(back, first, last):
        return lax.ppermute(kv, "ulysses", [(d - back, d) for d in range(max(first, back), last)])

    halves = {back: [forward(back, reach + 1, devices), forward(back, 0, reach + 1)] for back in (1, 2)}
    kv_blocks = {0: kv}
    for back in ordered(list(range(blocks)), IN_ORDER)[1:]:
        kv_blocks[back] = halves[back][0] if back in halves else forward(back, 0, devices)
    late = list(kv_blocks)[1]
    early = [0] + [back for back in kv_blocks if back not in (0, late)]
    places = early + [late]
    window_early = len(early) * tokens

    attention, grad_queries, totals, far = [], [], [], []
    for shared in range(shared_heads):
        own_queries = query_rows[:, block(shared, group_width)]
        own_grads = grad_out[:, block(shared, group_width)]
        if attention:
            own_queries, attention[-1] = lax.optimization_barrier((own_queries, attention[-1]))
        early_kv, late_kv = [
            [rows[:, block(shared, 2 * HD)] for rows in arrays]
            for arrays in (
                [kv_blocks[back] for back in early] + halves[1][1:],
                halves[late],
            )
        ]
        queries, grads, queries_t, grads_t, bias = call(
            functools.partial(prepare_kernel, reach),
            "prepare",
            [
                ((columns, HD), low),
                ((columns, HD), low),
                ((HD + tokens, columns), low),
                ((HD, columns), low),
                ((window, tokens), low),
            ],
            [],
            product // 4,
            first_key,
            own_queries,
            own_grads,
        )
        weights, grad_weights, stats, early_out_t = call(
            functools.partial(early_kernel, early, late),
            "early",
            [
                ((window_early, columns), low),
                ((window_early, columns), jnp.float32),
                ((3, columns), jnp.float32),
                ((HD, columns), jnp.float32),
            ],
            [pltpu.VMEM((window_early, columns), jnp.float32)],
            3 * product,
            queries_t,
            grads_t,
            bias,
            *early_kv[:2],
            late_kv[1],
            *early_kv[2:],
        )
        weights, scores_grad, rescale, *own_far = call(
            functools.partial(late_kernel, early, late),
            "late",
            [((window, columns), low), ((window, columns), low), ((1, columns), jnp.float32)]
            + [((tokens, 2 * HD), low)] * (reach + 1),
            [],
            2 * product,
            queries,
            grads,
            queries_t,
            grads_t,
            bias,
            weights,
            grad_weights,
            stats,
            *late_kv,
        )
        own_out, own_query_grad, own_total = call(
            functools.partial(near_kernel, early),
            "near",
            [((tokens, group_width), low)] * 2 + [((tokens, 2 * HD), jnp.float32)],
            [],
            2 * product,
            queries,
            grads,
            weights,
            scores_grad,
            rescale,
            early_out_t,
            *late_kv,
            *early_kv,
        )
        attention.append(own_out)
        grad_queries.append(own_query_grad)
        totals.append(own_total)
        far.append(own_far)

    def side_by_side(parts):
        return parts[0] if len(parts) == 1 else jnp.concatenate(parts, axis=1)

    far_places = [late] + sorted(early)[1:]
    total = side_by_side(totals)
    returns = [(back, 0, devices) for back in ordered(list(range(blocks)), OUT_ORDER)[1:]]
    returns[-2:] = [(1, reach + 1, devices), returns[-2], (1, 0, reach + 1)]
    for back, first, last in returns:
        index = reach if last == reach + 1 else far_places.index(back)
        terms = side_by_side([own[index] for own in far])
        terms = lax.ppermute(
            terms, "ulysses", [(d + back, d) for d in range(first, min(last, devices - back))]
        )
        total = total + terms.astype(jnp.float32)
    total = total.astype(low)
    grad_keys = side_by_side([total[:, block(2 * g, HD)] for g in range(shared_heads)])
    grad_values = side_by_side([total[:, block(2 * g + 1, HD)] for g in range(shared_heads)])
    return (side_by_side(attention), side_by_side(grad_queries), grad_keys, grad_values)


def solution(mesh):
    rows = P(("dp", "ulysses"), None)
    return jax.shard_map(
        functools.partial(per_device, mesh.shape["ulysses"]),
        mesh=mesh,
        in_specs=(rows, rows, rows, rows, P()),
        out_specs=(rows, rows, rows, rows),
        check_vma=False,
    )
```

```python
import functools
import math

import jax
import jax.numpy as jnp
from jax import lax
from jax.experimental import pallas as pl
from jax.experimental.pallas import tpu as pltpu
from jax.sharding import PartitionSpec as P

HD = 128
PAIR = 2
masked_score = -1e30
IN_ORDER = (0, 2, 1, 4, 3)
OUT_ORDER = (0, 4, 3, 2, 1)
score_scale = 1.0 / math.sqrt(HD)
exponent_scale = score_scale * math.log2(math.e)

NN = (((1,), (0,)), ((), ()))
NT = (((1,), (1,)), ((), ()))


def dot(a, b, dims=NN):
    return lax.dot_general(a, b, dims, preferred_element_type=jnp.float32)


def block(index, size):
    return slice(index * size, (index + 1) * size)


def fetch_kernel(key_hbm, value_hbm, kv_ref, sems):
    pairs = []
    for shared in range(key_hbm.shape[1] // HD):
        for part, ref in enumerate((key_hbm, value_hbm)):
            pairs.append(
                (ref.at[:, pl.ds(shared * HD, HD)], kv_ref.at[:, pl.ds((2 * shared + part) * HD, HD)])
            )
    copies = [pltpu.make_async_copy(src, dst, sems.at[i]) for i, (src, dst) in enumerate(pairs)]
    for copy in copies:
        copy.start()
    for copy in copies:
        copy.wait()


def prepare_kernel(reach, doc_ref, query_ref, grad_ref, *refs):
    query_rows_ref, grad_rows_ref, query_t_ref, grad_t_ref, bias_ref = refs
    tokens = query_ref.shape[0]
    place = lax.axis_index("ulysses")
    inner = lax.broadcasted_iota(jnp.int32, (tokens, tokens), 0)
    lanes = lax.broadcasted_iota(jnp.int32, (tokens, tokens), 1)
    row = lax.axis_index("dp")
    first_key = jnp.zeros((1, tokens), jnp.int32)
    doc_end = jnp.int32(0)
    for doc in range(doc_ref.shape[1]):
        doc_end = doc_end + doc_ref[row, doc]
        first_key = jnp.where(doc_end <= place * tokens + lanes[:1], doc_end, first_key)
    first_key = first_key - place * tokens
    for back in range(reach + 1):
        key_pos = inner - back * tokens
        allowed = (key_pos >= first_key) & (key_pos <= lanes)
        bias_ref[block(back, tokens), :] = jnp.where(allowed, 0.0, masked_score).astype(
            jnp.bfloat16
        )
    identity = jnp.where(inner == lanes, 1.0, 0.0).astype(jnp.bfloat16)
    for head in range(query_ref.shape[1] // HD):
        own = block(head, tokens)
        queries = query_ref[:, block(head, HD)]
        grads = grad_ref[:, block(head, HD)]
        query_rows_ref[own, :] = queries
        grad_rows_ref[own, :] = grads
        query_t_ref[:HD, own] = queries.T
        query_t_ref[HD:, own] = identity
        grad_t_ref[:, own] = grads.T


def gradient_terms(weights, scores_grad, queries, grads):
    key_terms = dot(scores_grad, queries) * score_scale
    value_terms = dot(weights, grads)
    return jnp.concatenate([key_terms, value_terms], axis=1)


def parts(columns, tokens):
    width = min(columns, PAIR * tokens)
    return [slice(start, start + width) for start in range(0, columns, width)]


def joined(early, kv_refs):
    *kv_blocks, more = [ref[...] for ref in kv_refs]
    kv_blocks[early.index(1)] += more
    return [kv_blocks[early.index(back)] for back in sorted(early)]


def biased_keys(kv_blocks, bias_ref, places):
    tokens = kv_blocks[0].shape[0]
    keys = jnp.concatenate([rows[:, :HD] for rows in kv_blocks], axis=0)
    bias = jnp.concatenate([bias_ref[block(back, tokens), :] for back in places], axis=0)
    return jnp.concatenate([keys, bias], axis=1)


def early_kernel(early, late, query_t_ref, grad_t_ref, bias_ref, *refs):
    *kv_refs, weights_ref, grad_weights_ref, stats_ref, out_t_ref, scores_ref = refs
    tokens = kv_refs[0].shape[0]
    columns = parts(query_t_ref.shape[1], tokens)
    place = lax.axis_index("ulysses")

    def with_blocks(count):
        rows = slice(0, count * tokens)
        kv_blocks = joined(early, kv_refs)[:count]
        keys = biased_keys(kv_blocks, bias_ref, sorted(early)[:count])
        values = jnp.concatenate([own[:, HD:] for own in kv_blocks], axis=0)
        values_t = values.T
        for part in columns:
            scores_ref[rows, part] = dot(keys, query_t_ref[:, part])
        for part in columns:
            grad_weights = dot(values, grad_t_ref[:, part])
            grad_weights_ref[rows, part] = grad_weights
            top = jnp.max(scores_ref[rows, part], axis=0, keepdims=True) * exponent_scale
            weights = jnp.exp2(scores_ref[rows, part] * exponent_scale - top)
            stats_ref[0:1, part] = top
            stats_ref[1:2, part] = jnp.sum(weights, axis=0, keepdims=True)
            stats_ref[2:3, part] = jnp.sum(weights * grad_weights, axis=0, keepdims=True)
            weights_ref[rows, part] = weights.astype(jnp.bfloat16)
        for part in columns:
            out_t_ref[:, part] = dot(values_t, weights_ref[rows, part])

    pl.when(place <= late)(lambda: with_blocks(sum(back <= late for back in early)))
    pl.when(place > late)(lambda: with_blocks(len(early)))


def late_kernel(early, late, query_ref, grad_ref, query_t_ref, grad_t_ref, bias_ref, *refs):
    late_kv_ref, early_weights_ref, grad_weights_ref, stats_ref = refs[:4]
    weights_ref, scores_grad_ref, rescale_ref, late_term_ref, *term_refs, again_ref = refs[4:]
    tokens = late_kv_ref.shape[0]
    columns = parts(query_t_ref.shape[1], tokens)
    late_rows = block(len(early), tokens)
    place = lax.axis_index("ulysses")

    def with_blocks(count, has_late=True):
        early_rows = slice(0, count * tokens)
        far_rows = slice(tokens, count * tokens)
        term_rows = ([late_rows] if has_late else []) + [far_rows]
        if has_late:
            keys = biased_keys([late_kv_ref[...]], bias_ref, [late])
            values = late_kv_ref[:, HD:]
            scores = [dot(keys, query_t_ref[:, part]) for part in columns]
            grad_weights = [dot(values, grad_t_ref[:, part]) for part in columns]
        else:
            for ref in (weights_ref, scores_grad_ref):
                ref[late_rows, :] = jnp.zeros((tokens, ref.shape[1]), jnp.bfloat16)
        key_terms = value_terms = jnp.zeros(((count - 1 + has_late) * tokens, HD), jnp.float32)
        for index, part in enumerate(columns):
            rescale = 1.0
            total = stats_ref[1:2, part]
            if has_late:
                own, own_grad = scores[index], grad_weights[index]
                early_top = stats_ref[0:1, part]
                top = jnp.maximum(early_top, jnp.max(own, axis=0, keepdims=True) * exponent_scale)
                rescale = jnp.exp2(early_top - top)
                own = jnp.exp2(own * exponent_scale - top)
                total = rescale * total + jnp.sum(own, axis=0, keepdims=True)
            inverse = 1.0 / total
            rescale = rescale * inverse
            row_dots = rescale * stats_ref[2:3, part]
            rescale_ref[:, part] = rescale
            if has_late:
                own = own * inverse
                row_dots += jnp.sum(own * own_grad, axis=0, keepdims=True)
                weights_ref[late_rows, part] = own.astype(jnp.bfloat16)
                scores_grad_ref[late_rows, part] = (own * (own_grad - row_dots)).astype(
                    jnp.bfloat16
                )
            own = early_weights_ref[early_rows, part].astype(jnp.float32) * rescale
            weights_ref[early_rows, part] = own.astype(jnp.bfloat16)
            scores_grad_ref[early_rows, part] = (
                own * (grad_weights_ref[early_rows, part] - row_dots)
            ).astype(jnp.bfloat16)
            low_grad = [scores_grad_ref[rows, part] for rows in term_rows]
            low = [weights_ref[rows, part] for rows in term_rows]
            key_terms += dot(jnp.concatenate(low_grad, axis=0), query_ref[part, :])
            value_terms += dot(jnp.concatenate(low, axis=0), grad_ref[part, :])
        missing = len(early) - count
        if missing:
            scores_grad_ref[count * tokens : len(early) * tokens, :] = jnp.zeros(
                (missing * tokens, scores_grad_ref.shape[1]), jnp.bfloat16
            )
        terms = jnp.concatenate([key_terms * score_scale, value_terms], axis=1)
        terms = terms.astype(jnp.bfloat16)
        existing = ([late_term_ref] if has_late else []) + term_refs[: count - 1]
        for index, ref in enumerate(existing):
            ref[...] = terms[block(index, tokens)]
        for ref in term_refs[count - 1 :] + ([] if has_late else [late_term_ref]):
            ref[...] = jnp.zeros_like(ref)
        again_ref[...] = term_refs[0][...]

    exist = [sum(back <= reach for back in early) for reach in (late, max(early) - 1, max(early))]
    pl.when(place < late)(lambda: with_blocks(exist[0], has_late=False))
    pl.when(place == late)(lambda: with_blocks(exist[0]))
    pl.when((place > late) & (place < max(early)))(lambda: with_blocks(exist[1]))
    pl.when(place >= max(early))(lambda: with_blocks(exist[2]))


def near_kernel(early, query_ref, grad_ref, weights_ref, scores_grad_ref, rescale_ref, *refs):
    early_out_t_ref, late_kv_ref, *kv_refs, out_ref, query_grad_ref, near_ref = refs
    tokens = late_kv_ref.shape[0]
    late_out_t = dot(late_kv_ref[:, HD:].T, weights_ref[-tokens:, :])
    out_t = (early_out_t_ref[...] * rescale_ref[...] + late_out_t).astype(jnp.bfloat16)
    near_ref[...] = gradient_terms(
        weights_ref[:tokens, :], scores_grad_ref[:tokens, :], query_ref[...], grad_ref[...]
    )
    kv_blocks = joined(early, kv_refs) + [late_kv_ref[...]]
    keys_t = jnp.concatenate([rows[:, :HD] for rows in kv_blocks], axis=0).T
    query_grad_t = (dot(keys_t, scores_grad_ref[...]) * score_scale).astype(jnp.bfloat16)
    for head in range(out_ref.shape[1] // HD):
        own = block(head, tokens)
        query_grad_ref[:, block(head, HD)] = query_grad_t[:, own].T
        out_ref[:, block(head, HD)] = out_t[:, own].T


def call(body, name, outs, scratch, flops, *operands, fetched=False):
    vmem = pl.BlockSpec(memory_space=pltpu.VMEM)
    if fetched:
        operands = [pltpu.with_memory_space_constraint(a, pltpu.HBM) for a in operands]
    held = sum(math.prod(a.shape) * a.dtype.itemsize for a in operands)
    held += sum(math.prod(shape) * dtype.dtype.itemsize for shape, dtype in outs)
    held += sum(math.prod(s.shape) * 4 for s in scratch if hasattr(s, "shape"))
    return pl.pallas_call(
        body,
        out_shape=[jax.ShapeDtypeStruct(shape, dtype) for shape, dtype in outs],
        in_specs=[
            pl.BlockSpec(memory_space=pltpu.HBM)
            if fetched
            else pl.BlockSpec(memory_space=pltpu.SMEM)
            if a.dtype == jnp.int32
            else vmem
            for a in operands
        ],
        out_specs=[vmem] * len(outs),
        scratch_shapes=scratch,
        compiler_params=pltpu.CompilerParams(
            vmem_limit_bytes=held + 12 * 1024 * 1024
        ),
        cost_estimate=pl.CostEstimate(flops=flops, bytes_accessed=held, transcendentals=0),
        name=name,
    )(*operands)


def ordered(values, order):
    first = [values[place] for place in order if place < len(values)]
    return first + [v for place, v in enumerate(values) if place not in order]


def per_device(devices, query_rows, key_rows, value_rows, grad_out, doc_lengths):
    tokens, query_width = query_rows.shape
    shared_heads = key_rows.shape[1] // HD
    length = tokens * devices
    reach = min(devices - 1, (length // 2 - 1 + tokens - 1) // tokens)
    blocks = reach + 1
    window = blocks * tokens
    low = jnp.bfloat16

    group_width = query_width // shared_heads
    columns = group_width // HD * tokens
    product = 2 * window * columns * HD
    (kv,) = call(
        fetch_kernel,
        "fetch",
        [
            ((tokens, 2 * shared_heads * HD), low),
        ],
        [pltpu.SemaphoreType.DMA((2 * shared_heads,))],
        16 * product,
        key_rows,
        value_rows,
        fetched=True,
    )
    def forward(back, first, last):
        return lax.ppermute(kv, "ulysses", [(d - back, d) for d in range(max(first, back), last)])

    previous = [forward(1, reach + 1, devices), forward(1, 0, reach + 1)]
    kv_blocks = {0: kv}
    for back in ordered(list(range(blocks)), IN_ORDER)[1:]:
        kv_blocks[back] = previous[0] if back == 1 else forward(back, 0, devices)
    late = list(kv_blocks)[1]
    early = [0] + [back for back in kv_blocks if back not in (0, late)]
    places = early + [late]
    window_early = len(early) * tokens

    attention, grad_queries, totals, far = [], [], [], []
    for shared in range(shared_heads):
        own_queries = query_rows[:, block(shared, group_width)]
        own_grads = grad_out[:, block(shared, group_width)]
        if attention:
            own_queries, attention[-1] = lax.optimization_barrier((own_queries, attention[-1]))
        own_kv = [
            rows[:, block(shared, 2 * HD)]
            for rows in [kv_blocks[back] for back in places] + previous[1:]
        ]
        early_kv = own_kv[:-2] + own_kv[-1:]
        queries, grads, queries_t, grads_t, bias = call(
            functools.partial(prepare_kernel, reach),
            "prepare",
            [
                ((columns, HD), low),
                ((columns, HD), low),
                ((HD + tokens, columns), low),
                ((HD, columns), low),
                ((window, tokens), low),
            ],
            [],
            product // 4,
            doc_lengths,
            own_queries,
            own_grads,
        )
        weights, grad_weights, stats, early_out_t = call(
            functools.partial(early_kernel, early, late),
            "early",
            [
                ((window_early, columns), low),
                ((window_early, columns), jnp.float32),
                ((3, columns), jnp.float32),
                ((HD, columns), jnp.float32),
            ],
            [pltpu.VMEM((window_early, columns), jnp.float32)],
            3 * product,
            queries_t,
            grads_t,
            bias,
            *early_kv,
        )
        weights, scores_grad, rescale, *own_far = call(
            functools.partial(late_kernel, early, late),
            "late",
            [((window, columns), low), ((window, columns), low), ((1, columns), jnp.float32)]
            + [((tokens, 2 * HD), low)] * (reach + 1),
            [],
            2 * product,
            queries,
            grads,
            queries_t,
            grads_t,
            bias,
            own_kv[-2],
            weights,
            grad_weights,
            stats,
        )
        own_out, own_query_grad, own_total = call(
            functools.partial(near_kernel, early),
            "near",
            [((tokens, group_width), low)] * 2 + [((tokens, 2 * HD), jnp.float32)],
            [],
            2 * product,
            queries,
            grads,
            weights,
            scores_grad,
            rescale,
            early_out_t,
            own_kv[-2],
            *early_kv,
        )
        attention.append(own_out)
        grad_queries.append(own_query_grad)
        totals.append(own_total)
        far.append(own_far)

    def side_by_side(parts):
        return parts[0] if len(parts) == 1 else jnp.concatenate(parts, axis=1)

    far_places = [late] + sorted(early)[1:]
    total = side_by_side(totals)
    returns = [(back, 0, devices) for back in ordered(list(range(blocks)), OUT_ORDER)[1:]]
    returns[-2:] = [(1, reach + 1, devices), returns[-2], (1, 0, reach + 1)]
    for back, first, last in returns:
        index = reach if last == reach + 1 else far_places.index(back)
        terms = side_by_side([own[index] for own in far])
        terms = lax.ppermute(
            terms, "ulysses", [(d + back, d) for d in range(first, min(last, devices - back))]
        )
        total = total + terms.astype(jnp.float32)
    total = total.astype(low)
    grad_keys = side_by_side([total[:, block(2 * g, HD)] for g in range(shared_heads)])
    grad_values = side_by_side([total[:, block(2 * g + 1, HD)] for g in range(shared_heads)])
    return (side_by_side(attention), side_by_side(grad_queries), grad_keys, grad_values)


def solution(mesh):
    rows = P(("dp", "ulysses"), None)
    return jax.shard_map(
        functools.partial(per_device, mesh.shape["ulysses"]),
        mesh=mesh,
        in_specs=(rows, rows, rows, rows, P()),
        out_specs=(rows, rows, rows, rows),
        check_vma=False,
    )
```

```python
import functools
import math

import jax
import jax.numpy as jnp
from jax import lax
from jax.experimental import pallas as pl
from jax.experimental.pallas import tpu as pltpu
from jax.sharding import PartitionSpec as P

HD = 128
PAIR = 2
masked_score = -1e30
IN_ORDER = (0, 2, 1, 4, 3)
OUT_ORDER = (0, 4, 2, 3, 1)
score_scale = 1.0 / math.sqrt(HD)
exponent_scale = score_scale * math.log2(math.e)

NN = (((1,), (0,)), ((), ()))
NT = (((1,), (1,)), ((), ()))


def dot(a, b, dims=NN):
    return lax.dot_general(a, b, dims, preferred_element_type=jnp.float32)


def block(index, size):
    return slice(index * size, (index + 1) * size)


def fetch_kernel(key_hbm, value_hbm, kv_ref, sems):
    pairs = []
    for shared in range(key_hbm.shape[1] // HD):
        for part, ref in enumerate((key_hbm, value_hbm)):
            pairs.append(
                (ref.at[:, pl.ds(shared * HD, HD)], kv_ref.at[:, pl.ds((2 * shared + part) * HD, HD)])
            )
    copies = [pltpu.make_async_copy(src, dst, sems.at[i]) for i, (src, dst) in enumerate(pairs)]
    for copy in copies:
        copy.start()
    for copy in copies:
        copy.wait()


def prepare_kernel(reach, doc_ref, query_ref, grad_ref, *refs):
    query_rows_ref, grad_rows_ref, query_t_ref, grad_t_ref, bias_ref = refs
    tokens = query_ref.shape[0]
    place = lax.axis_index("ulysses")
    inner = lax.broadcasted_iota(jnp.int32, (tokens, tokens), 0)
    lanes = lax.broadcasted_iota(jnp.int32, (tokens, tokens), 1)
    row = lax.axis_index("dp")
    first_key = jnp.zeros((1, tokens), jnp.int32)
    doc_end = jnp.int32(0)
    for doc in range(doc_ref.shape[1]):
        doc_end = doc_end + doc_ref[row, doc]
        first_key = jnp.where(doc_end <= place * tokens + lanes[:1], doc_end, first_key)
    first_key = first_key - place * tokens
    for back in range(reach + 1):
        key_pos = inner - back * tokens
        allowed = (key_pos >= first_key) & (key_pos <= lanes)
        bias_ref[block(back, tokens), :] = jnp.where(allowed, 0.0, masked_score).astype(
            jnp.bfloat16
        )
    identity = jnp.where(inner == lanes, 1.0, 0.0).astype(jnp.bfloat16)
    for head in range(query_ref.shape[1] // HD):
        own = block(head, tokens)
        queries = query_ref[:, block(head, HD)]
        grads = grad_ref[:, block(head, HD)]
        query_rows_ref[own, :] = queries
        grad_rows_ref[own, :] = grads
        query_t_ref[:HD, own] = queries.T
        query_t_ref[HD:, own] = identity
        grad_t_ref[:, own] = grads.T


def gradient_terms(weights, scores_grad, queries, grads):
    key_terms = dot(scores_grad, queries) * score_scale
    value_terms = dot(weights, grads)
    return jnp.concatenate([key_terms, value_terms], axis=1)


def parts(columns, tokens):
    width = min(columns, PAIR * tokens)
    return [slice(start, start + width) for start in range(0, columns, width)]


def joined(early, kv_refs):
    *kv_blocks, more = [ref[...] for ref in kv_refs]
    kv_blocks[early.index(1)] += more
    return [kv_blocks[early.index(back)] for back in sorted(early)]


def biased_keys(kv_blocks, bias_ref, places):
    tokens = kv_blocks[0].shape[0]
    keys = jnp.concatenate([rows[:, :HD] for rows in kv_blocks], axis=0)
    bias = jnp.concatenate([bias_ref[block(back, tokens), :] for back in places], axis=0)
    return jnp.concatenate([keys, bias], axis=1)


def early_kernel(early, late, query_t_ref, grad_t_ref, bias_ref, *refs):
    *kv_refs, weights_ref, grad_weights_ref, stats_ref, out_t_ref, scores_ref = refs
    tokens = kv_refs[0].shape[0]
    columns = parts(query_t_ref.shape[1], tokens)
    place = lax.axis_index("ulysses")

    def with_blocks(count):
        rows = slice(0, count * tokens)
        kv_blocks = joined(early, kv_refs)[:count]
        keys = biased_keys(kv_blocks, bias_ref, sorted(early)[:count])
        values = jnp.concatenate([own[:, HD:] for own in kv_blocks], axis=0)
        values_t = values.T
        for part in columns:
            scores_ref[rows, part] = dot(keys, query_t_ref[:, part])
        for part in columns:
            grad_weights = dot(values, grad_t_ref[:, part])
            grad_weights_ref[rows, part] = grad_weights
            top = jnp.max(scores_ref[rows, part], axis=0, keepdims=True) * exponent_scale
            weights = jnp.exp2(scores_ref[rows, part] * exponent_scale - top)
            stats_ref[0:1, part] = top
            stats_ref[1:2, part] = jnp.sum(weights, axis=0, keepdims=True)
            stats_ref[2:3, part] = jnp.sum(weights * grad_weights, axis=0, keepdims=True)
            weights_ref[rows, part] = weights.astype(jnp.bfloat16)
        for part in columns:
            out_t_ref[:, part] = dot(values_t, weights_ref[rows, part])

    pl.when(place <= late)(lambda: with_blocks(sum(back <= late for back in early)))
    pl.when(place > late)(lambda: with_blocks(len(early)))


def late_kernel(early, late, query_ref, grad_ref, query_t_ref, grad_t_ref, bias_ref, *refs):
    late_kv_ref, early_weights_ref, grad_weights_ref, stats_ref = refs[:4]
    weights_ref, scores_grad_ref, rescale_ref, late_term_ref, *term_refs, again_ref = refs[4:]
    tokens = late_kv_ref.shape[0]
    columns = parts(query_t_ref.shape[1], tokens)
    late_rows = block(len(early), tokens)
    place = lax.axis_index("ulysses")

    def with_blocks(count, has_late=True):
        early_rows = slice(0, count * tokens)
        far_rows = slice(tokens, count * tokens)
        term_rows = ([late_rows] if has_late else []) + [far_rows]
        if has_late:
            keys = biased_keys([late_kv_ref[...]], bias_ref, [late])
            values = late_kv_ref[:, HD:]
            scores = [dot(keys, query_t_ref[:, part]) for part in columns]
            grad_weights = [dot(values, grad_t_ref[:, part]) for part in columns]
        else:
            for ref in (weights_ref, scores_grad_ref):
                ref[late_rows, :] = jnp.zeros((tokens, ref.shape[1]), jnp.bfloat16)
        key_terms = value_terms = jnp.zeros(((count - 1 + has_late) * tokens, HD), jnp.float32)
        for index, part in enumerate(columns):
            rescale = 1.0
            total = stats_ref[1:2, part]
            if has_late:
                own, own_grad = scores[index], grad_weights[index]
                early_top = stats_ref[0:1, part]
                top = jnp.maximum(early_top, jnp.max(own, axis=0, keepdims=True) * exponent_scale)
                rescale = jnp.exp2(early_top - top)
                own = jnp.exp2(own * exponent_scale - top)
                total = rescale * total + jnp.sum(own, axis=0, keepdims=True)
            inverse = 1.0 / total
            rescale = rescale * inverse
            row_dots = rescale * stats_ref[2:3, part]
            rescale_ref[:, part] = rescale
            if has_late:
                own = own * inverse
                row_dots += jnp.sum(own * own_grad, axis=0, keepdims=True)
                weights_ref[late_rows, part] = own.astype(jnp.bfloat16)
                scores_grad_ref[late_rows, part] = (own * (own_grad - row_dots)).astype(
                    jnp.bfloat16
                )
            own = early_weights_ref[early_rows, part].astype(jnp.float32) * rescale
            weights_ref[early_rows, part] = own.astype(jnp.bfloat16)
            scores_grad_ref[early_rows, part] = (
                own * (grad_weights_ref[early_rows, part] - row_dots)
            ).astype(jnp.bfloat16)
            low_grad = [scores_grad_ref[rows, part] for rows in term_rows]
            low = [weights_ref[rows, part] for rows in term_rows]
            key_terms += dot(jnp.concatenate(low_grad, axis=0), query_ref[part, :])
            value_terms += dot(jnp.concatenate(low, axis=0), grad_ref[part, :])
        missing = len(early) - count
        if missing:
            scores_grad_ref[count * tokens : len(early) * tokens, :] = jnp.zeros(
                (missing * tokens, scores_grad_ref.shape[1]), jnp.bfloat16
            )
        terms = jnp.concatenate([key_terms * score_scale, value_terms], axis=1)
        terms = terms.astype(jnp.bfloat16)
        existing = ([late_term_ref] if has_late else []) + term_refs[: count - 1]
        for index, ref in enumerate(existing):
            ref[...] = terms[block(index, tokens)]
        for ref in term_refs[count - 1 :] + ([] if has_late else [late_term_ref]):
            ref[...] = jnp.zeros_like(ref)
        again_ref[...] = term_refs[0][...]

    exist = [sum(back <= reach for back in early) for reach in (late, max(early) - 1, max(early))]
    pl.when(place < late)(lambda: with_blocks(exist[0], has_late=False))
    pl.when(place == late)(lambda: with_blocks(exist[0]))
    pl.when((place > late) & (place < max(early)))(lambda: with_blocks(exist[1]))
    pl.when(place >= max(early))(lambda: with_blocks(exist[2]))


def near_kernel(early, query_ref, grad_ref, weights_ref, scores_grad_ref, rescale_ref, *refs):
    early_out_t_ref, late_kv_ref, *kv_refs, out_ref, query_grad_ref, near_ref = refs
    tokens = late_kv_ref.shape[0]
    late_out_t = dot(late_kv_ref[:, HD:].T, weights_ref[-tokens:, :])
    out_t = (early_out_t_ref[...] * rescale_ref[...] + late_out_t).astype(jnp.bfloat16)
    near_ref[...] = gradient_terms(
        weights_ref[:tokens, :], scores_grad_ref[:tokens, :], query_ref[...], grad_ref[...]
    )
    kv_blocks = joined(early, kv_refs) + [late_kv_ref[...]]
    keys_t = jnp.concatenate([rows[:, :HD] for rows in kv_blocks], axis=0).T
    query_grad_t = (dot(keys_t, scores_grad_ref[...]) * score_scale).astype(jnp.bfloat16)
    for head in range(out_ref.shape[1] // HD):
        own = block(head, tokens)
        query_grad_ref[:, block(head, HD)] = query_grad_t[:, own].T
        out_ref[:, block(head, HD)] = out_t[:, own].T


def call(body, name, outs, scratch, flops, *operands, fetched=False):
    vmem = pl.BlockSpec(memory_space=pltpu.VMEM)
    if fetched:
        operands = [pltpu.with_memory_space_constraint(a, pltpu.HBM) for a in operands]
    held = sum(math.prod(a.shape) * a.dtype.itemsize for a in operands)
    held += sum(math.prod(shape) * dtype.dtype.itemsize for shape, dtype in outs)
    held += sum(math.prod(s.shape) * 4 for s in scratch if hasattr(s, "shape"))
    return pl.pallas_call(
        body,
        out_shape=[jax.ShapeDtypeStruct(shape, dtype) for shape, dtype in outs],
        in_specs=[
            pl.BlockSpec(memory_space=pltpu.HBM)
            if fetched
            else pl.BlockSpec(memory_space=pltpu.SMEM)
            if a.dtype == jnp.int32
            else vmem
            for a in operands
        ],
        out_specs=[vmem] * len(outs),
        scratch_shapes=scratch,
        compiler_params=pltpu.CompilerParams(
            vmem_limit_bytes=held + 12 * 1024 * 1024
        ),
        cost_estimate=pl.CostEstimate(flops=flops, bytes_accessed=held, transcendentals=0),
        name=name,
    )(*operands)


def ordered(values, order):
    first = [values[place] for place in order if place < len(values)]
    return first + [v for place, v in enumerate(values) if place not in order]


def per_device(devices, query_rows, key_rows, value_rows, grad_out, doc_lengths):
    tokens, query_width = query_rows.shape
    shared_heads = key_rows.shape[1] // HD
    length = tokens * devices
    reach = min(devices - 1, (length // 2 - 1 + tokens - 1) // tokens)
    blocks = reach + 1
    window = blocks * tokens
    low = jnp.bfloat16

    group_width = query_width // shared_heads
    columns = group_width // HD * tokens
    product = 2 * window * columns * HD
    (kv,) = call(
        fetch_kernel,
        "fetch",
        [
            ((tokens, 2 * shared_heads * HD), low),
        ],
        [pltpu.SemaphoreType.DMA((2 * shared_heads,))],
        16 * product,
        key_rows,
        value_rows,
        fetched=True,
    )
    def forward(back, first, last):
        return lax.ppermute(kv, "ulysses", [(d - back, d) for d in range(max(first, back), last)])

    previous = [forward(1, reach + 1, devices), forward(1, 0, reach + 1)]
    kv_blocks = {0: kv}
    for back in ordered(list(range(blocks)), IN_ORDER)[1:]:
        kv_blocks[back] = previous[0] if back == 1 else forward(back, 0, devices)
    late = list(kv_blocks)[1]
    early = [0] + [back for back in kv_blocks if back not in (0, late)]
    places = early + [late]
    window_early = len(early) * tokens

    attention, grad_queries, totals, far = [], [], [], []
    for shared in range(shared_heads):
        own_queries = query_rows[:, block(shared, group_width)]
        own_grads = grad_out[:, block(shared, group_width)]
        if attention:
            own_queries, attention[-1] = lax.optimization_barrier((own_queries, attention[-1]))
        own_kv = [
            rows[:, block(shared, 2 * HD)]
            for rows in [kv_blocks[back] for back in places] + previous[1:]
        ]
        early_kv = own_kv[:-2] + own_kv[-1:]
        queries, grads, queries_t, grads_t, bias = call(
            functools.partial(prepare_kernel, reach),
            "prepare",
            [
                ((columns, HD), low),
                ((columns, HD), low),
                ((HD + tokens, columns), low),
                ((HD, columns), low),
                ((window, tokens), low),
            ],
            [],
            product // 4,
            doc_lengths,
            own_queries,
            own_grads,
        )
        weights, grad_weights, stats, early_out_t = call(
            functools.partial(early_kernel, early, late),
            "early",
            [
                ((window_early, columns), low),
                ((window_early, columns), jnp.float32),
                ((3, columns), jnp.float32),
                ((HD, columns), jnp.float32),
            ],
            [pltpu.VMEM((window_early, columns), jnp.float32)],
            3 * product,
            queries_t,
            grads_t,
            bias,
            *early_kv,
        )
        weights, scores_grad, rescale, *own_far = call(
            functools.partial(late_kernel, early, late),
            "late",
            [((window, columns), low), ((window, columns), low), ((1, columns), jnp.float32)]
            + [((tokens, 2 * HD), low)] * (reach + 1),
            [],
            2 * product,
            queries,
            grads,
            queries_t,
            grads_t,
            bias,
            own_kv[-2],
            weights,
            grad_weights,
            stats,
        )
        own_out, own_query_grad, own_total = call(
            functools.partial(near_kernel, early),
            "near",
            [((tokens, group_width), low)] * 2 + [((tokens, 2 * HD), jnp.float32)],
            [],
            2 * product,
            queries,
            grads,
            weights,
            scores_grad,
            rescale,
            early_out_t,
            own_kv[-2],
            *early_kv,
        )
        attention.append(own_out)
        grad_queries.append(own_query_grad)
        totals.append(own_total)
        far.append(own_far)

    def side_by_side(parts):
        return parts[0] if len(parts) == 1 else jnp.concatenate(parts, axis=1)

    far_places = [late] + sorted(early)[1:]
    total = side_by_side(totals)
    returns = [(back, 0, devices) for back in ordered(list(range(blocks)), OUT_ORDER)[1:]]
    returns[-1:] = [(1, reach, devices), (1, 0, reach)]
    for back, first, last in returns:
        index = reach if last == reach else far_places.index(back)
        terms = side_by_side([own[index] for own in far])
        terms = lax.ppermute(
            terms, "ulysses", [(d + back, d) for d in range(first, min(last, devices - back))]
        )
        total = total + terms.astype(jnp.float32)
    total = total.astype(low)
    grad_keys = side_by_side([total[:, block(2 * g, HD)] for g in range(shared_heads)])
    grad_values = side_by_side([total[:, block(2 * g + 1, HD)] for g in range(shared_heads)])
    return (side_by_side(attention), side_by_side(grad_queries), grad_keys, grad_values)


def solution(mesh):
    rows = P(("dp", "ulysses"), None)
    return jax.shard_map(
        functools.partial(per_device, mesh.shape["ulysses"]),
        mesh=mesh,
        in_specs=(rows, rows, rows, rows, P()),
        out_specs=(rows, rows, rows, rows),
        check_vma=False,
    )
```
